128 devices in a mesh: face: 4 (over x), tile: 32 (over z, y, core).
Axes of the slice: x: 4, y: 4, z: 4, core: 2. Of those that a mesh axis runs over, the one named last changes fastest.
Arguments:
- squeeze_anomaly: float32 [8, 32, 4096], P(None, 'face', 'tile'), may hold values from -6 to 6
- eastward_airflow: float32 [8, 32, 4096], P(None, 'face', 'tile'), may hold values from -6 to 6
- northward_airflow: float32 [8, 32, 4096], P(None, 'face', 'tile'), may hold values from -6 to 6
- thermal_anomaly: float32 [8, 32, 4096], P(None, 'face', 'tile'), may hold values from -6 to 6
- diffusivity_link: float32 [8, 32, 4096], P(None, 'face', 'tile'), may hold values from 0.1 to 4
- sound_stability_ratio: float32 [8], replicated, may hold values from 0.1 to 0.3
- overlay_source_site: int32 [128, 128, 128], P(('face', 'tile')), may hold values from 0 to 1023
- overlay_target_floe: int32 [128, 128, 128], P(('face', 'tile')), may hold values from 0 to 2047
- overlay_fraction: float32 [128, 128, 128], P(('face', 'tile')), may hold values from 0 to 1, as said below
- floe_skin_kelvin: float32 [262144], P(('face', 'tile')), may hold values from -6 to 6
- frozen_indicator: int32 [262144], P(('face', 'tile')), may hold values 0 or 1
- floe_motion: float32 [262144], P(('face', 'tile')), may hold values from -4 to 4
- floe_strain_tensor: float32 [262144], P(('face', 'tile')), may hold values from -4 to 4
- floe_compress_resist: float32 [262144], P(('face', 'tile')), may hold values from 0.5 to 2
Outputs:
- temp_new: float32 [8, 32, 4096], P(None, 'face', 'tile')
- pressure_new: float32 [8, 32, 4096], P(None, 'face', 'tile')
- floe_skin_fresh: float32 [262144], P(('face', 'tile'))
- ice_velocity_new: float32 [262144], P(('face', 'tile'))
The draws below stay inside these ranges and needn't reach their ends.
Inputs may be any that keep to these rules, and one draw needn't show every extreme that they name: `overlay_fraction`: A slot with area 0 is empty; for each pair of devices the live slots come first; in every draw some destination devices receive 128 live slots from every source.
All inputs are finite; a program needn't handle non-finite values. No bound on the sum of `frozen_indicator` on one device may be relied on, other than what follows from the above.
Results may differ from the reference program's by a relative error of at most 0.00002.
Values sent between devices are 32-bit elements; how exact they have to be, the bound alone decides.
No kernel may reach another device: no remote copies, remote signals or barrier semaphores. Data moves between devices by JAX's collectives and lax.ppermute only.
A program may use at most 64 MiB of HBM per device.

```python
import math
import jax
import jax.numpy as jnp
from jax import lax

HEIGHT_LAYERS = 8
AX_DEV = 8
AY_DEV = 128
SLOT = 128
ICE_DEV = 2048
SUBS = 2
EVP = 20
NDEV = 128
GRID_EASTWARD = 32
GRID_NORTHWARD = 4096
FLOE_TOTAL = 262144
N_TILE = 32


def draw_overlay_fraction(key, part):
    key = jax.random.fold_in(key, 7)
    key_pick, key_count, key_value = jax.random.split(key, 3)
    ranking = jax.random.permutation(key_pick, NDEV)
    filled = ranking < max(NDEV // 4, 1)
    counts = jax.random.randint(key_count, (NDEV, NDEV), SLOT // 8, SLOT // 2 + 1)
    counts = jnp.where(filled[None, :], SLOT, counts)
    living = jnp.arange(SLOT)[None, None, :] < counts[:, :, None]
    values = jax.random.uniform(key_value, (NDEV, NDEV, SLOT), jnp.float32, 0.2, 1.0)
    return jnp.where(living, values, 0.0).astype(jnp.float32)


def place_ends(entries, rng, smallest, largest):
    extent = entries.shape
    place = [jax.random.randint(jax.random.fold_in(rng, axis), (), 0, extent[axis]) for axis in range(len(extent))]
    entries = entries.at[tuple(place)].set(smallest)
    longest = extent.index(max(extent))
    place[longest] = (place[longest] + 1) % extent[longest]
    return entries.at[tuple(place)].set(largest)


def level_of(rng, dims, cuts, least, largest):
    loudness, own = 1.0, jax.random.fold_in(rng, 6)
    for axis_at, parts in cuts:
        heights = jnp.exp(jax.random.uniform(jax.random.fold_in(own, axis_at), (parts,), jnp.float32, least / len(cuts), largest / len(cuts)))
        loudness = loudness * jnp.repeat(heights, dims[axis_at] // parts).reshape([-1 if axis == axis_at else 1 for axis in range(len(dims))])
    return loudness


def centred(own_key, extent, scale, bound, shards=(), held_as=jnp.bfloat16):
    values = jax.random.normal(own_key, extent, jnp.float32) * scale
    if len(shards) > 0:
        values = level_of(own_key, extent, shards, -0.22, 0.18) * values
    return jnp.clip(values, min=-bound, max=bound).astype(held_as)


def setup_inputs(seed: int = 0) -> dict:
    key_of = jax.random.split(jax.random.key(seed), 15)
    squeeze_anomaly = centred(key_of[0], (HEIGHT_LAYERS, GRID_EASTWARD, GRID_NORTHWARD), 1.0, 6.0, ((1, 4), (2, 32)), jnp.float32)
    eastward_airflow = centred(key_of[1], (HEIGHT_LAYERS, GRID_EASTWARD, GRID_NORTHWARD), 1.0, 6.0, ((1, 4), (2, 32)), jnp.float32)
    northward_airflow = centred(key_of[2], (HEIGHT_LAYERS, GRID_EASTWARD, GRID_NORTHWARD), 1.0, 6.0, ((1, 4), (2, 32)), jnp.float32)
    thermal_anomaly = centred(key_of[3], (HEIGHT_LAYERS, GRID_EASTWARD, GRID_NORTHWARD), 1.0, 6.0, ((1, 4), (2, 32)), jnp.float32)
    diffusivity_link = jnp.clip(jnp.exp(math.log(4.0) - 3.6888794 * jax.random.uniform(key_of[4], (HEIGHT_LAYERS, GRID_EASTWARD, GRID_NORTHWARD), jnp.float32) ** level_of(key_of[4], (HEIGHT_LAYERS, GRID_EASTWARD, GRID_NORTHWARD), ((1, 4), (2, 32)), -0.2, 0.2)), 0.1, 4.0)
    sound_stability_ratio = jnp.clip(jnp.exp(jax.random.uniform(key_of[5], (HEIGHT_LAYERS,), jnp.float32, math.log(0.1), math.log(0.3))), 0.1, 0.3)
    overlay_source_site = place_ends(jax.random.randint(key_of[6], (NDEV, NDEV, SLOT), 0, AX_DEV * AY_DEV), jax.random.fold_in(key_of[6], 1), 0, (AX_DEV * AY_DEV) - 1).astype(jnp.int32)
    overlay_target_floe = place_ends(jax.random.randint(key_of[7], (NDEV, NDEV, SLOT), 0, ICE_DEV), jax.random.fold_in(key_of[7], 1), 0, ICE_DEV - 1).astype(jnp.int32)
    overlay_fraction = draw_overlay_fraction(jax.random.fold_in(key_of[14], 71), 0)
    floe_skin_kelvin = centred(key_of[9], (FLOE_TOTAL,), 1.0, 6.0, ((0, 128),), jnp.float32)
    frozen_indicator = place_ends((jax.random.randint(key_of[10], (FLOE_TOTAL,), 0, 4) < 3).astype(jnp.int32), jax.random.fold_in(key_of[10], 1), 0, 1)
    floe_motion = centred(key_of[11], (FLOE_TOTAL,), 0.5, 4.0, ((0, 128),), jnp.float32)
    floe_strain_tensor = centred(key_of[12], (FLOE_TOTAL,), 0.5, 4.0, ((0, 128),), jnp.float32)
    floe_compress_resist = jnp.clip(jnp.exp(math.log(2.0) - 1.3862944 * jax.random.uniform(key_of[13], (FLOE_TOTAL,), jnp.float32) ** level_of(key_of[13], (FLOE_TOTAL,), ((0, 128),), -0.2, 0.2)), 0.5, 2.0)
    return {"squeeze_anomaly": squeeze_anomaly, "eastward_airflow": eastward_airflow, "northward_airflow": northward_airflow, "thermal_anomaly": thermal_anomaly, "diffusivity_link": diffusivity_link, "sound_stability_ratio": sound_stability_ratio, "overlay_source_site": overlay_source_site, "overlay_target_floe": overlay_target_floe, "overlay_fraction": overlay_fraction, "floe_skin_kelvin": floe_skin_kelvin, "frozen_indicator": frozen_indicator, "floe_motion": floe_motion, "floe_strain_tensor": floe_strain_tensor, "floe_compress_resist": floe_compress_resist}


isentropic_lapse = 0.3
gravity_step = 0.5
floe_warmth = 2.0
floor_conductance = 1.0
relaxation = 0.5
stress_decay = 0.05
mobility = 0.3
water_drag = 0.1


def acoustic(fields, speed):
    speeds = speed[:, None, None]
    press = fields[0]
    zonal = fields[1]
    meridional = fields[2]
    zonal_new = zonal[:, :-1, :] - speeds * (press[:, 1:, :] - press[:, :-1, :])
    merid_new = meridional[:, :, :-1] - speeds * (press[:, :, 1:] - press[:, :, :-1])
    fresh_squeeze = press[:, 1:-1, 1:-1] - speeds * (zonal_new[:, 1:, 1:-1] - zonal_new[:, :-1, 1:-1] + merid_new[:, 1:-1, 1:] - merid_new[:, 1:-1, :-1])
    return jnp.stack([fresh_squeeze, zonal_new[:, 1:, 1:-1], merid_new[:, 1:-1, 1:]])


def forward_elimination(earlier_thermal, diffusivity_link):
    def descending_pass(carry, level):
        gain_prev, rest_prev, coef_prev = carry
        temp_level, coef_level = level
        denom = 1.0 + coef_prev + coef_level - coef_prev * gain_prev
        gain = coef_level / denom
        rest = (temp_level + coef_prev * rest_prev) / denom
        return (gain, rest, coef_level), (gain, rest)

    blank_vector = jnp.zeros_like(earlier_thermal[0])
    (final_multiplier, final_remainder, final_coupler), (sweep_multipliers, sweep_remainders) = lax.scan(descending_pass, (blank_vector, blank_vector, blank_vector), (earlier_thermal[:-1], diffusivity_link[:-1]))
    lowest_divisor = 1.0 + final_coupler * (1.0 - final_multiplier)
    lower_diagonal = gravity_step / lowest_divisor
    upper_diagonal = (earlier_thermal[-1] + final_coupler * final_remainder) / lowest_divisor
    return sweep_multipliers, sweep_remainders, lower_diagonal, upper_diagonal


def sweep_up(sweep_multipliers, sweep_remainders, bottom):
    def upward(below, level):
        value = level[0] * below + level[1]
        return value, value

    _, upper = lax.scan(upward, bottom, (sweep_multipliers, sweep_remainders), reverse=True)
    return jnp.concatenate([upper, bottom[None]], 0)


def reference(squeeze_anomaly, eastward_airflow, northward_airflow, thermal_anomaly, diffusivity_link, sound_stability_ratio, overlay_source_site, overlay_target_floe, overlay_fraction, floe_skin_kelvin, frozen_indicator, floe_motion, floe_strain_tensor, floe_compress_resist):
    fields = jnp.stack([squeeze_anomaly, eastward_airflow, northward_airflow])
    for substep in range(SUBS):
        padded = jnp.pad(fields, ((0, 0), (0, 0), (1, 1), (1, 1)), mode="wrap")
        fields = acoustic(padded, sound_stability_ratio)
    fresh_squeeze = fields[0]
    earlier_thermal = thermal_anomaly + isentropic_lapse * fresh_squeeze
    sweep_multipliers, sweep_remainders, lower_diagonal, upper_diagonal = forward_elimination(earlier_thermal, diffusivity_link)
    drag = diffusivity_link[-1]
    weight = drag / (1.0 + drag * lower_diagonal)
    wind_stress = drag * (fields[1][-1] + 0.5 * fields[2][-1])
    source = jnp.arange(NDEV, dtype=jnp.int32)[:, None, None]
    face_row = source // N_TILE
    tile_col = source % N_TILE
    glob_x = face_row * AX_DEV + overlay_source_site // AY_DEV
    glob_y = tile_col * AY_DEV + overlay_source_site % AY_DEV
    column = (glob_x * GRID_NORTHWARD + glob_y).astype(jnp.int32)
    slot_w = overlay_fraction * weight.reshape(-1)[column]
    slot_wg = slot_w * upper_diagonal.reshape(-1)[column]
    slot_tau = overlay_fraction * wind_stress.reshape(-1)[column]
    target = jnp.arange(NDEV, dtype=jnp.int32)[None, :, None]
    ice_cell = (target * ICE_DEV + jnp.transpose(overlay_target_floe, (1, 0, 2))).astype(jnp.int32)
    flat_ice = ice_cell.reshape(-1)
    weight_total = jax.ops.segment_sum(slot_w.reshape(-1), flat_ice, FLOE_TOTAL)
    weighted_factor_total = jax.ops.segment_sum(slot_wg.reshape(-1), flat_ice, FLOE_TOTAL)
    tau_sum = jax.ops.segment_sum(slot_tau.reshape(-1), flat_ice, FLOE_TOTAL)
    floe_skin_fresh = jnp.where(frozen_indicator == 1, (floe_warmth * floe_skin_kelvin + weighted_factor_total) / (floe_warmth + floor_conductance + weight_total), floe_skin_kelvin)
    slot_flux = slot_w * floe_skin_fresh[ice_cell] - slot_wg
    surface_flux = jax.ops.segment_sum(slot_flux.reshape(-1), column.reshape(-1), GRID_EASTWARD * GRID_NORTHWARD).reshape(GRID_EASTWARD, GRID_NORTHWARD)
    temp_new = sweep_up(sweep_multipliers, sweep_remainders, lower_diagonal * surface_flux + upper_diagonal)
    strength = floe_compress_resist * (0.1 + 0.9 * frozen_indicator.astype(jnp.float32))

    def cycle(index, state):
        velocity, stress = state
        vel_pad = jnp.pad(velocity, 1)
        stress = (stress + relaxation * strength * (vel_pad[2:] - vel_pad[1:-1])) / (1.0 + stress_decay)
        stress_pad = jnp.pad(stress, 1)
        velocity = (velocity + mobility * (stress - stress_pad[:-2] + tau_sum)) / (1.0 + mobility * water_drag)
        return velocity, stress

    velocity, stress = lax.fori_loop(0, EVP, cycle, (floe_motion, floe_strain_tensor))
    return temp_new, fresh_squeeze, floe_skin_fresh, velocity
```

```python
import functools

import jax
import jax.numpy as jnp
from jax import lax
from jax.experimental import pallas as pl
from jax.experimental.pallas import tpu as pltpu
from jax.sharding import PartitionSpec as P

SUBS = 2
EVP = 20
LEVELS = 8
ROWS = 8
LANES = 128
SOURCES = 128
ICE_ROWS = 16
FIELDS = 3 * LEVELS
SLAB = 56

isentropic_lapse = 0.3
gravity_step = 0.5
floe_warmth = 2.0
floor_conductance = 1.0
relaxation = 0.5
stress_decay = 0.05
mobility = 0.3
water_drag = 0.1

BOTH = ("face", "tile")
VMEM = pl.BlockSpec(memory_space=pltpu.VMEM)
SMEM = pl.BlockSpec(memory_space=pltpu.SMEM)


def struct(*shape):
    return jax.ShapeDtypeStruct(shape, jnp.float32)


def lanes_of(shape):
    return lax.broadcasted_iota(jnp.int32, shape, len(shape) - 1)


def rows_of(shape):
    return lax.broadcasted_iota(jnp.int32, shape, len(shape) - 2)


def pack_columns(p_ref, u_ref, v_ref, out_ref):
    lane = lanes_of((ROWS, LANES))
    packed = jnp.zeros((ROWS, LANES), jnp.float32)
    for field, ref in enumerate((p_ref, u_ref, v_ref)):
        for level in range(LEVELS):
            at = 4 * (field * LEVELS + level)
            moved = pltpu.roll(ref[level], 2 + at, 1)
            packed = jnp.where((lane >= at) & (lane < at + 4), moved, packed)
    out_ref[...] = packed


def joined(left, right):
    return jnp.where(lanes_of((ROWS, LANES)) % 4 < 2, left, right)


def pack_rows(p_ref, u_ref, v_ref, left_ref, right_ref, down_ref, up_ref):
    sides = joined(left_ref[...], right_ref[...])
    for out_ref, row in ((down_ref, 0), (up_ref, ROWS - 2)):
        for field, ref in enumerate((p_ref, u_ref, v_ref)):
            for level in range(LEVELS):
                out_ref[pl.ds(2 * (field * LEVELS + level), 2), :] = ref[level, pl.ds(row, 2), :]
        out_ref[pl.ds(2 * FIELDS, 2), :] = sides[row : row + 2]
        out_ref[pl.ds(2 * FIELDS + 2, SLAB - 2 * FIELDS - 2), :] = jnp.zeros(
            (SLAB - 2 * FIELDS - 2, LANES), jnp.float32
        )


def look_up(table, high, low):
    shape = low.shape
    found = [None] * len(table)
    for row in range(table[0].shape[0]):
        here = high == row
        for at, values in enumerate(table):
            spread = jnp.broadcast_to(values[row : row + 1], shape)
            taken = jnp.take_along_axis(spread, low, axis=1, mode="promise_in_bounds")
            found[at] = taken if row == 0 else jnp.where(here, taken, found[at])
    return found


def columns_kernel(
    speed_ref,
    p_ref,
    u_ref,
    v_ref,
    heat_ref,
    link_ref,
    left_ref,
    right_ref,
    below_ref,
    above_ref,
    site_ref,
    area_ref,
    press_out,
    coef_out,
    slots_out,
    wide,
    sides,
):
    sides[pl.ds(0, ROWS), :] = joined(left_ref[...], right_ref[...])
    sides[pl.ds(8, 8), :] = jnp.zeros((8, LANES), jnp.float32)
    sides[pl.ds(8, 2), :] = above_ref[pl.ds(2 * FIELDS, 2), :]
    sides[pl.ds(14, 2), :] = below_ref[pl.ds(2 * FIELDS, 2), :]
    border = sides[...]
    temps = []
    for level in range(LEVELS):
        speed = speed_ref[level]
        now = []
        for field, ref in enumerate((p_ref, u_ref, v_ref)):
            at = field * LEVELS + level
            wide[at, pl.ds(0, ROWS), :] = ref[level]
            wide[at, pl.ds(8, 8), :] = jnp.zeros((8, LANES), jnp.float32)
            wide[at, pl.ds(8, 2), :] = above_ref[pl.ds(2 * at, 2), :]
            wide[at, pl.ds(14, 2), :] = below_ref[pl.ds(2 * at, 2), :]
            outer = pltpu.roll(border, (126 - 4 * at) % LANES, 1)
            now.append(jnp.concatenate([wide[at], outer], axis=1))
        press, zonal, merid = now
        for _ in range(SUBS):
            zonal = zonal - speed * (pltpu.roll(press, 15, 0) - press)
            merid = merid - speed * (pltpu.roll(press, 255, 1) - press)
            press = press - speed * (
                zonal - pltpu.roll(zonal, 1, 0) + merid - pltpu.roll(merid, 1, 1)
            )
        final = press[:ROWS, :LANES]
        press_out[level] = final
        temps.append(heat_ref[level] + isentropic_lapse * final)
    last_zonal = zonal[:ROWS, :LANES]
    last_merid = merid[:ROWS, :LANES]

    link = link_ref[0]
    gain = link / (1.0 + link)
    rest = temps[0] / (1.0 + link)
    coef_out[0] = gain
    coef_out[LEVELS] = rest
    for level in range(1, LEVELS - 1):
        earlier, link = link, link_ref[level]
        denom = 1.0 + earlier + link - earlier * gain
        gain = link / denom
        rest = (temps[level] + earlier * rest) / denom
        coef_out[level] = gain
        coef_out[LEVELS + level] = rest
    divisor = 1.0 + link * (1.0 - gain)
    beta = gravity_step / divisor
    gamma = (temps[LEVELS - 1] + link * rest) / divisor
    coef_out[LEVELS - 1] = beta
    coef_out[2 * LEVELS - 1] = gamma
    drag = link_ref[LEVELS - 1]
    weight = drag / (1.0 + drag * beta)
    stress = drag * (last_zonal + 0.5 * last_merid)

    site = site_ref[0]
    area = area_ref[0]
    found = look_up((weight, gamma, stress), site // LANES, site % LANES)
    slot_w = area * found[0]
    slots_out[pl.ds(0, SOURCES, stride=4), :] = slot_w
    slots_out[pl.ds(1, SOURCES, stride=4), :] = slot_w * found[1]
    slots_out[pl.ds(2, SOURCES, stride=4), :] = area * found[2]
    slots_out[pl.ds(3, SOURCES, stride=4), :] = jnp.zeros((SOURCES, LANES), jnp.float32)


def in_three(values):
    first = values.astype(jnp.bfloat16)
    left = values - first.astype(jnp.float32)
    second = left.astype(jnp.bfloat16)
    third = (left - second.astype(jnp.float32)).astype(jnp.bfloat16)
    return first.astype(jnp.float32), second.astype(jnp.float32), third.astype(jnp.float32)


def segment_sums(read, index_ref, high_count, values, group=8):
    shape = (high_count, LANES)
    high_row = rows_of(shape)
    low_row = rows_of((LANES, LANES))
    count = 3 * values * high_count

    def step(block, total):
        start = pl.multiple_of(block * group, group)
        index = index_ref[0, pl.ds(start, group), :]
        high = index // LANES
        low = index % LANES
        parts = [part for value in range(values) for part in in_three(read(value, start, group))]
        carried, spread = [], []
        for row in range(group):
            here = high_row == high[row : row + 1]
            carried.append(
                jnp.concatenate(
                    [
                        jnp.where(here, jnp.broadcast_to(part[row : row + 1], shape), 0.0).astype(
                            jnp.bfloat16
                        )
                        for part in parts
                    ]
                    if high_count % 16 == 0
                    else [
                        jnp.concatenate(
                            [
                                jnp.where(here, jnp.broadcast_to(part[row : row + 1], shape), 0.0)
                                for part in parts
                            ],
                            axis=0,
                        ).astype(jnp.bfloat16)
                    ],
                    axis=0,
                )
            )
            spread.append(
                jnp.where(low_row == low[row : row + 1], 1.0, 0.0).astype(jnp.bfloat16)
            )
        return total + lax.dot_general(
            jnp.concatenate(carried, axis=1),
            jnp.concatenate(spread, axis=1),
            (((1,), (1,)), ((), ())),
            preferred_element_type=jnp.float32,
        )

    total = lax.fori_loop(0, SOURCES // group, step, jnp.zeros((count, LANES), jnp.float32))
    sums = []
    for value in range(values):
        at = 3 * value * high_count
        sums.append(
            total[at + 2 * high_count : at + 3 * high_count]
            + total[at + high_count : at + 2 * high_count]
            + total[at : at + high_count]
        )
    return sums


def ice_kernel(
    slots_ref,
    target_ref,
    skin_ref,
    frozen_ref,
    motion_ref,
    strain_ref,
    resist_ref,
    skin_out,
    flux_out,
    ice_out,
    ahead_out,
    behind_out,
):
    def read(value, start, group):
        return slots_ref[pl.ds(4 * start + value, group, stride=4), :]

    heat, warmth, tau = segment_sums(read, target_ref, ICE_ROWS, 3)
    skin = skin_ref[...]
    frozen = frozen_ref[...]
    fresh = jnp.where(
        frozen == 1,
        (floe_warmth * skin + warmth) / (floe_warmth + floor_conductance + heat),
        skin,
    )
    skin_out[...] = fresh
    target = target_ref[0]
    (at_floe,) = look_up((fresh,), target // LANES, target % LANES)
    flux_out[...] = (
        slots_ref[pl.ds(0, SOURCES, stride=4), :] * at_floe
        - slots_ref[pl.ds(1, SOURCES, stride=4), :]
    )
    strength = resist_ref[...] * (0.1 + 0.9 * frozen.astype(jnp.float32))
    ice_out[0] = strength
    ice_out[1] = tau
    blank = jnp.zeros((4, LANES), jnp.float32)
    for out_ref, row in ((ahead_out, ICE_ROWS - 1), (behind_out, 0)):
        out_ref[0:1] = motion_ref[row : row + 1]
        out_ref[1:2] = strain_ref[row : row + 1]
        out_ref[2:3] = strength[row : row + 1]
        out_ref[3:4] = tau[row : row + 1]
        out_ref[4:8] = blank


def drift_kernel(last_ref, motion_ref, strain_ref, ice_ref, before_ref, after_ref, out_ref, held):
    height = 24
    held[:, pl.ds(16, 8), :] = jnp.zeros((4, 8, LANES), jnp.float32)
    for at in range(4):
        held[at, 0:1, :] = before_ref[at : at + 1]
        held[at, 17:18, :] = after_ref[at : at + 1]
    held[0, pl.ds(1, ICE_ROWS), :] = motion_ref[...]
    held[1, pl.ds(1, ICE_ROWS), :] = strain_ref[...]
    held[2, pl.ds(1, ICE_ROWS), :] = ice_ref[0]
    held[3, pl.ds(1, ICE_ROWS), :] = ice_ref[1]
    velocity = held[0]
    stress = held[1]
    pull = held[2] * (relaxation / (1.0 + stress_decay))
    push = held[3] * (mobility / (1.0 + mobility * water_drag))
    shape = (height, LANES)
    lane = lanes_of(shape)
    row = rows_of(shape)
    inside = jnp.where((last_ref[0] == 1) & (row >= 17), 0.0, 1.0)
    keep = inside / (1.0 + mobility * water_drag)
    move = inside * (mobility / (1.0 + mobility * water_drag))
    push = push * inside

    def next_of(cells):
        turned = pltpu.roll(cells, LANES - 1, 1)
        return jnp.where(lane == LANES - 1, pltpu.roll(turned, height - 1, 0), turned)

    def prior_of(cells):
        turned = pltpu.roll(cells, 1, 1)
        return jnp.where(lane == 0, pltpu.roll(turned, 1, 0), turned)

    for _ in range(EVP):
        stress = stress * (1.0 / (1.0 + stress_decay)) + pull * (next_of(velocity) - velocity)
        velocity = velocity * keep + (move * (stress - prior_of(stress)) + push)
    held[0] = velocity
    out_ref[...] = held[0, pl.ds(1, ICE_ROWS), :]


def upward_kernel(flux_ref, site_ref, coef_ref, out_ref):
    def read(value, start, group):
        return flux_ref[pl.ds(start, group), :]

    (surface_flux,) = segment_sums(read, site_ref, ROWS, 1)
    below = coef_ref[LEVELS - 1] * surface_flux + coef_ref[2 * LEVELS - 1]
    out_ref[LEVELS - 1] = below
    for level in range(LEVELS - 2, -1, -1):
        below = coef_ref[level] * below + coef_ref[LEVELS + level]
        out_ref[level] = below


def ring(axis, step):
    count = lax.axis_size(axis)
    return [(i, (i + step) % count) for i in range(count)]


def line(step):
    count = lax.axis_size(BOTH)
    return [(i, i + step) for i in range(count) if 0 <= i + step < count]


def local(
    squeeze_anomaly,
    eastward_airflow,
    northward_airflow,
    thermal_anomaly,
    diffusivity_link,
    sound_stability_ratio,
    overlay_source_site,
    overlay_target_floe,
    overlay_fraction,
    floe_skin_kelvin,
    frozen_indicator,
    floe_motion,
    floe_strain_tensor,
    floe_compress_resist,
):
    fields = (squeeze_anomaly, eastward_airflow, northward_airflow)
    edges = pl.pallas_call(
        pack_columns, out_shape=struct(ROWS, LANES), in_specs=[VMEM] * 3, out_specs=VMEM
    )(*fields)
    left = lax.ppermute(edges, "tile", ring("tile", 1))
    right = lax.ppermute(edges, "tile", ring("tile", -1))
    first_rows, last_rows = pl.pallas_call(
        pack_rows,
        out_shape=[struct(SLAB, LANES)] * 2,
        in_specs=[VMEM] * 5,
        out_specs=[VMEM] * 2,
    )(*fields, left, right)
    below = lax.ppermute(last_rows, "face", ring("face", 1))
    above = lax.ppermute(first_rows, "face", ring("face", -1))
    pressure_new, coef, slots = pl.pallas_call(
        columns_kernel,
        out_shape=[
            struct(LEVELS, ROWS, LANES),
            struct(2 * LEVELS, ROWS, LANES),
            struct(4 * SOURCES, LANES),
        ],
        in_specs=[SMEM] + [VMEM] * 11,
        out_specs=[VMEM] * 3,
        scratch_shapes=[
            pltpu.VMEM((FIELDS, 16, LANES), jnp.float32),
            pltpu.VMEM((16, LANES), jnp.float32),
        ],
    )(
        sound_stability_ratio,
        *fields,
        thermal_anomaly,
        diffusivity_link,
        left,
        right,
        below,
        above,
        overlay_source_site,
        overlay_fraction,
    )
    arrived = lax.all_to_all(slots, BOTH, split_axis=0, concat_axis=0, tiled=True)
    ice = (ICE_ROWS, LANES)
    motion = floe_motion.reshape(ice)
    strain = floe_strain_tensor.reshape(ice)
    fresh, flux, ice_terms, ahead, behind = pl.pallas_call(
        ice_kernel,
        out_shape=[
            struct(*ice),
            struct(SOURCES, LANES),
            struct(2, *ice),
            struct(8, LANES),
            struct(8, LANES),
        ],
        in_specs=[VMEM] * 7,
        out_specs=[VMEM] * 5,
    )(
        arrived,
        overlay_target_floe,
        floe_skin_kelvin.reshape(ice),
        frozen_indicator.reshape(ice),
        motion,
        strain,
        floe_compress_resist.reshape(ice),
    )
    returned = lax.all_to_all(flux, BOTH, split_axis=0, concat_axis=0, tiled=True)
    before = lax.ppermute(ahead, BOTH, line(1))
    after = lax.ppermute(behind, BOTH, line(-1))
    last = (lax.axis_index(BOTH) == lax.axis_size(BOTH) - 1).astype(jnp.int32).reshape(1)
    velocity = pl.pallas_call(
        drift_kernel,
        out_shape=struct(*ice),
        in_specs=[SMEM] + [VMEM] * 5,
        out_specs=VMEM,
        scratch_shapes=[pltpu.VMEM((4, 24, LANES), jnp.float32)],
    )(last, motion, strain, ice_terms, before, after)
    temp_new = pl.pallas_call(
        upward_kernel,
        out_shape=struct(LEVELS, ROWS, LANES),
        in_specs=[VMEM] * 3,
        out_specs=VMEM,
    )(returned, overlay_source_site, coef)
    return (temp_new, pressure_new, fresh.reshape(-1), velocity.reshape(-1))


def solution(mesh):
    block = P(None, "face", "tile")
    slot = P(BOTH, None, None)
    cells = P(BOTH)
    return jax.shard_map(
        local,
        mesh=mesh,
        in_specs=(block,) * 5 + (P(),) + (slot,) * 3 + (cells,) * 5,
        out_specs=(block, block, cells, cells),
        check_vma=False,
    )
```

```python
import functools

import jax
import jax.numpy as jnp
from jax import lax
from jax.experimental import pallas as pl
from jax.experimental.pallas import tpu as pltpu
from jax.sharding import PartitionSpec as P

SUBS = 2
EVP = 20
LEVELS = 8
ROWS = 8
LANES = 128
SOURCES = 128
ICE_ROWS = 16
FIELDS = 3 * LEVELS
SLAB = 56
TILES = 32
STAGED = (
    "press",
    "zonal",
    "merid",
    "motion",
    "strain",
    "resist",
    "frozen",
    "skin",
    "heat",
    "link",
    "site",
    "area",
    "target",
)

isentropic_lapse = 0.3
gravity_step = 0.5
floe_warmth = 2.0
floor_conductance = 1.0
relaxation = 0.5
stress_decay = 0.05
mobility = 0.3
water_drag = 0.1

BOTH = ("face", "tile")
VMEM = pl.BlockSpec(memory_space=pltpu.VMEM)
SMEM = pl.BlockSpec(memory_space=pltpu.SMEM)


def struct(*shape):
    return jax.ShapeDtypeStruct(shape, jnp.float32)


def kept(*shape):
    return pltpu.VMEM(shape, jnp.float32)


def near(values):
    return pltpu.with_memory_space_constraint(values, pltpu.VMEM)


def lanes_of(shape):
    return lax.broadcasted_iota(jnp.int32, shape, len(shape) - 1)


def rows_of(shape):
    return lax.broadcasted_iota(jnp.int32, shape, len(shape) - 2)


def stage_kernel(*refs):
    count = len(STAGED)
    sources, targets = refs[:count], refs[count : 2 * count]
    side_out, down_out, up_out, sems = refs[2 * count :]
    copies = [
        pltpu.make_async_copy(source, target, sems.at[at])
        for at, (source, target) in enumerate(zip(sources, targets))
    ]
    for copy in copies:
        copy.start()
    motion_ref, strain_ref, resist_ref, frozen_ref = targets[3:7]
    for copy in copies[:3]:
        copy.wait()
    lane = lanes_of((ROWS, LANES))
    packed = jnp.zeros((ROWS, LANES), jnp.float32)
    for field, ref in enumerate(targets[:3]):
        for level in range(LEVELS):
            cells = ref[level]
            at = 4 * (field * LEVELS + level)
            moved = pltpu.roll(cells, 2 + at, 1)
            packed = jnp.where((lane >= at) & (lane < at + 4), moved, packed)
            here = pl.ds(2 * (field * LEVELS + level), 2)
            down_out[here, :] = cells[:2]
            up_out[here, :] = cells[ROWS - 2 :]
    side_out[pl.ds(0, ROWS), :] = packed
    for copy in copies[3:7]:
        copy.wait()
    edge = jnp.zeros((1, LANES), jnp.float32)
    lane = lanes_of((1, LANES))
    for row, first, shift in ((ICE_ROWS - 1, 0, EVP), (0, 3, 0)):
        here = pl.ds(row, 1)
        strength = resist_ref[here] * (0.1 + 0.9 * frozen_ref[here].astype(jnp.float32))
        for at, cells in enumerate((motion_ref[here], strain_ref[here], strength), first):
            moved = pltpu.roll(cells, (EVP * at + shift) % LANES, 1)
            edge = jnp.where((lane >= EVP * at) & (lane < EVP * at + EVP), moved, edge)
    side_out[pl.ds(ROWS, ROWS), :] = jnp.broadcast_to(edge, (ROWS, LANES))
    for copy in copies[7:]:
        copy.wait()


def joined(left_ref, right_ref):
    here = pl.ds(0, ROWS)
    return jnp.where(lanes_of((ROWS, LANES)) % 4 < 2, left_ref[here], right_ref[here])


def corner_kernel(left_ref, right_ref, down_ref, up_ref, down_out, up_out):
    sides = joined(left_ref, right_ref)
    for slab_ref, out_ref, row in ((down_ref, down_out, 0), (up_ref, up_out, ROWS - 2)):
        out_ref[pl.ds(0, 2 * FIELDS), :] = slab_ref[pl.ds(0, 2 * FIELDS), :]
        out_ref[pl.ds(2 * FIELDS, 2), :] = sides[row : row + 2]
        out_ref[pl.ds(2 * FIELDS + 2, 1), :] = left_ref[pl.ds(ROWS, 1), :]
        out_ref[pl.ds(2 * FIELDS + 3, 5), :] = right_ref[pl.ds(ROWS, 5), :]


def look_up(table, high, low):
    shape = low.shape
    found = [None] * len(table)
    for row in range(table[0].shape[0]):
        here = high == row
        for at, values in enumerate(table):
            spread = jnp.broadcast_to(values[row : row + 1], shape)
            taken = jnp.take_along_axis(spread, low, axis=1, mode="promise_in_bounds")
            found[at] = taken if row == 0 else jnp.where(here, taken, found[at])
    return found


def columns_kernel(
    speed_ref,
    place_ref,
    p_ref,
    u_ref,
    v_ref,
    heat_ref,
    link_ref,
    site_ref,
    area_ref,
    left_ref,
    right_ref,
    below_ref,
    above_ref,
    press_out,
    coef_out,
    halo_out,
    slots_out,
    wide,
    sides,
):
    sides[pl.ds(0, ROWS), :] = joined(left_ref, right_ref)
    sides[pl.ds(8, 8), :] = jnp.zeros((8, LANES), jnp.float32)
    sides[pl.ds(8, 2), :] = above_ref[pl.ds(2 * FIELDS, 2), :]
    sides[pl.ds(14, 2), :] = below_ref[pl.ds(2 * FIELDS, 2), :]
    border = sides[...]
    temps = []
    for level in range(LEVELS):
        speed = speed_ref[level]
        now = []
        for field, ref in enumerate((p_ref, u_ref, v_ref)):
            at = field * LEVELS + level
            wide[at, pl.ds(0, ROWS), :] = ref[level]
            wide[at, pl.ds(8, 8), :] = jnp.zeros((8, LANES), jnp.float32)
            wide[at, pl.ds(8, 2), :] = above_ref[pl.ds(2 * at, 2), :]
            wide[at, pl.ds(14, 2), :] = below_ref[pl.ds(2 * at, 2), :]
            outer = pltpu.roll(border, (126 - 4 * at) % LANES, 1)
            now.append(jnp.concatenate([wide[at], outer], axis=1))
        press, zonal, merid = now
        for _ in range(SUBS):
            zonal = zonal - speed * (pltpu.roll(press, 15, 0) - press)
            merid = merid - speed * (pltpu.roll(press, 255, 1) - press)
            press = press - speed * (
                zonal - pltpu.roll(zonal, 1, 0) + merid - pltpu.roll(merid, 1, 1)
            )
        final = press[:ROWS, :LANES]
        press_out[level] = final
        temps.append(heat_ref[level] + isentropic_lapse * final)
    last_zonal = zonal[:ROWS, :LANES]
    last_merid = merid[:ROWS, :LANES]

    link = link_ref[0]
    gain = link / (1.0 + link)
    rest = temps[0] / (1.0 + link)
    coef_out[0] = gain
    coef_out[LEVELS] = rest
    for level in range(1, LEVELS - 1):
        earlier, link = link, link_ref[level]
        denom = 1.0 + earlier + link - earlier * gain
        gain = link / denom
        rest = (temps[level] + earlier * rest) / denom
        coef_out[level] = gain
        coef_out[LEVELS + level] = rest
    divisor = 1.0 + link * (1.0 - gain)
    beta = gravity_step / divisor
    gamma = (temps[LEVELS - 1] + link * rest) / divisor
    coef_out[LEVELS - 1] = beta
    coef_out[2 * LEVELS - 1] = gamma
    drag = link_ref[LEVELS - 1]
    weight = drag / (1.0 + drag * beta)
    stress = drag * (last_zonal + 0.5 * last_merid)

    site = site_ref[...]
    area = area_ref[...]
    found = look_up((weight, gamma, stress), site // LANES, site % LANES)
    slot_w = area * found[0]
    slots_out[pl.ds(0, SOURCES, stride=3), :] = slot_w
    slots_out[pl.ds(1, SOURCES, stride=3), :] = slot_w * found[1]
    slots_out[pl.ds(2, SOURCES, stride=3), :] = area * found[2]
    place = lax.rem(place_ref[0], TILES)
    at_row = lambda ref, row: ref[pl.ds(row, 1), :]
    before = jnp.where(place == 0, at_row(below_ref, 2 * FIELDS + 2), at_row(left_ref, ROWS))
    after = jnp.where(place == TILES - 1, at_row(above_ref, 2 * FIELDS + 3), at_row(right_ref, ROWS))
    for at in range(3):
        halo_out[pl.ds(at, 1), :] = pltpu.roll(before, LANES - EVP - EVP * at, 1)
        halo_out[pl.ds(4 + at, 1), :] = pltpu.roll(after, LANES - EVP * (at + 3), 1)


def in_three(values):
    first = values.astype(jnp.bfloat16)
    left = values - first.astype(jnp.float32)
    second = left.astype(jnp.bfloat16)
    third = (left - second.astype(jnp.float32)).astype(jnp.bfloat16)
    return first.astype(jnp.float32), second.astype(jnp.float32), third.astype(jnp.float32)


def segment_sums(read, index_ref, high_count, values, group=8):
    shape = (high_count, LANES)
    high_row = rows_of(shape)
    low_row = rows_of((LANES, LANES))
    count = 3 * values * high_count

    def step(block, total):
        start = pl.multiple_of(block * group, group)
        index = index_ref[pl.ds(start, group), :]
        high = index // LANES
        low = index % LANES
        parts = [part for value in range(values) for part in in_three(read(value, start, group))]
        carried, spread = [], []
        for row in range(group):
            here = high_row == high[row : row + 1]
            carried.append(
                jnp.concatenate(
                    [
                        jnp.where(here, jnp.broadcast_to(part[row : row + 1], shape), 0.0).astype(
                            jnp.bfloat16
                        )
                        for part in parts
                    ]
                    if high_count % 16 == 0
                    else [
                        jnp.concatenate(
                            [
                                jnp.where(here, jnp.broadcast_to(part[row : row + 1], shape), 0.0)
                                for part in parts
                            ],
                            axis=0,
                        ).astype(jnp.bfloat16)
                    ],
                    axis=0,
                )
            )
            spread.append(
                jnp.where(low_row == low[row : row + 1], 1.0, 0.0).astype(jnp.bfloat16)
            )
        return total + lax.dot_general(
            jnp.concatenate(carried, axis=1),
            jnp.concatenate(spread, axis=1),
            (((1,), (1,)), ((), ())),
            preferred_element_type=jnp.float32,
        )

    total = lax.fori_loop(0, SOURCES // group, step, jnp.zeros((count, LANES), jnp.float32))
    sums = []
    for value in range(values):
        at = 3 * value * high_count
        sums.append(
            total[at + 2 * high_count : at + 3 * high_count]
            + total[at + high_count : at + 2 * high_count]
            + total[at : at + high_count]
        )
    return sums


def ice_kernel(
    slots_ref, target_ref, skin_ref, frozen_ref, resist_ref, skin_out, flux_out, ice_out
):
    def read(value, start, group):
        return slots_ref[pl.ds(3 * start + value, group, stride=3), :]

    heat, warmth, tau = segment_sums(read, target_ref, ICE_ROWS, 3)
    skin = skin_ref[...]
    frozen = frozen_ref[...]
    fresh = jnp.where(
        frozen == 1,
        (floe_warmth * skin + warmth) / (floe_warmth + floor_conductance + heat),
        skin,
    )
    skin_out[...] = fresh
    target = target_ref[...]
    (at_floe,) = look_up((fresh,), target // LANES, target % LANES)
    flux_out[pl.ds(0, SOURCES, stride=2), :] = (
        slots_ref[pl.ds(0, SOURCES, stride=3), :] * at_floe
        - slots_ref[pl.ds(1, SOURCES, stride=3), :]
    )
    ends = jnp.where(
        lanes_of((1, LANES)) < LANES // 2, tau[0:1], tau[ICE_ROWS - 1 : ICE_ROWS]
    )
    flux_out[pl.ds(1, SOURCES, stride=2), :] = jnp.broadcast_to(ends, (SOURCES, LANES))
    ice_out[0] = resist_ref[...] * (0.1 + 0.9 * frozen.astype(jnp.float32))
    ice_out[1] = tau


def paired(even_rows, odd_rows):
    lane = lanes_of((ROWS, LANES))
    out = []
    for at in range(2):
        index = (2 * lane + at) % LANES
        out.append(
            jnp.where(
                lane < LANES // 2,
                jnp.take_along_axis(even_rows, index, axis=1, mode="promise_in_bounds"),
                jnp.take_along_axis(odd_rows, index, axis=1, mode="promise_in_bounds"),
            )
        )
    return out


def neighbourhood(even_rows, odd_rows, before, after):
    shape = (ROWS, LANES)
    lane = lanes_of(shape)
    row = rows_of(shape)
    own = paired(even_rows, odd_rows)
    behind = paired(jnp.broadcast_to(before, shape), jnp.broadcast_to(before, shape))
    ahead = paired(jnp.broadcast_to(after, shape), jnp.broadcast_to(after, shape))
    cells = {}
    for at in range(2):
        cells[at] = own[at]
        up = jnp.where(row == ROWS - 1, ahead[at], pltpu.roll(own[at], ROWS - 1, 0))
        down = jnp.where(row == 0, behind[at], pltpu.roll(own[at], 1, 0))
        for far in range(1, EVP // 2 + 1):
            cells[at + 2 * far] = pltpu.roll(
                jnp.where(lane < far, up, own[at]), LANES - far, 1
            )
            cells[at - 2 * far] = pltpu.roll(
                jnp.where(lane >= LANES - far, down, own[at]), far, 1
            )
    return cells


def drift(place, motion_ref, strain_ref, ice_ref, halo_ref, before_tau, after_tau, out_ref, held):
    even, odd = pl.ds(0, ROWS, stride=2), pl.ds(1, ROWS, stride=2)
    first = jnp.where(place == 0, 0.0, 1.0)
    last = jnp.where(place == SOURCES - 1, 0.0, 1.0)
    slow = 1.0 / (1.0 + mobility * water_drag)
    fade = 1.0 / (1.0 + stress_decay)
    arrays = (
        (motion_ref[even], motion_ref[odd], halo_ref[0:1], halo_ref[4:5], 1.0),
        (strain_ref[even], strain_ref[odd], halo_ref[1:2], halo_ref[5:6], mobility * slow),
        (
            ice_ref[0, even],
            ice_ref[0, odd],
            halo_ref[2:3],
            halo_ref[6:7],
            mobility * slow * relaxation * fade,
        ),
        (ice_ref[1, even], ice_ref[1, odd], before_tau, after_tau, mobility * slow),
    )
    for at, (even_rows, odd_rows, before, after, scale) in enumerate(arrays):
        cells = neighbourhood(
            even_rows * scale,
            odd_rows * scale,
            before * (first * scale),
            after * (last * scale),
        )
        for cell, values in cells.items():
            held[at, cell + EVP] = values
    shape = (ROWS, LANES)
    where = LANES * rows_of(shape) + lanes_of(shape)

    def inside(cell):
        end = (ROWS * LANES * 2 - cell) // 2
        return jnp.where((where == end) & (place == SOURCES - 1), 0.0, 1.0)

    width = 2 * EVP + 2
    velocity = [held[0, at] for at in range(width)]
    stress = [held[1, at] for at in range(width)]
    for turn in range(EVP):
        for at in range(turn, width - turn - 1):
            stress[at] = stress[at] * fade + held[2, at] * (velocity[at + 1] - velocity[at])
        for at in range(turn + 1, width - turn - 1):
            force = stress[at] - stress[at - 1] + held[3, at]
            if at >= EVP + 2 and at % 2 == 0:
                force = force * inside(at - EVP)
            velocity[at] = velocity[at] * slow + force
    lane = lanes_of(shape)
    for rows, half in ((even, 0), (odd, LANES // 2)):
        index = lane // 2 + half
        out_ref[rows] = jnp.where(
            lane % 2 == 0,
            jnp.take_along_axis(velocity[EVP], index, axis=1, mode="promise_in_bounds"),
            jnp.take_along_axis(velocity[EVP + 1], index, axis=1, mode="promise_in_bounds"),
        )


def last_kernel(
    place_ref,
    flux_ref,
    site_ref,
    coef_ref,
    motion_ref,
    strain_ref,
    ice_ref,
    halo_ref,
    heat_out,
    motion_out,
    held,
):
    def read(value, start, group):
        return flux_ref[pl.ds(2 * start, group, stride=2), :]

    (surface_flux,) = segment_sums(read, site_ref, ROWS, 1)
    below = coef_ref[LEVELS - 1] * surface_flux + coef_ref[2 * LEVELS - 1]
    heat_out[LEVELS - 1] = below
    for level in range(LEVELS - 2, -1, -1):
        below = coef_ref[level] * below + coef_ref[LEVELS + level]
        heat_out[level] = below
    place = place_ref[0]
    drift(
        place,
        motion_ref,
        strain_ref,
        ice_ref,
        halo_ref,
        flux_ref[pl.ds(2 * jnp.maximum(place - 1, 0) + 1, 1), :],
        flux_ref[pl.ds(2 * jnp.minimum(place + 1, SOURCES - 1) + 1, 1), :],
        motion_out,
        held,
    )


def ring(axis, step):
    count = lax.axis_size(axis)
    return [(i, (i + step) % count) for i in range(count)]


def exchanged(rows, count):
    blocks = rows.reshape(SOURCES, count, 1, LANES)
    blocks = lax.all_to_all(blocks, BOTH, split_axis=0, concat_axis=0, tiled=True)
    return near(blocks.reshape(SOURCES * count, LANES))


def local(
    squeeze_anomaly,
    eastward_airflow,
    northward_airflow,
    thermal_anomaly,
    diffusivity_link,
    sound_stability_ratio,
    overlay_source_site,
    overlay_target_floe,
    overlay_fraction,
    floe_skin_kelvin,
    frozen_indicator,
    floe_motion,
    floe_strain_tensor,
    floe_compress_resist,
):
    ice = (ICE_ROWS, LANES)
    slot = (SOURCES, LANES)
    arguments = dict(
        press=squeeze_anomaly,
        zonal=eastward_airflow,
        merid=northward_airflow,
        motion=floe_motion.reshape(ice),
        strain=floe_strain_tensor.reshape(ice),
        resist=floe_compress_resist.reshape(ice),
        frozen=frozen_indicator.reshape(ice),
        skin=floe_skin_kelvin.reshape(ice),
        heat=thermal_anomaly,
        link=diffusivity_link,
        site=overlay_source_site.reshape(slot),
        area=overlay_fraction.reshape(slot),
        target=overlay_target_floe.reshape(slot),
    )
    sources = [arguments[name] for name in STAGED]
    *staged, sides, down, up = pl.pallas_call(
        stage_kernel,
        out_shape=[pltpu.VMEM(source.shape, source.dtype) for source in sources]
        + [kept(2 * ROWS, LANES), kept(SLAB, LANES), kept(SLAB, LANES)],
        in_specs=[pl.BlockSpec(memory_space=pl.ANY)] * len(sources),
        out_specs=[VMEM] * (len(sources) + 3),
        scratch_shapes=[pltpu.SemaphoreType.DMA((len(sources),))],
    )(*sources)
    at = {name: near(values) for name, values in zip(STAGED, staged)}
    place = lax.axis_index(BOTH).astype(jnp.int32).reshape(1)

    left = near(lax.ppermute(sides, "tile", ring("tile", 1)))
    right = near(lax.ppermute(sides, "tile", ring("tile", -1)))
    down, up = pl.pallas_call(
        corner_kernel,
        out_shape=[kept(SLAB, LANES)] * 2,
        in_specs=[VMEM] * 4,
        out_specs=[VMEM] * 2,
    )(left, right, near(down), near(up))
    below = near(lax.ppermute(up, "face", ring("face", 1)))
    above = near(lax.ppermute(down, "face", ring("face", -1)))
    pressure_new, coef, halo, slots = pl.pallas_call(
        columns_kernel,
        out_shape=[
            struct(LEVELS, ROWS, LANES),
            kept(2 * LEVELS, ROWS, LANES),
            kept(8, LANES),
            struct(3 * SOURCES, LANES),
        ],
        in_specs=[SMEM] * 2 + [VMEM] * 11,
        out_specs=[VMEM] * 4,
        scratch_shapes=[
            pltpu.VMEM((FIELDS, 16, LANES), jnp.float32),
            pltpu.VMEM((16, LANES), jnp.float32),
        ],
    )(
        sound_stability_ratio,
        place,
        *(at[name] for name in ("press", "zonal", "merid", "heat", "link", "site", "area")),
        left,
        right,
        below,
        above,
    )
    arrived = exchanged(slots, 3)
    fresh, flux, ice_terms = pl.pallas_call(
        ice_kernel,
        out_shape=[struct(*ice), struct(2 * SOURCES, LANES), kept(2, *ice)],
        in_specs=[VMEM] * 5,
        out_specs=[VMEM] * 3,
    )(arrived, *(at[name] for name in ("target", "skin", "frozen", "resist")))
    returned = exchanged(flux, 2)
    temp_new, velocity = pl.pallas_call(
        last_kernel,
        out_shape=[struct(LEVELS, ROWS, LANES), struct(*ice)],
        in_specs=[SMEM] + [VMEM] * 7,
        out_specs=[VMEM] * 2,
        scratch_shapes=[pltpu.VMEM((4, 2 * EVP + 2, ROWS, LANES), jnp.float32)],
    )(
        place,
        returned,
        at["site"],
        near(coef),
        at["motion"],
        at["strain"],
        near(ice_terms),
        near(halo),
    )
    return (temp_new, pressure_new, fresh.reshape(-1), velocity.reshape(-1))


def solution(mesh):
    block = P(None, "face", "tile")
    slot = P(BOTH, None, None)
    cells = P(BOTH)
    return jax.shard_map(
        local,
        mesh=mesh,
        in_specs=(block,) * 5 + (P(),) + (slot,) * 3 + (cells,) * 5,
        out_specs=(block, block, cells, cells),
        check_vma=False,
    )
```

```python
import functools

import jax
import jax.numpy as jnp
from jax import lax
from jax.experimental import pallas as pl
from jax.experimental.pallas import tpu as pltpu
from jax.sharding import PartitionSpec as P

SUBS = 2
EVP = 20
LEVELS = 8
ROWS = 8
LANES = 128
SOURCES = 128
ICE_ROWS = 16
FIELDS = 3 * LEVELS
SLAB = 56
TILES = 32
STAGED = (
    "press",
    "zonal",
    "merid",
    "motion",
    "strain",
    "resist",
    "frozen",
    "skin",
    "heat",
    "link",
    "site",
    "area",
    "target",
)

isentropic_lapse = 0.3
gravity_step = 0.5
floe_warmth = 2.0
floor_conductance = 1.0
relaxation = 0.5
stress_decay = 0.05
mobility = 0.3
water_drag = 0.1

BOTH = ("face", "tile")
VMEM = pl.BlockSpec(memory_space=pltpu.VMEM)


def struct(*shape):
    return jax.ShapeDtypeStruct(shape, jnp.float32)


def kept(*shape):
    return pltpu.VMEM(shape, jnp.float32)


def near(values):
    return pltpu.with_memory_space_constraint(values, pltpu.VMEM)


def lanes_of(shape):
    return lax.broadcasted_iota(jnp.int32, shape, len(shape) - 1)


def rows_of(shape):
    return lax.broadcasted_iota(jnp.int32, shape, len(shape) - 2)


def stage_kernel(*refs):
    count = len(STAGED)
    speed_ref, *refs = refs
    sources, targets = refs[:count], refs[count : 2 * count]
    side_out, down_out, up_out, speed_out, speeds, sems = refs[2 * count :]
    speed_copy = pltpu.make_async_copy(speed_ref, speeds, sems.at[count])
    speed_copy.start()
    copies = [
        pltpu.make_async_copy(source, target, sems.at[at])
        for at, (source, target) in enumerate(zip(sources, targets))
    ]
    for copy in copies:
        copy.start()
    motion_ref, strain_ref, resist_ref, frozen_ref = targets[3:7]
    for copy in copies[:3]:
        copy.wait()
    lane = lanes_of((ROWS, LANES))
    packed = jnp.zeros((ROWS, LANES), jnp.float32)
    for field, ref in enumerate(targets[:3]):
        for level in range(LEVELS):
            cells = ref[level]
            at = 4 * (field * LEVELS + level)
            moved = pltpu.roll(cells, 2 + at, 1)
            packed = jnp.where((lane >= at) & (lane < at + 4), moved, packed)
            here = pl.ds(2 * (field * LEVELS + level), 2)
            down_out[here, :] = cells[:2]
            up_out[here, :] = cells[ROWS - 2 :]
    for copy in copies[3:7]:
        copy.wait()
    edge = jnp.zeros((1, LANES), jnp.float32)
    lane = lanes_of((1, LANES))
    for row, first, shift in ((ICE_ROWS - 1, 0, EVP), (0, 3, 0)):
        here = pl.ds(row, 1)
        strength = resist_ref[here] * (0.1 + 0.9 * frozen_ref[here].astype(jnp.float32))
        for at, cells in enumerate((motion_ref[here], strain_ref[here], strength), first):
            moved = pltpu.roll(cells, (EVP * at + shift) % LANES, 1)
            edge = jnp.where((lane >= EVP * at) & (lane < EVP * at + EVP), moved, edge)
    edge = jnp.broadcast_to(edge, (ROWS, LANES))
    side_out[pl.ds(0, ROWS), :] = packed
    side_out[pl.ds(ROWS, ROWS), :] = edge
    down_out[pl.ds(2 * FIELDS, 2), :] = packed[:2]
    up_out[pl.ds(2 * FIELDS, 2), :] = packed[ROWS - 2 :]
    down_out[pl.ds(2 * FIELDS + 2, 6), :] = edge[:6]
    up_out[pl.ds(2 * FIELDS + 2, 6), :] = edge[:6]
    speed_copy.wait()
    for level in range(LEVELS):
        speed_out[pl.ds(level, 1), :] = jnp.full((1, LANES), speeds[level])
    for copy in copies[7:]:
        copy.wait()


def side_kernel(side_ref, below_ref, above_ref, out_ref):
    out_ref[pl.ds(0, ROWS + 3), :] = side_ref[pl.ds(0, ROWS + 3), :]
    out_ref[pl.ds(8, 2), :] = above_ref[pl.ds(2 * FIELDS, 2), :]
    out_ref[pl.ds(11, 1), :] = below_ref[pl.ds(2 * FIELDS + 2, 1), :]
    out_ref[pl.ds(12, 2), :] = above_ref[pl.ds(2 * FIELDS + 2, 2), :]
    out_ref[pl.ds(14, 2), :] = below_ref[pl.ds(2 * FIELDS, 2), :]


def look_up(tables, index):
    high = index // LANES
    low = index % LANES
    found = [None] * len(tables)
    for row in range(len(tables[0])):
        here = high == row
        for at, rows in enumerate(tables):
            taken = jnp.take_along_axis(rows[row], low, axis=1, mode="promise_in_bounds")
            found[at] = taken if row == 0 else jnp.where(here, taken, found[at])
    return found


def spread_rows(table):
    return [
        jnp.broadcast_to(table[row : row + 1], (ROWS, LANES)) for row in range(table.shape[0])
    ]


def columns_kernel(
    speed_ref,
    p_ref,
    u_ref,
    v_ref,
    heat_ref,
    link_ref,
    site_ref,
    area_ref,
    left_ref,
    right_ref,
    below_ref,
    above_ref,
    press_out,
    coef_out,
    halo_out,
    slots_out,
    wide,
):
    shape = (2 * ROWS, LANES)
    border = jnp.where(lanes_of(shape) % 4 < 2, left_ref[...], right_ref[...])
    temps = []
    for level in range(LEVELS):
        speed = jnp.broadcast_to(speed_ref[pl.ds(level, 1), 0:1], (2 * ROWS, 2 * LANES))
        now = []
        for field, ref in enumerate((p_ref, u_ref, v_ref)):
            at = field * LEVELS + level
            wide[at, pl.ds(0, ROWS), :] = ref[level]
            wide[at, pl.ds(8, 8), :] = jnp.zeros((8, LANES), jnp.float32)
            wide[at, pl.ds(8, 2), :] = above_ref[pl.ds(2 * at, 2), :]
            wide[at, pl.ds(14, 2), :] = below_ref[pl.ds(2 * at, 2), :]
            outer = pltpu.roll(border, (126 - 4 * at) % LANES, 1)
            now.append(jnp.concatenate([wide[at], outer], axis=1))
        press, zonal, merid = now
        for _ in range(SUBS):
            zonal = zonal - speed * (pltpu.roll(press, 15, 0) - press)
            merid = merid - speed * (pltpu.roll(press, 255, 1) - press)
            press = press - speed * (
                zonal - pltpu.roll(zonal, 1, 0) + merid - pltpu.roll(merid, 1, 1)
            )
        final = press[:ROWS, :LANES]
        press_out[level] = final
        temps.append(heat_ref[level] + isentropic_lapse * final)
    last_zonal = zonal[:ROWS, :LANES]
    last_merid = merid[:ROWS, :LANES]

    link = link_ref[0]
    gain = link / (1.0 + link)
    rest = temps[0] / (1.0 + link)
    coef_out[0] = gain
    coef_out[LEVELS] = rest
    for level in range(1, LEVELS - 1):
        earlier, link = link, link_ref[level]
        denom = 1.0 + earlier + link - earlier * gain
        gain = link / denom
        rest = (temps[level] + earlier * rest) / denom
        coef_out[level] = gain
        coef_out[LEVELS + level] = rest
    divisor = 1.0 + link * (1.0 - gain)
    beta = gravity_step / divisor
    gamma = (temps[LEVELS - 1] + link * rest) / divisor
    coef_out[LEVELS - 1] = beta
    coef_out[2 * LEVELS - 1] = gamma
    drag = link_ref[LEVELS - 1]
    weight = drag / (1.0 + drag * beta)
    stress = drag * (last_zonal + 0.5 * last_merid)

    tables = [spread_rows(table) for table in (weight, gamma, stress)]
    for start in range(0, SOURCES, ROWS):
        here = pl.ds(start, ROWS)
        area = area_ref[here, :]
        found = look_up(tables, site_ref[here, :])
        slot_w = area * found[0]
        slots_out[pl.ds(3 * start, ROWS, stride=3), :] = slot_w
        slots_out[pl.ds(3 * start + 1, ROWS, stride=3), :] = slot_w * found[1]
        slots_out[pl.ds(3 * start + 2, ROWS, stride=3), :] = area * found[2]
    place = lax.axis_index("tile")
    before = jnp.where(place == 0, left_ref[pl.ds(11, 1), :], left_ref[pl.ds(10, 1), :])
    after = jnp.where(place == TILES - 1, right_ref[pl.ds(12, 1), :], right_ref[pl.ds(10, 1), :])
    for at in range(3):
        halo_out[pl.ds(at, 1), :] = pltpu.roll(before, LANES - EVP - EVP * at, 1)
        halo_out[pl.ds(4 + at, 1), :] = pltpu.roll(after, LANES - EVP * (at + 3), 1)


def in_three(values):
    first = values.astype(jnp.bfloat16)
    left = values - first.astype(jnp.float32)
    second = left.astype(jnp.bfloat16)
    third = (left - second.astype(jnp.float32)).astype(jnp.bfloat16)
    return first.astype(jnp.float32), second.astype(jnp.float32), third.astype(jnp.float32)


def segment_sums(read, index_ref, values, high_row, low_count, group=8):
    high_count = len(high_row)
    shape = (high_count, LANES)
    rows = rows_of(shape)
    high_here = sum(jnp.where(rows == at, high, 0) for high, at in enumerate(high_row))
    low_here = rows_of((low_count, LANES))
    count = 3 * values * high_count

    def step(block, total):
        start = pl.multiple_of(block * group, group)
        index = index_ref[pl.ds(start, group), :]
        high = index // low_count
        low = index % low_count
        parts = [part for value in range(values) for part in in_three(read(value, start, group))]
        carried, spread = [], []
        for row in range(group):
            here = high_here == high[row : row + 1]
            carried.append(
                jnp.concatenate(
                    [
                        jnp.where(here, jnp.broadcast_to(part[row : row + 1], shape), 0.0).astype(
                            jnp.bfloat16
                        )
                        for part in parts
                    ],
                    axis=0,
                )
            )
            spread.append(
                jnp.where(low_here == low[row : row + 1], 1.0, 0.0).astype(jnp.bfloat16)
            )
        return total + lax.dot_general(
            jnp.concatenate(carried, axis=1),
            jnp.concatenate(spread, axis=1),
            (((1,), (1,)), ((), ())),
            preferred_element_type=jnp.float32,
        )

    total = lax.fori_loop(
        0, SOURCES // group, step, jnp.zeros((count, low_count), jnp.float32), unroll=True
    )
    sums = []
    for value in range(values):
        at = 3 * value * high_count
        sums.append(
            total[at + 2 * high_count : at + 3 * high_count]
            + total[at + high_count : at + 2 * high_count]
            + total[at : at + high_count]
        )
    return sums


def ice_kernel(
    slots_ref, target_ref, skin_ref, frozen_ref, resist_ref, skin_out, flux_out, ice_out
):
    def read(value, start, group):
        return slots_ref[pl.ds(3 * start + value, group, stride=3), :]

    heat, warmth, tau = segment_sums(read, target_ref, 3, range(ICE_ROWS), LANES)
    skin = skin_ref[...]
    frozen = frozen_ref[...]
    fresh = jnp.where(
        frozen == 1,
        (floe_warmth * skin + warmth) / (floe_warmth + floor_conductance + heat),
        skin,
    )
    skin_out[...] = fresh
    table = spread_rows(fresh)
    for start in range(0, SOURCES, ROWS):
        (at_floe,) = look_up((table,), target_ref[pl.ds(start, ROWS), :])
        flux_out[pl.ds(2 * start, ROWS, stride=2), :] = (
            slots_ref[pl.ds(3 * start, ROWS, stride=3), :] * at_floe
            - slots_ref[pl.ds(3 * start + 1, ROWS, stride=3), :]
        )
    ends = jnp.where(
        lanes_of((1, LANES)) < LANES // 2, tau[0:1], tau[ICE_ROWS - 1 : ICE_ROWS]
    )
    flux_out[pl.ds(1, SOURCES, stride=2), :] = jnp.broadcast_to(ends, (SOURCES, LANES))
    ice_out[0] = resist_ref[...] * (0.1 + 0.9 * frozen.astype(jnp.float32))
    ice_out[1] = tau


def paired(even_rows, odd_rows):
    lane = lanes_of((ROWS, LANES))
    out = []
    for at in range(2):
        index = (2 * lane + at) % LANES
        out.append(
            jnp.where(
                lane < LANES // 2,
                jnp.take_along_axis(even_rows, index, axis=1, mode="promise_in_bounds"),
                jnp.take_along_axis(odd_rows, index, axis=1, mode="promise_in_bounds"),
            )
        )
    return out


def neighbourhood(even_rows, odd_rows, before, after):
    shape = (ROWS, LANES)
    lane = lanes_of(shape)
    row = rows_of(shape)
    own = paired(even_rows, odd_rows)
    behind = paired(jnp.broadcast_to(before, shape), jnp.broadcast_to(before, shape))
    ahead = paired(jnp.broadcast_to(after, shape), jnp.broadcast_to(after, shape))
    cells = {}
    for at in range(2):
        cells[at] = own[at]
        up = jnp.where(row == ROWS - 1, ahead[at], pltpu.roll(own[at], ROWS - 1, 0))
        down = jnp.where(row == 0, behind[at], pltpu.roll(own[at], 1, 0))
        for far in range(1, EVP // 2 + 1):
            cells[at + 2 * far] = pltpu.roll(
                jnp.where(lane < far, up, own[at]), LANES - far, 1
            )
            cells[at - 2 * far] = pltpu.roll(
                jnp.where(lane >= LANES - far, down, own[at]), far, 1
            )
    return cells


def drift(place, motion_ref, strain_ref, ice_ref, halo_ref, before_tau, after_tau, out_ref, held):
    even, odd = pl.ds(0, ROWS, stride=2), pl.ds(1, ROWS, stride=2)
    first = jnp.where(place == 0, 0.0, 1.0)
    last = jnp.where(place == SOURCES - 1, 0.0, 1.0)
    slow = 1.0 / (1.0 + mobility * water_drag)
    fade = 1.0 / (1.0 + stress_decay)
    arrays = (
        (motion_ref[even], motion_ref[odd], halo_ref[0:1], halo_ref[4:5], 1.0),
        (strain_ref[even], strain_ref[odd], halo_ref[1:2], halo_ref[5:6], mobility * slow),
        (
            ice_ref[0, even],
            ice_ref[0, odd],
            halo_ref[2:3],
            halo_ref[6:7],
            mobility * slow * relaxation * fade,
        ),
        (ice_ref[1, even], ice_ref[1, odd], before_tau, after_tau, mobility * slow),
    )
    for at, (even_rows, odd_rows, before, after, scale) in enumerate(arrays):
        cells = neighbourhood(
            even_rows * scale,
            odd_rows * scale,
            before * (first * scale),
            after * (last * scale),
        )
        for cell, values in cells.items():
            held[at, cell + EVP] = values
    shape = (ROWS, LANES)
    where = LANES * rows_of(shape) + lanes_of(shape)

    def inside(cell):
        end = (ROWS * LANES * 2 - cell) // 2
        return jnp.where((where == end) & (place == SOURCES - 1), 0.0, 1.0)

    width = 2 * EVP + 2
    velocity = [held[0, at] for at in range(width)]
    stress = [held[1, at] for at in range(width)]
    for turn in range(EVP):
        for at in range(turn, width - turn - 1):
            stress[at] = stress[at] * fade + held[2, at] * (velocity[at + 1] - velocity[at])
        for at in range(turn + 1, width - turn - 1):
            force = stress[at] - stress[at - 1] + held[3, at]
            if at >= EVP + 2 and at % 2 == 0:
                force = force * inside(at - EVP)
            velocity[at] = velocity[at] * slow + force
    lane = lanes_of(shape)
    for rows, half in ((even, 0), (odd, LANES // 2)):
        index = lane // 2 + half
        out_ref[rows] = jnp.where(
            lane % 2 == 0,
            jnp.take_along_axis(velocity[EVP], index, axis=1, mode="promise_in_bounds"),
            jnp.take_along_axis(velocity[EVP + 1], index, axis=1, mode="promise_in_bounds"),
        )


def last_kernel(
    flux_ref,
    site_ref,
    coef_ref,
    motion_ref,
    strain_ref,
    ice_ref,
    halo_ref,
    heat_out,
    motion_out,
    held,
):
    def read(value, start, group):
        return flux_ref[pl.ds(2 * start, group, stride=2), :]

    order = [ROWS * (half % 2) + half // 2 for half in range(2 * ROWS)]
    (halves,) = segment_sums(read, site_ref, 1, order, LANES // 2)
    surface_flux = jnp.concatenate([halves[:ROWS], halves[ROWS:]], axis=1)
    below = coef_ref[LEVELS - 1] * surface_flux + coef_ref[2 * LEVELS - 1]
    heat_out[LEVELS - 1] = below
    for level in range(LEVELS - 2, -1, -1):
        below = coef_ref[level] * below + coef_ref[LEVELS + level]
        heat_out[level] = below
    place = lax.axis_index("face") * TILES + lax.axis_index("tile")
    drift(
        place,
        motion_ref,
        strain_ref,
        ice_ref,
        halo_ref,
        flux_ref[pl.ds(2 * jnp.maximum(place - 1, 0) + 1, 1), :],
        flux_ref[pl.ds(2 * jnp.minimum(place + 1, SOURCES - 1) + 1, 1), :],
        motion_out,
        held,
    )


def ring(axis, step):
    count = lax.axis_size(axis)
    return [(i, (i + step) % count) for i in range(count)]


def exchanged(rows, count):
    blocks = rows.reshape(SOURCES, count, 1, LANES)
    blocks = lax.all_to_all(blocks, BOTH, split_axis=0, concat_axis=0, tiled=True)
    return near(blocks.reshape(SOURCES * count, LANES))


def local(
    squeeze_anomaly,
    eastward_airflow,
    northward_airflow,
    thermal_anomaly,
    diffusivity_link,
    sound_stability_ratio,
    overlay_source_site,
    overlay_target_floe,
    overlay_fraction,
    floe_skin_kelvin,
    frozen_indicator,
    floe_motion,
    floe_strain_tensor,
    floe_compress_resist,
):
    ice = (ICE_ROWS, LANES)
    slot = (SOURCES, LANES)
    arguments = dict(
        press=squeeze_anomaly,
        zonal=eastward_airflow,
        merid=northward_airflow,
        motion=floe_motion.reshape(ice),
        strain=floe_strain_tensor.reshape(ice),
        resist=floe_compress_resist.reshape(ice),
        frozen=frozen_indicator.reshape(ice),
        skin=floe_skin_kelvin.reshape(ice),
        heat=thermal_anomaly,
        link=diffusivity_link,
        site=overlay_source_site.reshape(slot),
        area=overlay_fraction.reshape(slot),
        target=overlay_target_floe.reshape(slot),
    )
    sources = [arguments[name] for name in STAGED]
    *staged, sides, down, up, speeds = pl.pallas_call(
        stage_kernel,
        out_shape=[pltpu.VMEM(source.shape, source.dtype) for source in sources]
        + [kept(2 * ROWS, LANES), kept(SLAB, LANES), kept(SLAB, LANES), kept(LEVELS, LANES)],
        in_specs=[pl.BlockSpec(memory_space=pl.ANY)] * (len(sources) + 1),
        out_specs=[VMEM] * (len(sources) + 4),
        scratch_shapes=[
            pltpu.SMEM((LEVELS,), jnp.float32),
            pltpu.SemaphoreType.DMA((len(sources) + 1,)),
        ],
    )(sound_stability_ratio, *sources)
    at = {name: near(values) for name, values in zip(STAGED, staged)}

    below = near(lax.ppermute(up, "face", ring("face", 1)))
    above = near(lax.ppermute(down, "face", ring("face", -1)))
    sides = pl.pallas_call(
        side_kernel, out_shape=kept(2 * ROWS, LANES), in_specs=[VMEM] * 3, out_specs=VMEM
    )(near(sides), below, above)
    left = near(lax.ppermute(sides, "tile", ring("tile", 1)))
    right = near(lax.ppermute(sides, "tile", ring("tile", -1)))
    pressure_new, coef, halo, slots = pl.pallas_call(
        columns_kernel,
        out_shape=[
            struct(LEVELS, ROWS, LANES),
            kept(2 * LEVELS, ROWS, LANES),
            kept(8, LANES),
            struct(3 * SOURCES, LANES),
        ],
        in_specs=[VMEM] * 12,
        out_specs=[VMEM] * 4,
        scratch_shapes=[pltpu.VMEM((FIELDS, 16, LANES), jnp.float32)],
    )(
        near(speeds),
        *(at[name] for name in ("press", "zonal", "merid", "heat", "link", "site", "area")),
        left,
        right,
        below,
        above,
    )
    arrived = exchanged(slots, 3)
    fresh, flux, ice_terms = pl.pallas_call(
        ice_kernel,
        out_shape=[struct(*ice), struct(2 * SOURCES, LANES), kept(2, *ice)],
        in_specs=[VMEM] * 5,
        out_specs=[VMEM] * 3,
    )(arrived, *(at[name] for name in ("target", "skin", "frozen", "resist")))
    returned = exchanged(flux, 2)
    temp_new, velocity = pl.pallas_call(
        last_kernel,
        out_shape=[struct(LEVELS, ROWS, LANES), struct(*ice)],
        in_specs=[VMEM] * 7,
        out_specs=[VMEM] * 2,
        scratch_shapes=[pltpu.VMEM((4, 2 * EVP + 2, ROWS, LANES), jnp.float32)],
    )(
        returned,
        at["site"],
        near(coef),
        at["motion"],
        at["strain"],
        near(ice_terms),
        near(halo),
    )
    return (temp_new, pressure_new, fresh.reshape(-1), velocity.reshape(-1))


def solution(mesh):
    block = P(None, "face", "tile")
    slot = P(BOTH, None, None)
    cells = P(BOTH)
    return jax.shard_map(
        local,
        mesh=mesh,
        in_specs=(block,) * 5 + (P(),) + (slot,) * 3 + (cells,) * 5,
        out_specs=(block, block, cells, cells),
        check_vma=False,
    )
```

```python
import functools

import jax
import jax.numpy as jnp
from jax import lax
from jax.experimental import pallas as pl
from jax.experimental.pallas import tpu as pltpu
from jax.sharding import PartitionSpec as P

SUBS = 2
EVP = 20
LEVELS = 8
ROWS = 8
LANES = 128
SOURCES = 128
ICE_ROWS = 16
FIELDS = 3 * LEVELS
SLAB = 56
TILES = 32
STAGED = (
    "press",
    "zonal",
    "merid",
    "motion",
    "strain",
    "resist",
    "frozen",
    "skin",
    "heat",
    "link",
    "site",
    "area",
    "target",
)

isentropic_lapse = 0.3
gravity_step = 0.5
floe_warmth = 2.0
floor_conductance = 1.0
relaxation = 0.5
stress_decay = 0.05
mobility = 0.3
water_drag = 0.1

BOTH = ("face", "tile")
VMEM = pl.BlockSpec(memory_space=pltpu.VMEM)


def struct(*shape):
    return jax.ShapeDtypeStruct(shape, jnp.float32)


def kept(*shape):
    return pltpu.VMEM(shape, jnp.float32)


def near(values):
    return pltpu.with_memory_space_constraint(values, pltpu.VMEM)


def lanes_of(shape):
    return lax.broadcasted_iota(jnp.int32, shape, len(shape) - 1)


def rows_of(shape):
    return lax.broadcasted_iota(jnp.int32, shape, len(shape) - 2)


def stage_kernel(*refs):
    count = len(STAGED)
    speed_ref, *refs = refs
    sources, targets = refs[:count], refs[count : 2 * count]
    side_out, down_out, up_out, speed_out, speeds, sems = refs[2 * count :]
    speed_copy = pltpu.make_async_copy(speed_ref, speeds, sems.at[count])
    speed_copy.start()
    copies = [
        pltpu.make_async_copy(source, target, sems.at[at])
        for at, (source, target) in enumerate(zip(sources, targets))
    ]
    for copy in copies:
        copy.start()
    motion_ref, strain_ref, resist_ref, frozen_ref = targets[3:7]
    for copy in copies[:3]:
        copy.wait()
    lane = lanes_of((ROWS, LANES))
    packed = jnp.zeros((ROWS, LANES), jnp.float32)
    for field, ref in enumerate(targets[:3]):
        for level in range(LEVELS):
            cells = ref[level]
            at = 4 * (field * LEVELS + level)
            moved = pltpu.roll(cells, 2 + at, 1)
            packed = jnp.where((lane >= at) & (lane < at + 4), moved, packed)
            here = pl.ds(2 * (field * LEVELS + level), 2)
            down_out[here, :] = cells[:2]
            up_out[here, :] = cells[ROWS - 2 :]
    for copy in copies[3:7]:
        copy.wait()
    edge = jnp.zeros((1, LANES), jnp.float32)
    lane = lanes_of((1, LANES))
    for row, first, shift in ((ICE_ROWS - 1, 0, EVP), (0, 3, 0)):
        here = pl.ds(row, 1)
        strength = resist_ref[here] * (0.1 + 0.9 * frozen_ref[here].astype(jnp.float32))
        for at, cells in enumerate((motion_ref[here], strain_ref[here], strength), first):
            moved = pltpu.roll(cells, (EVP * at + shift) % LANES, 1)
            edge = jnp.where((lane >= EVP * at) & (lane < EVP * at + EVP), moved, edge)
    edge = jnp.broadcast_to(edge, (ROWS, LANES))
    side_out[pl.ds(0, ROWS), :] = packed
    side_out[pl.ds(ROWS, ROWS), :] = edge
    down_out[pl.ds(2 * FIELDS, 2), :] = packed[:2]
    up_out[pl.ds(2 * FIELDS, 2), :] = packed[ROWS - 2 :]
    down_out[pl.ds(2 * FIELDS + 2, 6), :] = edge[:6]
    up_out[pl.ds(2 * FIELDS + 2, 6), :] = edge[:6]
    speed_copy.wait()
    for level in range(LEVELS):
        speed_out[pl.ds(level, 1), :] = jnp.full((1, LANES), speeds[level])
    for copy in copies[7:]:
        copy.wait()


def side_kernel(side_ref, below_ref, above_ref, out_ref):
    out_ref[pl.ds(0, ROWS + 3), :] = side_ref[pl.ds(0, ROWS + 3), :]
    out_ref[pl.ds(8, 2), :] = above_ref[pl.ds(2 * FIELDS, 2), :]
    out_ref[pl.ds(11, 1), :] = below_ref[pl.ds(2 * FIELDS + 2, 1), :]
    out_ref[pl.ds(12, 2), :] = above_ref[pl.ds(2 * FIELDS + 2, 2), :]
    out_ref[pl.ds(14, 2), :] = below_ref[pl.ds(2 * FIELDS, 2), :]


def look_up(tables, index):
    high = index // LANES
    low = index % LANES
    found = [None] * len(tables)
    for row in range(len(tables[0])):
        here = high == row
        for at, rows in enumerate(tables):
            taken = jnp.take_along_axis(rows[row], low, axis=1, mode="promise_in_bounds")
            found[at] = taken if row == 0 else jnp.where(here, taken, found[at])
    return found


def spread_rows(table):
    return [
        jnp.broadcast_to(table[row : row + 1], (ROWS, LANES)) for row in range(table.shape[0])
    ]


def columns_kernel(
    speed_ref,
    p_ref,
    u_ref,
    v_ref,
    heat_ref,
    link_ref,
    below_ref,
    above_ref,
    site_ref,
    area_ref,
    twin_ref,
    cross_ref,
    press_out,
    coef_out,
    halo_out,
    slots_out,
    wide,
):
    shape = (2 * ROWS, LANES)
    place = lax.axis_index("tile")
    even = place % 2 == 0
    left = jnp.where(even, cross_ref[...], twin_ref[...])
    right = jnp.where(even, twin_ref[...], cross_ref[...])
    border = jnp.where(lanes_of(shape) % 4 < 2, left, right)
    temps = []
    for level in range(LEVELS):
        speed = jnp.broadcast_to(speed_ref[pl.ds(level, 1), 0:1], (2 * ROWS, 2 * LANES))
        now = []
        for field, ref in enumerate((p_ref, u_ref, v_ref)):
            at = field * LEVELS + level
            wide[at, pl.ds(0, ROWS), :] = ref[level]
            wide[at, pl.ds(8, 8), :] = jnp.zeros((8, LANES), jnp.float32)
            wide[at, pl.ds(8, 2), :] = above_ref[pl.ds(2 * at, 2), :]
            wide[at, pl.ds(14, 2), :] = below_ref[pl.ds(2 * at, 2), :]
            outer = pltpu.roll(border, (126 - 4 * at) % LANES, 1)
            now.append(jnp.concatenate([wide[at], outer], axis=1))
        press, zonal, merid = now
        for _ in range(SUBS):
            zonal = zonal - speed * (pltpu.roll(press, 15, 0) - press)
            merid = merid - speed * (pltpu.roll(press, 255, 1) - press)
            press = press - speed * (
                zonal - pltpu.roll(zonal, 1, 0) + merid - pltpu.roll(merid, 1, 1)
            )
        final = press[:ROWS, :LANES]
        press_out[level] = final
        temps.append(heat_ref[level] + isentropic_lapse * final)
    last_zonal = zonal[:ROWS, :LANES]
    last_merid = merid[:ROWS, :LANES]

    link = link_ref[0]
    gain = link / (1.0 + link)
    rest = temps[0] / (1.0 + link)
    coef_out[0] = gain
    coef_out[LEVELS] = rest
    for level in range(1, LEVELS - 1):
        earlier, link = link, link_ref[level]
        denom = 1.0 + earlier + link - earlier * gain
        gain = link / denom
        rest = (temps[level] + earlier * rest) / denom
        coef_out[level] = gain
        coef_out[LEVELS + level] = rest
    divisor = 1.0 + link * (1.0 - gain)
    beta = gravity_step / divisor
    gamma = (temps[LEVELS - 1] + link * rest) / divisor
    coef_out[LEVELS - 1] = beta
    coef_out[2 * LEVELS - 1] = gamma
    drag = link_ref[LEVELS - 1]
    weight = drag / (1.0 + drag * beta)
    stress = drag * (last_zonal + 0.5 * last_merid)

    tables = [spread_rows(table) for table in (weight, gamma, stress)]
    for start in range(0, SOURCES, ROWS):
        here = pl.ds(start, ROWS)
        area = area_ref[here, :]
        found = look_up(tables, site_ref[here, :])
        slot_w = area * found[0]
        slots_out[pl.ds(3 * start, ROWS, stride=3), :] = slot_w
        slots_out[pl.ds(3 * start + 1, ROWS, stride=3), :] = slot_w * found[1]
        slots_out[pl.ds(3 * start + 2, ROWS, stride=3), :] = area * found[2]
    before = jnp.where(place == 0, left[11:12], left[10:11])
    after = jnp.where(place == TILES - 1, right[12:13], right[10:11])
    for at in range(3):
        halo_out[pl.ds(at, 1), :] = pltpu.roll(before, LANES - EVP - EVP * at, 1)
        halo_out[pl.ds(4 + at, 1), :] = pltpu.roll(after, LANES - EVP * (at + 3), 1)


def in_three(values):
    first = values.astype(jnp.bfloat16)
    left = values - first.astype(jnp.float32)
    second = left.astype(jnp.bfloat16)
    third = (left - second.astype(jnp.float32)).astype(jnp.bfloat16)
    return first.astype(jnp.float32), second.astype(jnp.float32), third.astype(jnp.float32)


def segment_sums(read, index_ref, values, high_row, low_count, group=8):
    high_count = len(high_row)
    shape = (high_count, LANES)
    rows = rows_of(shape)
    high_here = sum(jnp.where(rows == at, high, 0) for high, at in enumerate(high_row))
    low_here = rows_of((low_count, LANES))
    count = 3 * values * high_count

    def step(block, total):
        start = pl.multiple_of(block * group, group)
        index = index_ref[pl.ds(start, group), :]
        high = index // low_count
        low = index % low_count
        parts = [part for value in range(values) for part in in_three(read(value, start, group))]
        carried, spread = [], []
        for row in range(group):
            here = high_here == high[row : row + 1]
            carried.append(
                jnp.concatenate(
                    [
                        jnp.where(here, jnp.broadcast_to(part[row : row + 1], shape), 0.0).astype(
                            jnp.bfloat16
                        )
                        for part in parts
                    ],
                    axis=0,
                )
            )
            spread.append(
                jnp.where(low_here == low[row : row + 1], 1.0, 0.0).astype(jnp.bfloat16)
            )
        return total + lax.dot_general(
            jnp.concatenate(carried, axis=1),
            jnp.concatenate(spread, axis=1),
            (((1,), (1,)), ((), ())),
            preferred_element_type=jnp.float32,
        )

    total = lax.fori_loop(
        0, SOURCES // group, step, jnp.zeros((count, low_count), jnp.float32), unroll=True
    )
    sums = []
    for value in range(values):
        at = 3 * value * high_count
        sums.append(
            total[at + 2 * high_count : at + 3 * high_count]
            + total[at + high_count : at + 2 * high_count]
            + total[at : at + high_count]
        )
    return sums


def ice_kernel(
    slots_ref, target_ref, skin_ref, frozen_ref, resist_ref, skin_out, flux_out, ice_out
):
    def read(value, start, group):
        return slots_ref[pl.ds(3 * start + value, group, stride=3), :]

    heat, warmth, tau = segment_sums(read, target_ref, 3, range(ICE_ROWS), LANES)
    skin = skin_ref[...]
    frozen = frozen_ref[...]
    fresh = jnp.where(
        frozen == 1,
        (floe_warmth * skin + warmth) / (floe_warmth + floor_conductance + heat),
        skin,
    )
    skin_out[...] = fresh
    table = spread_rows(fresh)
    for start in range(0, SOURCES, ROWS):
        (at_floe,) = look_up((table,), target_ref[pl.ds(start, ROWS), :])
        flux_out[pl.ds(2 * start, ROWS, stride=2), :] = (
            slots_ref[pl.ds(3 * start, ROWS, stride=3), :] * at_floe
            - slots_ref[pl.ds(3 * start + 1, ROWS, stride=3), :]
        )
    ends = jnp.where(
        lanes_of((1, LANES)) < LANES // 2, tau[0:1], tau[ICE_ROWS - 1 : ICE_ROWS]
    )
    flux_out[pl.ds(1, SOURCES, stride=2), :] = jnp.broadcast_to(ends, (SOURCES, LANES))
    ice_out[0] = resist_ref[...] * (0.1 + 0.9 * frozen.astype(jnp.float32))
    ice_out[1] = tau


def paired(even_rows, odd_rows):
    lane = lanes_of((ROWS, LANES))
    out = []
    for at in range(2):
        index = (2 * lane + at) % LANES
        out.append(
            jnp.where(
                lane < LANES // 2,
                jnp.take_along_axis(even_rows, index, axis=1, mode="promise_in_bounds"),
                jnp.take_along_axis(odd_rows, index, axis=1, mode="promise_in_bounds"),
            )
        )
    return out


def neighbourhood(even_rows, odd_rows, before, after):
    shape = (ROWS, LANES)
    lane = lanes_of(shape)
    row = rows_of(shape)
    own = paired(even_rows, odd_rows)
    behind = paired(jnp.broadcast_to(before, shape), jnp.broadcast_to(before, shape))
    ahead = paired(jnp.broadcast_to(after, shape), jnp.broadcast_to(after, shape))
    cells = {}
    for at in range(2):
        cells[at] = own[at]
        up = jnp.where(row == ROWS - 1, ahead[at], pltpu.roll(own[at], ROWS - 1, 0))
        down = jnp.where(row == 0, behind[at], pltpu.roll(own[at], 1, 0))
        for far in range(1, EVP // 2 + 1):
            cells[at + 2 * far] = pltpu.roll(
                jnp.where(lane < far, up, own[at]), LANES - far, 1
            )
            cells[at - 2 * far] = pltpu.roll(
                jnp.where(lane >= LANES - far, down, own[at]), far, 1
            )
    return cells


def drift(place, motion_ref, strain_ref, ice_ref, halo_ref, before_tau, after_tau, out_ref, held):
    even, odd = pl.ds(0, ROWS, stride=2), pl.ds(1, ROWS, stride=2)
    first = jnp.where(place == 0, 0.0, 1.0)
    last = jnp.where(place == SOURCES - 1, 0.0, 1.0)
    slow = 1.0 / (1.0 + mobility * water_drag)
    fade = 1.0 / (1.0 + stress_decay)
    arrays = (
        (motion_ref[even], motion_ref[odd], halo_ref[0:1], halo_ref[4:5], 1.0),
        (strain_ref[even], strain_ref[odd], halo_ref[1:2], halo_ref[5:6], mobility * slow),
        (
            ice_ref[0, even],
            ice_ref[0, odd],
            halo_ref[2:3],
            halo_ref[6:7],
            mobility * slow * relaxation * fade,
        ),
        (ice_ref[1, even], ice_ref[1, odd], before_tau, after_tau, mobility * slow),
    )
    for at, (even_rows, odd_rows, before, after, scale) in enumerate(arrays):
        cells = neighbourhood(
            even_rows * scale,
            odd_rows * scale,
            before * (first * scale),
            after * (last * scale),
        )
        for cell, values in cells.items():
            held[at, cell + EVP] = values
    shape = (ROWS, LANES)
    where = LANES * rows_of(shape) + lanes_of(shape)

    def inside(cell):
        end = (ROWS * LANES * 2 - cell) // 2
        return jnp.where((where == end) & (place == SOURCES - 1), 0.0, 1.0)

    width = 2 * EVP + 2
    velocity = [held[0, at] for at in range(width)]
    stress = [held[1, at] for at in range(width)]
    for turn in range(EVP):
        for at in range(turn, width - turn - 1):
            stress[at] = stress[at] * fade + held[2, at] * (velocity[at + 1] - velocity[at])
        for at in range(turn + 1, width - turn - 1):
            force = stress[at] - stress[at - 1] + held[3, at]
            if at >= EVP + 2 and at % 2 == 0:
                force = force * inside(at - EVP)
            velocity[at] = velocity[at] * slow + force
    lane = lanes_of(shape)
    for rows, half in ((even, 0), (odd, LANES // 2)):
        index = lane // 2 + half
        out_ref[rows] = jnp.where(
            lane % 2 == 0,
            jnp.take_along_axis(velocity[EVP], index, axis=1, mode="promise_in_bounds"),
            jnp.take_along_axis(velocity[EVP + 1], index, axis=1, mode="promise_in_bounds"),
        )


def last_kernel(
    flux_ref,
    site_ref,
    coef_ref,
    motion_ref,
    strain_ref,
    ice_ref,
    halo_ref,
    heat_out,
    motion_out,
    held,
):
    def read(value, start, group):
        return flux_ref[pl.ds(2 * start, group, stride=2), :]

    order = [ROWS * (half % 2) + half // 2 for half in range(2 * ROWS)]
    (halves,) = segment_sums(read, site_ref, 1, order, LANES // 2)
    surface_flux = jnp.concatenate([halves[:ROWS], halves[ROWS:]], axis=1)
    below = coef_ref[LEVELS - 1] * surface_flux + coef_ref[2 * LEVELS - 1]
    heat_out[LEVELS - 1] = below
    for level in range(LEVELS - 2, -1, -1):
        below = coef_ref[level] * below + coef_ref[LEVELS + level]
        heat_out[level] = below
    place = lax.axis_index("face") * TILES + lax.axis_index("tile")
    drift(
        place,
        motion_ref,
        strain_ref,
        ice_ref,
        halo_ref,
        flux_ref[pl.ds(2 * jnp.maximum(place - 1, 0) + 1, 1), :],
        flux_ref[pl.ds(2 * jnp.minimum(place + 1, SOURCES - 1) + 1, 1), :],
        motion_out,
        held,
    )


def ring(axis, step):
    count = lax.axis_size(axis)
    return [(i, (i + step) % count) for i in range(count)]


def swaps(axis, first):
    count = lax.axis_size(axis)
    pairs = [(i, (i + 1) % count) for i in range(first, count, 2)]
    return sorted(pairs + [(b, a) for a, b in pairs])


def exchanged(rows, count):
    blocks = rows.reshape(SOURCES, count, 1, LANES)
    blocks = lax.all_to_all(blocks, BOTH, split_axis=0, concat_axis=0, tiled=True)
    return near(blocks.reshape(SOURCES * count, LANES))


def local(
    squeeze_anomaly,
    eastward_airflow,
    northward_airflow,
    thermal_anomaly,
    diffusivity_link,
    sound_stability_ratio,
    overlay_source_site,
    overlay_target_floe,
    overlay_fraction,
    floe_skin_kelvin,
    frozen_indicator,
    floe_motion,
    floe_strain_tensor,
    floe_compress_resist,
):
    ice = (ICE_ROWS, LANES)
    slot = (SOURCES, LANES)
    arguments = dict(
        press=squeeze_anomaly,
        zonal=eastward_airflow,
        merid=northward_airflow,
        motion=floe_motion.reshape(ice),
        strain=floe_strain_tensor.reshape(ice),
        resist=floe_compress_resist.reshape(ice),
        frozen=frozen_indicator.reshape(ice),
        skin=floe_skin_kelvin.reshape(ice),
        heat=thermal_anomaly,
        link=diffusivity_link,
        site=overlay_source_site.reshape(slot),
        area=overlay_fraction.reshape(slot),
        target=overlay_target_floe.reshape(slot),
    )
    sources = [arguments[name] for name in STAGED]
    *staged, sides, down, up, speeds = pl.pallas_call(
        stage_kernel,
        out_shape=[pltpu.VMEM(source.shape, source.dtype) for source in sources]
        + [kept(2 * ROWS, LANES), kept(SLAB, LANES), kept(SLAB, LANES), kept(LEVELS, LANES)],
        in_specs=[pl.BlockSpec(memory_space=pl.ANY)] * (len(sources) + 1),
        out_specs=[VMEM] * (len(sources) + 4),
        scratch_shapes=[
            pltpu.SMEM((LEVELS,), jnp.float32),
            pltpu.SemaphoreType.DMA((len(sources) + 1,)),
        ],
    )(sound_stability_ratio, *sources)
    at = {name: near(values) for name, values in zip(STAGED, staged)}

    below = near(lax.ppermute(up, "face", ring("face", 1)))
    above = near(lax.ppermute(down, "face", ring("face", -1)))
    sides = pl.pallas_call(
        side_kernel, out_shape=kept(2 * ROWS, LANES), in_specs=[VMEM] * 3, out_specs=VMEM
    )(near(sides), below, above)
    twin = near(lax.ppermute(sides, "tile", swaps("tile", 0)))
    cross = near(lax.ppermute(sides, "tile", swaps("tile", 1)))
    pressure_new, coef, halo, slots = pl.pallas_call(
        columns_kernel,
        out_shape=[
            struct(LEVELS, ROWS, LANES),
            kept(2 * LEVELS, ROWS, LANES),
            kept(8, LANES),
            struct(3 * SOURCES, LANES),
        ],
        in_specs=[VMEM] * 12,
        out_specs=[VMEM] * 4,
        scratch_shapes=[pltpu.VMEM((FIELDS, 16, LANES), jnp.float32)],
    )(
        near(speeds),
        *(at[name] for name in ("press", "zonal", "merid", "heat", "link")),
        below,
        above,
        at["site"],
        at["area"],
        twin,
        cross,
    )
    arrived = exchanged(slots, 3)
    fresh, flux, ice_terms = pl.pallas_call(
        ice_kernel,
        out_shape=[struct(*ice), struct(2 * SOURCES, LANES), kept(2, *ice)],
        in_specs=[VMEM] * 5,
        out_specs=[VMEM] * 3,
    )(arrived, *(at[name] for name in ("target", "skin", "frozen", "resist")))
    returned = exchanged(flux, 2)
    temp_new, velocity = pl.pallas_call(
        last_kernel,
        out_shape=[struct(LEVELS, ROWS, LANES), struct(*ice)],
        in_specs=[VMEM] * 7,
        out_specs=[VMEM] * 2,
        scratch_shapes=[pltpu.VMEM((4, 2 * EVP + 2, ROWS, LANES), jnp.float32)],
    )(
        returned,
        at["site"],
        near(coef),
        at["motion"],
        at["strain"],
        near(ice_terms),
        near(halo),
    )
    return (temp_new, pressure_new, fresh.reshape(-1), velocity.reshape(-1))


def solution(mesh):
    block = P(None, "face", "tile")
    slot = P(BOTH, None, None)
    cells = P(BOTH)
    return jax.shard_map(
        local,
        mesh=mesh,
        in_specs=(block,) * 5 + (P(),) + (slot,) * 3 + (cells,) * 5,
        out_specs=(block, block, cells, cells),
        check_vma=False,
    )
```

```python
import functools

import jax
import jax.numpy as jnp
from jax import lax
from jax.experimental import pallas as pl
from jax.experimental.pallas import tpu as pltpu
from jax.sharding import PartitionSpec as P

SUBS = 2
EVP = 20
LEVELS = 8
ROWS = 8
LANES = 128
SOURCES = 128
ICE_ROWS = 16
FIELDS = 3 * LEVELS
SLAB = 56
TILES = 32
STAGED = ("press", "zonal", "merid", "motion", "strain", "resist", "frozen")
AFTER = ("link", "site", "area", "heat", "target", "skin")

isentropic_lapse = 0.3
gravity_step = 0.5
floe_warmth = 2.0
floor_conductance = 1.0
relaxation = 0.5
stress_decay = 0.05
mobility = 0.3
water_drag = 0.1

BOTH = ("face", "tile")
VMEM = pl.BlockSpec(memory_space=pltpu.VMEM)


def struct(*shape):
    return jax.ShapeDtypeStruct(shape, jnp.float32)


def kept(*shape):
    return pltpu.VMEM(shape, jnp.float32)


def near(values):
    return pltpu.with_memory_space_constraint(values, pltpu.VMEM)


def lanes_of(shape):
    return lax.broadcasted_iota(jnp.int32, shape, len(shape) - 1)


def rows_of(shape):
    return lax.broadcasted_iota(jnp.int32, shape, len(shape) - 2)


def copies_of(sources, targets, sems):
    copies = [
        pltpu.make_async_copy(source, target, sems.at[at])
        for at, (source, target) in enumerate(zip(sources, targets))
    ]
    for copy in copies:
        copy.start()
    return copies


def stage_kernel(*refs):
    count = len(STAGED)
    targets = refs[count : 2 * count]
    side_out, down_out, up_out, sems = refs[2 * count :]
    copies = copies_of(refs[:count], targets, sems)
    motion_ref, strain_ref, resist_ref, frozen_ref = targets[3:7]
    for copy in copies[:3]:
        copy.wait()
    lane = lanes_of((ROWS, LANES))
    packed = jnp.zeros((ROWS, LANES), jnp.float32)
    for field, ref in enumerate(targets[:3]):
        for level in range(LEVELS):
            cells = ref[level]
            at = 4 * (field * LEVELS + level)
            moved = pltpu.roll(cells, 2 + at, 1)
            packed = jnp.where((lane >= at) & (lane < at + 4), moved, packed)
            here = pl.ds(2 * (field * LEVELS + level), 2)
            down_out[here, :] = cells[:2]
            up_out[here, :] = cells[ROWS - 2 :]
    for copy in copies[3:]:
        copy.wait()
    edge = jnp.zeros((1, LANES), jnp.float32)
    lane = lanes_of((1, LANES))
    for row, first, shift in ((ICE_ROWS - 1, 0, EVP), (0, 3, 0)):
        here = pl.ds(row, 1)
        strength = resist_ref[here] * (0.1 + 0.9 * frozen_ref[here].astype(jnp.float32))
        for at, cells in enumerate((motion_ref[here], strain_ref[here], strength), first):
            moved = pltpu.roll(cells, (EVP * at + shift) % LANES, 1)
            edge = jnp.where((lane >= EVP * at) & (lane < EVP * at + EVP), moved, edge)
    edge = jnp.broadcast_to(edge, (ROWS, LANES))
    side_out[pl.ds(0, ROWS), :] = packed
    side_out[pl.ds(ROWS, ROWS), :] = edge
    down_out[pl.ds(2 * FIELDS, 2), :] = packed[:2]
    up_out[pl.ds(2 * FIELDS, 2), :] = packed[ROWS - 2 :]
    down_out[pl.ds(2 * FIELDS + 2, 6), :] = edge[:6]
    up_out[pl.ds(2 * FIELDS + 2, 6), :] = edge[:6]


def factor_kernel(*refs):
    count = len(AFTER)
    speed_ref, _, *refs = refs
    targets = refs[count : 2 * count]
    speed_out, gain_out, inverse_out, slot_out, speeds, sems = refs[2 * count :]
    speed_copy = pltpu.make_async_copy(speed_ref, speeds, sems.at[count])
    speed_copy.start()
    copies = copies_of(refs[:count], targets, sems)
    link_ref, site_ref, area_ref = targets[:3]
    copies[0].wait()
    link = link_ref[0]
    inverse = 1.0 / (1.0 + link)
    gain = link * inverse
    inverse_out[0] = inverse
    gain_out[0] = gain
    for level in range(1, LEVELS - 1):
        earlier, link = link, link_ref[level]
        inverse = 1.0 / (1.0 + earlier + link - earlier * gain)
        gain = link * inverse
        inverse_out[level] = inverse
        gain_out[level] = gain
    inverse = 1.0 / (1.0 + link * (1.0 - gain))
    beta = gravity_step * inverse
    inverse_out[LEVELS - 1] = inverse
    gain_out[LEVELS - 1] = beta
    drag = link_ref[LEVELS - 1]
    table = spread_rows(drag / (1.0 + drag * beta))
    for copy in copies[1:3]:
        copy.wait()
    for start in range(0, SOURCES, ROWS):
        here = pl.ds(start, ROWS)
        (found,) = look_up((table,), site_ref[here, :])
        slot_out[here, :] = area_ref[here, :] * found
    speed_copy.wait()
    for level in range(LEVELS):
        speed_out[pl.ds(level, 1), :] = jnp.full((1, LANES), speeds[level])
    for copy in copies[3:]:
        copy.wait()


def side_kernel(side_ref, below_ref, above_ref, out_ref):
    out_ref[pl.ds(0, ROWS + 3), :] = side_ref[pl.ds(0, ROWS + 3), :]
    out_ref[pl.ds(8, 2), :] = above_ref[pl.ds(2 * FIELDS, 2), :]
    out_ref[pl.ds(11, 1), :] = below_ref[pl.ds(2 * FIELDS + 2, 1), :]
    out_ref[pl.ds(12, 2), :] = above_ref[pl.ds(2 * FIELDS + 2, 2), :]
    out_ref[pl.ds(14, 2), :] = below_ref[pl.ds(2 * FIELDS, 2), :]


def look_up(tables, index):
    high = index // LANES
    low = index % LANES
    found = [None] * len(tables)
    for row in range(len(tables[0])):
        here = high == row
        for at, rows in enumerate(tables):
            taken = jnp.take_along_axis(rows[row], low, axis=1, mode="promise_in_bounds")
            found[at] = taken if row == 0 else jnp.where(here, taken, found[at])
    return found


def spread_rows(table):
    return [
        jnp.broadcast_to(table[row : row + 1], (ROWS, LANES)) for row in range(table.shape[0])
    ]


def columns_kernel(
    speed_ref,
    p_ref,
    u_ref,
    v_ref,
    heat_ref,
    link_ref,
    below_ref,
    above_ref,
    site_ref,
    area_ref,
    inverse_ref,
    weight_ref,
    twin_ref,
    cross_ref,
    press_out,
    rest_out,
    halo_out,
    slots_out,
    wide,
):
    shape = (2 * ROWS, LANES)
    place = lax.axis_index("tile")
    even = place % 2 == 0
    left = jnp.where(even, cross_ref[...], twin_ref[...])
    right = jnp.where(even, twin_ref[...], cross_ref[...])
    border = jnp.where(lanes_of(shape) % 4 < 2, left, right)
    temps = []
    for level in range(LEVELS):
        speed = jnp.broadcast_to(speed_ref[pl.ds(level, 1), 0:1], (2 * ROWS, 2 * LANES))
        now = []
        for field, ref in enumerate((p_ref, u_ref, v_ref)):
            at = field * LEVELS + level
            wide[at, pl.ds(0, ROWS), :] = ref[level]
            wide[at, pl.ds(8, 8), :] = jnp.zeros((8, LANES), jnp.float32)
            wide[at, pl.ds(8, 2), :] = above_ref[pl.ds(2 * at, 2), :]
            wide[at, pl.ds(14, 2), :] = below_ref[pl.ds(2 * at, 2), :]
            outer = pltpu.roll(border, (126 - 4 * at) % LANES, 1)
            now.append(jnp.concatenate([wide[at], outer], axis=1))
        press, zonal, merid = now
        for _ in range(SUBS):
            zonal = zonal - speed * (pltpu.roll(press, 15, 0) - press)
            merid = merid - speed * (pltpu.roll(press, 255, 1) - press)
            press = press - speed * (
                zonal - pltpu.roll(zonal, 1, 0) + merid - pltpu.roll(merid, 1, 1)
            )
        final = press[:ROWS, :LANES]
        press_out[level] = final
        temps.append(heat_ref[level] + isentropic_lapse * final)
    last_zonal = zonal[:ROWS, :LANES]
    last_merid = merid[:ROWS, :LANES]

    rest = temps[0] * inverse_ref[0]
    rest_out[0] = rest
    for level in range(1, LEVELS):
        rest = (temps[level] + link_ref[level - 1] * rest) * inverse_ref[level]
        rest_out[level] = rest
    gamma = rest
    stress = link_ref[LEVELS - 1] * (last_zonal + 0.5 * last_merid)

    tables = [spread_rows(table) for table in (gamma, stress)]
    for start in range(0, SOURCES, ROWS):
        here = pl.ds(start, ROWS)
        found = look_up(tables, site_ref[here, :])
        slot_w = weight_ref[here, :]
        slots_out[pl.ds(3 * start, ROWS, stride=3), :] = slot_w
        slots_out[pl.ds(3 * start + 1, ROWS, stride=3), :] = slot_w * found[0]
        slots_out[pl.ds(3 * start + 2, ROWS, stride=3), :] = area_ref[here, :] * found[1]
    before = jnp.where(place == 0, left[11:12], left[10:11])
    after = jnp.where(place == TILES - 1, right[12:13], right[10:11])
    for at in range(3):
        halo_out[pl.ds(at, 1), :] = pltpu.roll(before, LANES - EVP - EVP * at, 1)
        halo_out[pl.ds(4 + at, 1), :] = pltpu.roll(after, LANES - EVP * (at + 3), 1)


def in_three(values):
    first = values.astype(jnp.bfloat16)
    left = values - first.astype(jnp.float32)
    second = left.astype(jnp.bfloat16)
    third = (left - second.astype(jnp.float32)).astype(jnp.bfloat16)
    return first.astype(jnp.float32), second.astype(jnp.float32), third.astype(jnp.float32)


def segment_sums(read, index_ref, values, high_row, low_count, group=8):
    high_count = len(high_row)
    shape = (high_count, LANES)
    rows = rows_of(shape)
    high_here = sum(jnp.where(rows == at, high, 0) for high, at in enumerate(high_row))
    low_here = rows_of((low_count, LANES))
    count = 3 * values * high_count

    def step(block, total):
        start = pl.multiple_of(block * group, group)
        index = index_ref[pl.ds(start, group), :]
        high = index // low_count
        low = index % low_count
        parts = [part for value in range(values) for part in in_three(read(value, start, group))]
        carried, spread = [], []
        for row in range(group):
            here = high_here == high[row : row + 1]
            carried.append(
                jnp.concatenate(
                    [
                        jnp.where(here, jnp.broadcast_to(part[row : row + 1], shape), 0.0).astype(
                            jnp.bfloat16
                        )
                        for part in parts
                    ],
                    axis=0,
                )
            )
            spread.append(
                jnp.where(low_here == low[row : row + 1], 1.0, 0.0).astype(jnp.bfloat16)
            )
        return total + lax.dot_general(
            jnp.concatenate(carried, axis=1),
            jnp.concatenate(spread, axis=1),
            (((1,), (1,)), ((), ())),
            preferred_element_type=jnp.float32,
        )

    total = lax.fori_loop(
        0, SOURCES // group, step, jnp.zeros((count, low_count), jnp.float32), unroll=True
    )
    sums = []
    for value in range(values):
        at = 3 * value * high_count
        sums.append(
            total[at + 2 * high_count : at + 3 * high_count]
            + total[at + high_count : at + 2 * high_count]
            + total[at : at + high_count]
        )
    return sums


def ice_kernel(
    slots_ref, target_ref, skin_ref, frozen_ref, resist_ref, _, skin_out, flux_out, ice_out
):
    def read(value, start, group):
        return slots_ref[pl.ds(3 * start + value, group, stride=3), :]

    heat, warmth, tau = segment_sums(read, target_ref, 3, range(ICE_ROWS), LANES)
    skin = skin_ref[...]
    frozen = frozen_ref[...]
    fresh = jnp.where(
        frozen == 1,
        (floe_warmth * skin + warmth) / (floe_warmth + floor_conductance + heat),
        skin,
    )
    skin_out[...] = fresh
    table = spread_rows(fresh)
    for start in range(0, SOURCES, ROWS):
        (at_floe,) = look_up((table,), target_ref[pl.ds(start, ROWS), :])
        flux_out[pl.ds(2 * start, ROWS, stride=2), :] = (
            slots_ref[pl.ds(3 * start, ROWS, stride=3), :] * at_floe
            - slots_ref[pl.ds(3 * start + 1, ROWS, stride=3), :]
        )
    ends = jnp.where(
        lanes_of((1, LANES)) < LANES // 2, tau[0:1], tau[ICE_ROWS - 1 : ICE_ROWS]
    )
    flux_out[pl.ds(1, SOURCES, stride=2), :] = jnp.broadcast_to(ends, (SOURCES, LANES))
    ice_out[0] = resist_ref[...] * (0.1 + 0.9 * frozen.astype(jnp.float32))
    ice_out[1] = tau


def paired(even_rows, odd_rows):
    lane = lanes_of((ROWS, LANES))
    out = []
    for at in range(2):
        index = (2 * lane + at) % LANES
        out.append(
            jnp.where(
                lane < LANES // 2,
                jnp.take_along_axis(even_rows, index, axis=1, mode="promise_in_bounds"),
                jnp.take_along_axis(odd_rows, index, axis=1, mode="promise_in_bounds"),
            )
        )
    return out


def neighbourhood(even_rows, odd_rows, before, after):
    shape = (ROWS, LANES)
    lane = lanes_of(shape)
    row = rows_of(shape)
    own = paired(even_rows, odd_rows)
    behind = paired(jnp.broadcast_to(before, shape), jnp.broadcast_to(before, shape))
    ahead = paired(jnp.broadcast_to(after, shape), jnp.broadcast_to(after, shape))
    cells = {}
    for at in range(2):
        cells[at] = own[at]
        up = jnp.where(row == ROWS - 1, ahead[at], pltpu.roll(own[at], ROWS - 1, 0))
        down = jnp.where(row == 0, behind[at], pltpu.roll(own[at], 1, 0))
        for far in range(1, EVP // 2 + 1):
            cells[at + 2 * far] = pltpu.roll(
                jnp.where(lane < far, up, own[at]), LANES - far, 1
            )
            cells[at - 2 * far] = pltpu.roll(
                jnp.where(lane >= LANES - far, down, own[at]), far, 1
            )
    return cells


def drift_kernel(motion_ref, strain_ref, ice_ref, halo_ref, out_ref, held):
    place = lax.axis_index("face") * TILES + lax.axis_index("tile")
    blank = jnp.zeros((1, LANES), jnp.float32)
    even, odd = pl.ds(0, ROWS, stride=2), pl.ds(1, ROWS, stride=2)
    first = jnp.where(place == 0, 0.0, 1.0)
    last = jnp.where(place == SOURCES - 1, 0.0, 1.0)
    slow = 1.0 / (1.0 + mobility * water_drag)
    fade = 1.0 / (1.0 + stress_decay)
    arrays = (
        (motion_ref[even], motion_ref[odd], halo_ref[0:1], halo_ref[4:5], 1.0),
        (strain_ref[even], strain_ref[odd], halo_ref[1:2], halo_ref[5:6], mobility * slow),
        (
            ice_ref[0, even],
            ice_ref[0, odd],
            halo_ref[2:3],
            halo_ref[6:7],
            mobility * slow * relaxation * fade,
        ),
        (ice_ref[1, even], ice_ref[1, odd], blank, blank, mobility * slow),
    )
    for at, (even_rows, odd_rows, before, after, scale) in enumerate(arrays):
        cells = neighbourhood(
            even_rows * scale,
            odd_rows * scale,
            before * (first * scale),
            after * (last * scale),
        )
        for cell, values in cells.items():
            held[at, cell + EVP] = values
    shape = (ROWS, LANES)
    where = LANES * rows_of(shape) + lanes_of(shape)

    def inside(cell):
        end = (ROWS * LANES * 2 - cell) // 2
        return jnp.where((where == end) & (place == SOURCES - 1), 0.0, 1.0)

    width = 2 * EVP + 2
    velocity = [held[0, at] for at in range(width)]
    stress = [held[1, at] for at in range(width)]
    for turn in range(EVP):
        for at in range(turn, width - turn - 1):
            stress[at] = stress[at] * fade + held[2, at] * (velocity[at + 1] - velocity[at])
        for at in range(turn + 1, width - turn - 1):
            force = stress[at] - stress[at - 1] + held[3, at]
            if at >= EVP + 2 and at % 2 == 0:
                force = force * inside(at - EVP)
            velocity[at] = velocity[at] * slow + force
    lane = lanes_of(shape)
    for rows, half in ((even, 0), (odd, LANES // 2)):
        index = lane // 2 + half
        out_ref[rows] = jnp.where(
            lane % 2 == 0,
            jnp.take_along_axis(velocity[EVP], index, axis=1, mode="promise_in_bounds"),
            jnp.take_along_axis(velocity[EVP + 1], index, axis=1, mode="promise_in_bounds"),
        )


def edge_kernel(resist_ref, frozen_ref, halo_ref, out_ref):
    slow = 1.0 / (1.0 + mobility * water_drag)
    fade = 1.0 / (1.0 + stress_decay)
    half = LANES // 2
    here = lanes_of((1, LANES)) < half
    ends = [
        resist_ref[pl.ds(row, 1)] * (0.1 + 0.9 * frozen_ref[pl.ds(row, 1)].astype(jnp.float32))
        for row in (0, ICE_ROWS - 1)
    ]
    strength = (
        jnp.where(here, ends[0], halo_ref[2:3]),
        jnp.where(here, halo_ref[6:7], ends[1]),
    )
    pull = jnp.concatenate(
        [jnp.broadcast_to(pltpu.roll(row, half, 1), (24, LANES)) for row in strength], axis=0
    ) * (mobility * slow * relaxation * fade)
    shape = (48, LANES)
    row = rows_of(shape)
    lane = lanes_of(shape)
    source = jnp.where(row < 24, half - EVP + row, half - 24 + row)
    push = jnp.where((lane == source) & (row % 24 < EVP), mobility * slow, 0.0)
    velocity = jnp.zeros(shape, jnp.float32)
    stress = jnp.zeros(shape, jnp.float32)
    for _ in range(EVP):
        stress = stress * fade + pull * (pltpu.roll(velocity, LANES - 1, 1) - velocity)
        velocity = velocity * slow + (stress - pltpu.roll(stress, 1, 1) + push)
    velocity = pltpu.roll(velocity, half, 1)
    velocity = jnp.where(
        ((row < 24) & (lane < EVP)) | ((row >= 24) & (lane >= LANES - EVP)), velocity, 0.0
    )
    out_ref[...] = jnp.zeros((LANES, LANES), jnp.float32)
    out_ref[pl.ds(0, EVP), :] = velocity[24 : 24 + EVP]
    out_ref[pl.ds(LANES - EVP, EVP), :] = velocity[:EVP]


def last_kernel(
    flux_ref, site_ref, gain_ref, rest_ref, drift_ref, edge_ref, heat_out, motion_out
):
    def read(value, start, group):
        return flux_ref[pl.ds(2 * start, group, stride=2), :]

    place = lax.axis_index("face") * TILES + lax.axis_index("tile")
    lane = lanes_of((1, LANES))
    before = flux_ref[pl.ds(2 * jnp.maximum(place - 1, 0) + 1, 1), :]
    after = flux_ref[pl.ds(2 * jnp.minimum(place + 1, SOURCES - 1) + 1, 1), :]
    outside = jnp.where(
        lane < LANES // 2,
        after * jnp.where(place == SOURCES - 1, 0.0, 1.0),
        before * jnp.where(place == 0, 0.0, 1.0),
    )
    added = lax.dot_general(
        jnp.broadcast_to(outside, (ROWS, LANES)),
        edge_ref[...],
        (((1,), (0,)), ((), ())),
        precision=lax.Precision.HIGHEST,
        preferred_element_type=jnp.float32,
    )[0:1]
    motion_out[...] = drift_ref[...]
    motion_out[0:1] = drift_ref[0:1] + jnp.where(lane < EVP, added, 0.0)
    end = pl.ds(ICE_ROWS - 1, 1)
    motion_out[end] = drift_ref[end] + jnp.where(lane >= LANES - EVP, added, 0.0)

    order = [ROWS * (half % 2) + half // 2 for half in range(2 * ROWS)]
    (halves,) = segment_sums(read, site_ref, 1, order, LANES // 2)
    surface_flux = jnp.concatenate([halves[:ROWS], halves[ROWS:]], axis=1)
    below = gain_ref[LEVELS - 1] * surface_flux + rest_ref[LEVELS - 1]
    heat_out[LEVELS - 1] = below
    for level in range(LEVELS - 2, -1, -1):
        below = gain_ref[level] * below + rest_ref[level]
        heat_out[level] = below


def ring(axis, step):
    count = lax.axis_size(axis)
    return [(i, (i + step) % count) for i in range(count)]


def swaps(axis, first):
    count = lax.axis_size(axis)
    pairs = [(i, (i + 1) % count) for i in range(first, count, 2)]
    return sorted(pairs + [(b, a) for a, b in pairs])


def exchanged(rows, count):
    blocks = rows.reshape(SOURCES, count, 1, LANES)
    blocks = lax.all_to_all(blocks, BOTH, split_axis=0, concat_axis=0, tiled=True)
    return near(blocks.reshape(SOURCES * count, LANES))


def local(
    squeeze_anomaly,
    eastward_airflow,
    northward_airflow,
    thermal_anomaly,
    diffusivity_link,
    sound_stability_ratio,
    overlay_source_site,
    overlay_target_floe,
    overlay_fraction,
    floe_skin_kelvin,
    frozen_indicator,
    floe_motion,
    floe_strain_tensor,
    floe_compress_resist,
):
    ice = (ICE_ROWS, LANES)
    slot = (SOURCES, LANES)
    arguments = dict(
        press=squeeze_anomaly,
        zonal=eastward_airflow,
        merid=northward_airflow,
        motion=floe_motion.reshape(ice),
        strain=floe_strain_tensor.reshape(ice),
        resist=floe_compress_resist.reshape(ice),
        frozen=frozen_indicator.reshape(ice),
        skin=floe_skin_kelvin.reshape(ice),
        heat=thermal_anomaly,
        link=diffusivity_link,
        site=overlay_source_site.reshape(slot),
        area=overlay_fraction.reshape(slot),
        target=overlay_target_floe.reshape(slot),
    )
    hbm = pl.BlockSpec(memory_space=pl.ANY)
    sources = [arguments[name] for name in STAGED]
    *staged, sides, down, up = pl.pallas_call(
        stage_kernel,
        out_shape=[pltpu.VMEM(source.shape, source.dtype) for source in sources]
        + [kept(2 * ROWS, LANES), kept(SLAB, LANES), kept(SLAB, LANES)],
        in_specs=[hbm] * len(sources),
        out_specs=[VMEM] * (len(sources) + 3),
        scratch_shapes=[pltpu.SemaphoreType.DMA((len(sources),))],
    )(*sources)
    at = {name: near(values) for name, values in zip(STAGED, staged)}
    sides = near(sides)
    sources = [arguments[name] for name in AFTER]
    *staged, speeds, gain, inverse, weight = pl.pallas_call(
        factor_kernel,
        out_shape=[pltpu.VMEM(source.shape, source.dtype) for source in sources]
        + [kept(LEVELS, LANES)]
        + [kept(LEVELS, ROWS, LANES)] * 2
        + [kept(*slot)],
        in_specs=[hbm, VMEM] + [hbm] * len(sources),
        out_specs=[VMEM] * (len(sources) + 4),
        scratch_shapes=[
            pltpu.SMEM((LEVELS,), jnp.float32),
            pltpu.SemaphoreType.DMA((len(sources) + 1,)),
        ],
    )(sound_stability_ratio, sides, *sources)
    at.update({name: near(values) for name, values in zip(AFTER, staged)})
    below = near(lax.ppermute(up, "face", ring("face", 1)))
    above = near(lax.ppermute(down, "face", ring("face", -1)))
    sides = pl.pallas_call(
        side_kernel, out_shape=kept(2 * ROWS, LANES), in_specs=[VMEM] * 3, out_specs=VMEM
    )(sides, below, above)
    twin = near(lax.ppermute(sides, "tile", swaps("tile", 0)))
    cross = near(lax.ppermute(sides, "tile", swaps("tile", 1)))
    pressure_new, rest, halo, slots = pl.pallas_call(
        columns_kernel,
        out_shape=[
            struct(LEVELS, ROWS, LANES),
            kept(LEVELS, ROWS, LANES),
            kept(8, LANES),
            struct(3 * SOURCES, LANES),
        ],
        in_specs=[VMEM] * 14,
        out_specs=[VMEM] * 4,
        scratch_shapes=[pltpu.VMEM((FIELDS, 16, LANES), jnp.float32)],
    )(
        near(speeds),
        *(at[name] for name in ("press", "zonal", "merid", "heat", "link")),
        below,
        above,
        at["site"],
        at["area"],
        near(inverse),
        near(weight),
        twin,
        cross,
    )
    arrived = exchanged(slots, 3)
    edge = near(
        pl.pallas_call(
            edge_kernel, out_shape=kept(LANES, LANES), in_specs=[VMEM] * 3, out_specs=VMEM
        )(at["resist"], at["frozen"], near(halo))
    )
    fresh, flux, ice_terms = pl.pallas_call(
        ice_kernel,
        out_shape=[struct(*ice), struct(2 * SOURCES, LANES), kept(2, *ice)],
        in_specs=[VMEM] * 6,
        out_specs=[VMEM] * 3,
    )(arrived, *(at[name] for name in ("target", "skin", "frozen", "resist")), edge)
    returned = exchanged(flux, 2)
    drifted = pl.pallas_call(
        drift_kernel,
        out_shape=kept(*ice),
        in_specs=[VMEM] * 4,
        out_specs=VMEM,
        scratch_shapes=[pltpu.VMEM((4, 2 * EVP + 2, ROWS, LANES), jnp.float32)],
    )(at["motion"], at["strain"], near(ice_terms), near(halo))
    temp_new, velocity = pl.pallas_call(
        last_kernel,
        out_shape=[struct(LEVELS, ROWS, LANES), struct(*ice)],
        in_specs=[VMEM] * 6,
        out_specs=[VMEM] * 2,
    )(returned, at["site"], near(gain), near(rest), near(drifted), edge)
    return (temp_new, pressure_new, fresh.reshape(-1), velocity.reshape(-1))


def solution(mesh):
    block = P(None, "face", "tile")
    slot = P(BOTH, None, None)
    cells = P(BOTH)
    return jax.shard_map(
        local,
        mesh=mesh,
        in_specs=(block,) * 5 + (P(),) + (slot,) * 3 + (cells,) * 5,
        out_specs=(block, block, cells, cells),
        check_vma=False,
    )
```

```python
import functools

import jax
import jax.numpy as jnp
from jax import lax
from jax.experimental import pallas as pl
from jax.experimental.pallas import tpu as pltpu
from jax.sharding import PartitionSpec as P

SUBS = 2
EVP = 20
LEVELS = 8
ROWS = 8
LANES = 128
SOURCES = 128
ICE_ROWS = 16
FIELDS = 3 * LEVELS
UP_ROWS = (2, 2, 1)
DOWN_ROWS = (2, 1, 1)
UP = LEVELS * sum(UP_ROWS)
DOWN = LEVELS * sum(DOWN_ROWS)
TILES = 32
STAGED = ("press", "zonal", "merid", "motion", "strain", "resist", "frozen")
AFTER = ("link", "site", "area", "heat", "target", "skin")

isentropic_lapse = 0.3
gravity_step = 0.5
floe_warmth = 2.0
floor_conductance = 1.0
relaxation = 0.5
stress_decay = 0.05
mobility = 0.3
water_drag = 0.1

BOTH = ("face", "tile")
VMEM = pl.BlockSpec(memory_space=pltpu.VMEM)


def struct(*shape):
    return jax.ShapeDtypeStruct(shape, jnp.float32)


def kept(*shape):
    return pltpu.VMEM(shape, jnp.float32)


def near(values):
    return pltpu.with_memory_space_constraint(values, pltpu.VMEM)


def lanes_of(shape):
    return lax.broadcasted_iota(jnp.int32, shape, len(shape) - 1)


def rows_of(shape):
    return lax.broadcasted_iota(jnp.int32, shape, len(shape) - 2)


def copies_of(sources, targets, sems):
    copies = [
        pltpu.make_async_copy(source, target, sems.at[at])
        for at, (source, target) in enumerate(zip(sources, targets))
    ]
    for copy in copies:
        copy.start()
    return copies


def slab_rows(counts, field, level):
    return pl.ds(LEVELS * sum(counts[:field]) + counts[field] * level, counts[field])


def stage_kernel(*refs):
    count = len(STAGED)
    targets = refs[count : 2 * count]
    side_out, down_out, up_out, sems = refs[2 * count :]
    copies = copies_of(refs[:count], targets, sems)
    motion_ref, strain_ref, resist_ref, frozen_ref = targets[3:7]
    for copy in copies[:3]:
        copy.wait()
    lane = lanes_of((ROWS, LANES))
    packed = jnp.zeros((ROWS, LANES), jnp.float32)
    for field, ref in enumerate(targets[:3]):
        for level in range(LEVELS):
            cells = ref[level]
            at = 4 * (field * LEVELS + level)
            moved = pltpu.roll(cells, 2 + at, 1)
            packed = jnp.where((lane >= at) & (lane < at + 4), moved, packed)
            down_out[slab_rows(DOWN_ROWS, field, level), :] = cells[: DOWN_ROWS[field]]
            up_out[slab_rows(UP_ROWS, field, level), :] = cells[ROWS - UP_ROWS[field] :]
    for copy in copies[3:]:
        copy.wait()
    edge = jnp.zeros((1, LANES), jnp.float32)
    lane = lanes_of((1, LANES))
    for row, first, shift in ((ICE_ROWS - 1, 0, EVP), (0, 3, 0)):
        here = pl.ds(row, 1)
        strength = resist_ref[here] * (0.1 + 0.9 * frozen_ref[here].astype(jnp.float32))
        for at, cells in enumerate((motion_ref[here], strain_ref[here], strength), first):
            moved = pltpu.roll(cells, (EVP * at + shift) % LANES, 1)
            edge = jnp.where((lane >= EVP * at) & (lane < EVP * at + EVP), moved, edge)
    edge = jnp.broadcast_to(edge, (ROWS, LANES))
    side_out[pl.ds(0, ROWS), :] = packed
    side_out[pl.ds(ROWS, ROWS), :] = edge
    down_out[pl.ds(DOWN, 2), :] = packed[:2]
    up_out[pl.ds(UP, 2), :] = packed[ROWS - 2 :]
    down_out[pl.ds(DOWN + 2, 6), :] = edge[:6]
    up_out[pl.ds(UP + 2, 6), :] = edge[:6]


def factor_kernel(*refs):
    count = len(AFTER)
    speed_ref, _, *refs = refs
    targets = refs[count : 2 * count]
    speed_out, gain_out, inverse_out, answer_out, slot_out, speeds, sems = refs[2 * count :]
    speed_copy = pltpu.make_async_copy(speed_ref, speeds, sems.at[count])
    speed_copy.start()
    copies = copies_of(refs[:count], targets, sems)
    link_ref, site_ref, area_ref = targets[:3]
    copies[0].wait()
    link = link_ref[0]
    inverse = 1.0 / (1.0 + link)
    gain = link * inverse
    inverse_out[0] = inverse
    gain_out[0] = gain
    for level in range(1, LEVELS - 1):
        earlier, link = link, link_ref[level]
        inverse = 1.0 / (1.0 + earlier + link - earlier * gain)
        gain = link * inverse
        inverse_out[level] = inverse
        gain_out[level] = gain
    inverse = 1.0 / (1.0 + link * (1.0 - gain))
    beta = gravity_step * inverse
    inverse_out[LEVELS - 1] = inverse
    answer_out[LEVELS - 1] = answer = beta
    for level in range(LEVELS - 2, -1, -1):
        answer = gain_out[level] * answer
        answer_out[level] = answer
    drag = link_ref[LEVELS - 1]
    table = spread_rows(drag / (1.0 + drag * beta))
    for copy in copies[1:3]:
        copy.wait()
    for start in range(0, SOURCES, ROWS):
        here = pl.ds(start, ROWS)
        (found,) = look_up((table,), site_ref[here, :])
        slot_out[here, :] = area_ref[here, :] * found
    speed_copy.wait()
    for level in range(LEVELS):
        speed_out[pl.ds(level, 1), :] = jnp.full((1, LANES), speeds[level])
    for copy in copies[3:]:
        copy.wait()


def side_kernel(side_ref, above_ref, below_ref, out_ref):
    out_ref[pl.ds(0, ROWS + 3), :] = side_ref[pl.ds(0, ROWS + 3), :]
    out_ref[pl.ds(8, 2), :] = above_ref[pl.ds(DOWN, 2), :]
    out_ref[pl.ds(11, 1), :] = below_ref[pl.ds(UP + 2, 1), :]
    out_ref[pl.ds(12, 2), :] = above_ref[pl.ds(DOWN + 2, 2), :]
    out_ref[pl.ds(14, 2), :] = below_ref[pl.ds(UP, 2), :]


def widen_kernel(p_ref, u_ref, v_ref, above_ref, below_ref, wide_out):
    for field, ref in enumerate((p_ref, u_ref, v_ref)):
        above, below = DOWN_ROWS[field], UP_ROWS[field]
        for level in range(LEVELS):
            at = field * LEVELS + level
            wide_out[at, pl.ds(0, ROWS), :] = ref[level]
            wide_out[at, pl.ds(8, 8), :] = jnp.zeros((8, LANES), jnp.float32)
            wide_out[at, pl.ds(8, above), :] = above_ref[slab_rows(DOWN_ROWS, field, level), :]
            wide_out[at, pl.ds(16 - below, below), :] = below_ref[
                slab_rows(UP_ROWS, field, level), :
            ]


def look_up(tables, index):
    high = index // LANES
    low = index % LANES
    found = [None] * len(tables)
    for row in range(len(tables[0])):
        here = high == row
        for at, rows in enumerate(tables):
            taken = jnp.take_along_axis(rows[row], low, axis=1, mode="promise_in_bounds")
            found[at] = taken if row == 0 else jnp.where(here, taken, found[at])
    return found


def spread_rows(table):
    return [
        jnp.broadcast_to(table[row : row + 1], (ROWS, LANES)) for row in range(table.shape[0])
    ]


def columns_kernel(
    speed_ref,
    wide_ref,
    heat_ref,
    link_ref,
    site_ref,
    area_ref,
    inverse_ref,
    weight_ref,
    twin_ref,
    cross_ref,
    press_out,
    rest_out,
    halo_out,
    slots_out,
):
    shape = (2 * ROWS, LANES)
    place = lax.axis_index("tile")
    even = place % 2 == 0
    left = jnp.where(even, cross_ref[...], twin_ref[...])
    right = jnp.where(even, twin_ref[...], cross_ref[...])
    border = jnp.where(lanes_of(shape) % 4 < 2, left, right)
    temps = []
    for level in range(LEVELS):
        speed = jnp.broadcast_to(speed_ref[pl.ds(level, 1), 0:1], (2 * ROWS, 2 * LANES))
        now = []
        for field in range(3):
            at = field * LEVELS + level
            outer = pltpu.roll(border, (126 - 4 * at) % LANES, 1)
            now.append(jnp.concatenate([wide_ref[at], outer], axis=1))
        press, zonal, merid = now
        for _ in range(SUBS):
            zonal = zonal - speed * (pltpu.roll(press, 15, 0) - press)
            merid = merid - speed * (pltpu.roll(press, 255, 1) - press)
            press = press - speed * (
                zonal - pltpu.roll(zonal, 1, 0) + merid - pltpu.roll(merid, 1, 1)
            )
        final = press[:ROWS, :LANES]
        press_out[level] = final
        temps.append(heat_ref[level] + isentropic_lapse * final)
    last_zonal = zonal[:ROWS, :LANES]
    last_merid = merid[:ROWS, :LANES]

    rest = temps[0] * inverse_ref[0]
    rest_out[0] = rest
    for level in range(1, LEVELS):
        rest = (temps[level] + link_ref[level - 1] * rest) * inverse_ref[level]
        rest_out[level] = rest
    gamma = rest
    stress = link_ref[LEVELS - 1] * (last_zonal + 0.5 * last_merid)

    tables = [spread_rows(table) for table in (gamma, stress)]
    for start in range(0, SOURCES, ROWS):
        here = pl.ds(start, ROWS)
        found = look_up(tables, site_ref[here, :])
        slot_w = weight_ref[here, :]
        slots_out[pl.ds(3 * start, ROWS, stride=3), :] = slot_w
        slots_out[pl.ds(3 * start + 1, ROWS, stride=3), :] = slot_w * found[0]
        slots_out[pl.ds(3 * start + 2, ROWS, stride=3), :] = area_ref[here, :] * found[1]
    before = jnp.where(place == 0, left[11:12], left[10:11])
    after = jnp.where(place == TILES - 1, right[12:13], right[10:11])
    for at in range(3):
        halo_out[pl.ds(at, 1), :] = pltpu.roll(before, LANES - EVP - EVP * at, 1)
        halo_out[pl.ds(4 + at, 1), :] = pltpu.roll(after, LANES - EVP * (at + 3), 1)


def in_three(values):
    first = values.astype(jnp.bfloat16)
    left = values - first.astype(jnp.float32)
    second = left.astype(jnp.bfloat16)
    third = (left - second.astype(jnp.float32)).astype(jnp.bfloat16)
    return first.astype(jnp.float32), second.astype(jnp.float32), third.astype(jnp.float32)


def segment_sums(read, index_ref, values, high_row, low_count, group=32):
    high_count = len(high_row)
    shape = (high_count, LANES)
    rows = rows_of(shape)
    high_here = sum(jnp.where(rows == at, high, 0) for high, at in enumerate(high_row))
    low_here = rows_of((low_count, LANES))
    count = 3 * values * high_count

    def step(block, total):
        start = pl.multiple_of(block * group, group)
        index = index_ref[pl.ds(start, group), :]
        high = index // low_count
        low = index % low_count
        parts = [part for value in range(values) for part in in_three(read(value, start, group))]
        carried, spread = [], []
        for row in range(group):
            here = high_here == high[row : row + 1]
            carried.append(
                jnp.concatenate(
                    [
                        jnp.where(here, jnp.broadcast_to(part[row : row + 1], shape), 0.0).astype(
                            jnp.bfloat16
                        )
                        for part in parts
                    ],
                    axis=0,
                )
            )
            spread.append(
                jnp.where(low_here == low[row : row + 1], 1.0, 0.0).astype(jnp.bfloat16)
            )
        return total + lax.dot_general(
            jnp.concatenate(carried, axis=1),
            jnp.concatenate(spread, axis=1),
            (((1,), (1,)), ((), ())),
            preferred_element_type=jnp.float32,
        )

    total = lax.fori_loop(
        0, SOURCES // group, step, jnp.zeros((count, low_count), jnp.float32), unroll=True
    )
    sums = []
    for value in range(values):
        at = 3 * value * high_count
        sums.append(
            total[at + 2 * high_count : at + 3 * high_count]
            + total[at + high_count : at + 2 * high_count]
            + total[at : at + high_count]
        )
    return sums


def ice_kernel(
    slots_ref, target_ref, skin_ref, frozen_ref, resist_ref, _, skin_out, flux_out, ice_out
):
    def read(value, start, group):
        return slots_ref[pl.ds(3 * start + value, group, stride=3), :]

    heat, warmth, tau = segment_sums(read, target_ref, 3, range(ICE_ROWS), LANES)
    skin = skin_ref[...]
    frozen = frozen_ref[...]
    fresh = jnp.where(
        frozen == 1,
        (floe_warmth * skin + warmth) / (floe_warmth + floor_conductance + heat),
        skin,
    )
    skin_out[...] = fresh
    table = spread_rows(fresh)
    for start in range(0, SOURCES, ROWS):
        (at_floe,) = look_up((table,), target_ref[pl.ds(start, ROWS), :])
        flux_out[pl.ds(2 * start, ROWS, stride=2), :] = (
            slots_ref[pl.ds(3 * start, ROWS, stride=3), :] * at_floe
            - slots_ref[pl.ds(3 * start + 1, ROWS, stride=3), :]
        )
    ends = jnp.where(
        lanes_of((1, LANES)) < LANES // 2, tau[0:1], tau[ICE_ROWS - 1 : ICE_ROWS]
    )
    flux_out[pl.ds(1, SOURCES, stride=2), :] = jnp.broadcast_to(ends, (SOURCES, LANES))
    ice_out[0] = resist_ref[...] * (0.1 + 0.9 * frozen.astype(jnp.float32))
    ice_out[1] = tau


def paired(even_rows, odd_rows):
    lane = lanes_of((ROWS, LANES))
    out = []
    for at in range(2):
        index = (2 * lane + at) % LANES
        out.append(
            jnp.where(
                lane < LANES // 2,
                jnp.take_along_axis(even_rows, index, axis=1, mode="promise_in_bounds"),
                jnp.take_along_axis(odd_rows, index, axis=1, mode="promise_in_bounds"),
            )
        )
    return out


def neighbourhood(even_rows, odd_rows, before, after):
    shape = (ROWS, LANES)
    lane = lanes_of(shape)
    row = rows_of(shape)
    own = paired(even_rows, odd_rows)
    behind = paired(jnp.broadcast_to(before, shape), jnp.broadcast_to(before, shape))
    ahead = paired(jnp.broadcast_to(after, shape), jnp.broadcast_to(after, shape))
    cells = {}
    for at in range(2):
        cells[at] = own[at]
        up = jnp.where(row == ROWS - 1, ahead[at], pltpu.roll(own[at], ROWS - 1, 0))
        down = jnp.where(row == 0, behind[at], pltpu.roll(own[at], 1, 0))
        for far in range(1, EVP // 2 + 1):
            cells[at + 2 * far] = pltpu.roll(
                jnp.where(lane < far, up, own[at]), LANES - far, 1
            )
            cells[at - 2 * far] = pltpu.roll(
                jnp.where(lane >= LANES - far, down, own[at]), far, 1
            )
    return cells


def drift_kernel(motion_ref, strain_ref, ice_ref, halo_ref, out_ref, held):
    place = lax.axis_index("face") * TILES + lax.axis_index("tile")
    blank = jnp.zeros((1, LANES), jnp.float32)
    even, odd = pl.ds(0, ROWS, stride=2), pl.ds(1, ROWS, stride=2)
    first = jnp.where(place == 0, 0.0, 1.0)
    last = jnp.where(place == SOURCES - 1, 0.0, 1.0)
    slow = 1.0 / (1.0 + mobility * water_drag)
    fade = 1.0 / (1.0 + stress_decay)
    arrays = (
        (motion_ref[even], motion_ref[odd], halo_ref[0:1], halo_ref[4:5], 1.0),
        (strain_ref[even], strain_ref[odd], halo_ref[1:2], halo_ref[5:6], mobility * slow),
        (
            ice_ref[0, even],
            ice_ref[0, odd],
            halo_ref[2:3],
            halo_ref[6:7],
            mobility * slow * relaxation * fade,
        ),
        (ice_ref[1, even], ice_ref[1, odd], blank, blank, mobility * slow),
    )
    for at, (even_rows, odd_rows, before, after, scale) in enumerate(arrays):
        cells = neighbourhood(
            even_rows * scale,
            odd_rows * scale,
            before * (first * scale),
            after * (last * scale),
        )
        for cell, values in cells.items():
            held[at, cell + EVP] = values
    shape = (ROWS, LANES)
    where = LANES * rows_of(shape) + lanes_of(shape)

    def inside(cell):
        end = (ROWS * LANES * 2 - cell) // 2
        return jnp.where((where == end) & (place == SOURCES - 1), 0.0, 1.0)

    width = 2 * EVP + 2
    velocity = [held[0, at] for at in range(width)]
    stress = [held[1, at] for at in range(width)]
    for turn in range(EVP):
        for at in range(turn, width - turn - 1):
            stress[at] = stress[at] * fade + held[2, at] * (velocity[at + 1] - velocity[at])
        for at in range(turn + 1, width - turn - 1):
            force = stress[at] - stress[at - 1] + held[3, at]
            if at >= EVP + 2 and at % 2 == 0:
                force = force * inside(at - EVP)
            velocity[at] = velocity[at] * slow + force
    lane = lanes_of(shape)
    for rows, half in ((even, 0), (odd, LANES // 2)):
        index = lane // 2 + half
        out_ref[rows] = jnp.where(
            lane % 2 == 0,
            jnp.take_along_axis(velocity[EVP], index, axis=1, mode="promise_in_bounds"),
            jnp.take_along_axis(velocity[EVP + 1], index, axis=1, mode="promise_in_bounds"),
        )


def edge_kernel(resist_ref, frozen_ref, halo_ref, gain_ref, rest_ref, out_ref, calm_out):
    calm_out[LEVELS - 1] = calm = rest_ref[LEVELS - 1]
    for level in range(LEVELS - 2, -1, -1):
        calm = gain_ref[level] * calm + rest_ref[level]
        calm_out[level] = calm
    slow = 1.0 / (1.0 + mobility * water_drag)
    fade = 1.0 / (1.0 + stress_decay)
    half = LANES // 2
    here = lanes_of((1, LANES)) < half
    ends = [
        resist_ref[pl.ds(row, 1)] * (0.1 + 0.9 * frozen_ref[pl.ds(row, 1)].astype(jnp.float32))
        for row in (0, ICE_ROWS - 1)
    ]
    strength = (
        jnp.where(here, ends[0], halo_ref[2:3]),
        jnp.where(here, halo_ref[6:7], ends[1]),
    )
    pull = jnp.concatenate(
        [jnp.broadcast_to(pltpu.roll(row, half, 1), (24, LANES)) for row in strength], axis=0
    ) * (mobility * slow * relaxation * fade)
    shape = (48, LANES)
    row = rows_of(shape)
    lane = lanes_of(shape)
    source = jnp.where(row < 24, half - EVP + row, half - 24 + row)
    push = jnp.where((lane == source) & (row % 24 < EVP), mobility * slow, 0.0)
    velocity = jnp.zeros(shape, jnp.float32)
    stress = jnp.zeros(shape, jnp.float32)
    for _ in range(EVP):
        stress = stress * fade + pull * (pltpu.roll(velocity, LANES - 1, 1) - velocity)
        velocity = velocity * slow + (stress - pltpu.roll(stress, 1, 1) + push)
    velocity = pltpu.roll(velocity, half, 1)
    velocity = jnp.where(
        ((row < 24) & (lane < EVP)) | ((row >= 24) & (lane >= LANES - EVP)), velocity, 0.0
    )
    out_ref[...] = jnp.zeros((LANES, LANES), jnp.float32)
    out_ref[pl.ds(0, EVP), :] = velocity[24 : 24 + EVP]
    out_ref[pl.ds(LANES - EVP, EVP), :] = velocity[:EVP]


def last_kernel(
    flux_ref, site_ref, answer_ref, calm_ref, drift_ref, edge_ref, heat_out, motion_out
):
    def read(value, start, group):
        return flux_ref[pl.ds(2 * start, group, stride=2), :]

    place = lax.axis_index("face") * TILES + lax.axis_index("tile")
    lane = lanes_of((1, LANES))
    before = flux_ref[pl.ds(2 * jnp.maximum(place - 1, 0) + 1, 1), :]
    after = flux_ref[pl.ds(2 * jnp.minimum(place + 1, SOURCES - 1) + 1, 1), :]
    outside = jnp.where(
        lane < LANES // 2,
        after * jnp.where(place == SOURCES - 1, 0.0, 1.0),
        before * jnp.where(place == 0, 0.0, 1.0),
    )
    added = lax.dot_general(
        jnp.broadcast_to(outside, (ROWS, LANES)),
        edge_ref[...],
        (((1,), (0,)), ((), ())),
        precision=lax.Precision.HIGHEST,
        preferred_element_type=jnp.float32,
    )[0:1]
    motion_out[...] = drift_ref[...]
    motion_out[0:1] = drift_ref[0:1] + jnp.where(lane < EVP, added, 0.0)
    end = pl.ds(ICE_ROWS - 1, 1)
    motion_out[end] = drift_ref[end] + jnp.where(lane >= LANES - EVP, added, 0.0)

    order = [ROWS * (half % 2) + half // 2 for half in range(2 * ROWS)]
    (halves,) = segment_sums(read, site_ref, 1, order, LANES // 2)
    surface_flux = jnp.concatenate([halves[:ROWS], halves[ROWS:]], axis=1)
    for level in range(LEVELS):
        heat_out[level] = answer_ref[level] * surface_flux + calm_ref[level]


def ring(axis, step):
    count = lax.axis_size(axis)
    return [(i, (i + step) % count) for i in range(count)]


def swaps(axis, first):
    count = lax.axis_size(axis)
    pairs = [(i, (i + 1) % count) for i in range(first, count, 2)]
    return sorted(pairs + [(b, a) for a, b in pairs])


def exchanged(rows, count):
    blocks = rows.reshape(SOURCES, count, 1, LANES)
    blocks = lax.all_to_all(blocks, BOTH, split_axis=0, concat_axis=0, tiled=True)
    return near(blocks.reshape(SOURCES * count, LANES))


def local(
    squeeze_anomaly,
    eastward_airflow,
    northward_airflow,
    thermal_anomaly,
    diffusivity_link,
    sound_stability_ratio,
    overlay_source_site,
    overlay_target_floe,
    overlay_fraction,
    floe_skin_kelvin,
    frozen_indicator,
    floe_motion,
    floe_strain_tensor,
    floe_compress_resist,
):
    ice = (ICE_ROWS, LANES)
    slot = (SOURCES, LANES)
    arguments = dict(
        press=squeeze_anomaly,
        zonal=eastward_airflow,
        merid=northward_airflow,
        motion=floe_motion.reshape(ice),
        strain=floe_strain_tensor.reshape(ice),
        resist=floe_compress_resist.reshape(ice),
        frozen=frozen_indicator.reshape(ice),
        skin=floe_skin_kelvin.reshape(ice),
        heat=thermal_anomaly,
        link=diffusivity_link,
        site=overlay_source_site.reshape(slot),
        area=overlay_fraction.reshape(slot),
        target=overlay_target_floe.reshape(slot),
    )
    hbm = pl.BlockSpec(memory_space=pl.ANY)
    sources = [arguments[name] for name in STAGED]
    *staged, sides, down, up = pl.pallas_call(
        stage_kernel,
        out_shape=[pltpu.VMEM(source.shape, source.dtype) for source in sources]
        + [kept(2 * ROWS, LANES), kept(DOWN + 8, LANES), kept(UP + 8, LANES)],
        in_specs=[hbm] * len(sources),
        out_specs=[VMEM] * (len(sources) + 3),
        scratch_shapes=[pltpu.SemaphoreType.DMA((len(sources),))],
    )(*sources)
    at = {name: near(values) for name, values in zip(STAGED, staged)}
    sides = near(sides)
    sources = [arguments[name] for name in AFTER]
    *staged, speeds, gain, inverse, answer, weight = pl.pallas_call(
        factor_kernel,
        out_shape=[pltpu.VMEM(source.shape, source.dtype) for source in sources]
        + [kept(LEVELS, LANES)]
        + [kept(LEVELS, ROWS, LANES)] * 3
        + [kept(*slot)],
        in_specs=[hbm, VMEM] + [hbm] * len(sources),
        out_specs=[VMEM] * (len(sources) + 5),
        scratch_shapes=[
            pltpu.SMEM((LEVELS,), jnp.float32),
            pltpu.SemaphoreType.DMA((len(sources) + 1,)),
        ],
    )(sound_stability_ratio, sides, *sources)
    at.update({name: near(values) for name, values in zip(AFTER, staged)})
    above = near(lax.ppermute(down, "face", ring("face", -1)))
    below = near(lax.ppermute(up, "face", ring("face", 1)))
    sides = pl.pallas_call(
        side_kernel, out_shape=kept(2 * ROWS, LANES), in_specs=[VMEM] * 3, out_specs=VMEM
    )(sides, above, below)
    wide = pl.pallas_call(
        widen_kernel, out_shape=kept(FIELDS, 2 * ROWS, LANES), in_specs=[VMEM] * 5, out_specs=VMEM
    )(*(at[name] for name in ("press", "zonal", "merid")), above, below)
    twin = near(lax.ppermute(sides, "tile", swaps("tile", 0)))
    cross = near(lax.ppermute(sides, "tile", swaps("tile", 1)))
    pressure_new, rest, halo, slots = pl.pallas_call(
        columns_kernel,
        out_shape=[
            struct(LEVELS, ROWS, LANES),
            kept(LEVELS, ROWS, LANES),
            kept(8, LANES),
            struct(3 * SOURCES, LANES),
        ],
        in_specs=[VMEM] * 10,
        out_specs=[VMEM] * 4,
    )(
        near(speeds),
        near(wide),
        at["heat"],
        at["link"],
        at["site"],
        at["area"],
        near(inverse),
        near(weight),
        twin,
        cross,
    )
    arrived = exchanged(slots, 3)
    edge, calm = pl.pallas_call(
        edge_kernel,
        out_shape=[kept(LANES, LANES), kept(LEVELS, ROWS, LANES)],
        in_specs=[VMEM] * 5,
        out_specs=[VMEM] * 2,
    )(at["resist"], at["frozen"], near(halo), near(gain), near(rest))
    edge = near(edge)
    fresh, flux, ice_terms = pl.pallas_call(
        ice_kernel,
        out_shape=[struct(*ice), struct(2 * SOURCES, LANES), kept(2, *ice)],
        in_specs=[VMEM] * 6,
        out_specs=[VMEM] * 3,
    )(arrived, *(at[name] for name in ("target", "skin", "frozen", "resist")), edge)
    returned = exchanged(flux, 2)
    drifted = pl.pallas_call(
        drift_kernel,
        out_shape=kept(*ice),
        in_specs=[VMEM] * 4,
        out_specs=VMEM,
        scratch_shapes=[pltpu.VMEM((4, 2 * EVP + 2, ROWS, LANES), jnp.float32)],
    )(at["motion"], at["strain"], near(ice_terms), near(halo))
    temp_new, velocity = pl.pallas_call(
        last_kernel,
        out_shape=[struct(LEVELS, ROWS, LANES), struct(*ice)],
        in_specs=[VMEM] * 6,
        out_specs=[VMEM] * 2,
    )(returned, at["site"], near(answer), near(calm), near(drifted), edge)
    return (temp_new, pressure_new, fresh.reshape(-1), velocity.reshape(-1))


def solution(mesh):
    block = P(None, "face", "tile")
    slot = P(BOTH, None, None)
    cells = P(BOTH)
    return jax.shard_map(
        local,
        mesh=mesh,
        in_specs=(block,) * 5 + (P(),) + (slot,) * 3 + (cells,) * 5,
        out_specs=(block, block, cells, cells),
        check_vma=False,
    )
```

```python
import functools

import jax
import jax.numpy as jnp
from jax import lax
from jax.experimental import pallas as pl
from jax.experimental.pallas import tpu as pltpu
from jax.sharding import PartitionSpec as P

SUBS = 2
EVP = 20
LEVELS = 8
ROWS = 8
LANES = 128
SOURCES = 128
ICE_ROWS = 16
FIELDS = 3 * LEVELS
UP_ROWS = (2, 2, 1)
DOWN_ROWS = (2, 1, 1)
UP = LEVELS * sum(UP_ROWS)
DOWN = LEVELS * sum(DOWN_ROWS)
TILES = 32
STAGED = ("press", "zonal", "merid", "motion", "strain", "resist", "frozen")
AFTER = ("link", "site", "area", "heat", "target", "skin")

isentropic_lapse = 0.3
gravity_step = 0.5
floe_warmth = 2.0
floor_conductance = 1.0
relaxation = 0.5
stress_decay = 0.05
mobility = 0.3
water_drag = 0.1

BOTH = ("face", "tile")
VMEM = pl.BlockSpec(memory_space=pltpu.VMEM)


def struct(*shape):
    return jax.ShapeDtypeStruct(shape, jnp.float32)


def kept(*shape):
    return pltpu.VMEM(shape, jnp.float32)


def near(values):
    return pltpu.with_memory_space_constraint(values, pltpu.VMEM)


def lanes_of(shape):
    return lax.broadcasted_iota(jnp.int32, shape, len(shape) - 1)


def rows_of(shape):
    return lax.broadcasted_iota(jnp.int32, shape, len(shape) - 2)


def copies_of(sources, targets, sems):
    copies = [
        pltpu.make_async_copy(source, target, sems.at[at])
        for at, (source, target) in enumerate(zip(sources, targets))
    ]
    for copy in copies:
        copy.start()
    return copies


def slab_rows(counts, field, level):
    return pl.ds(LEVELS * sum(counts[:field]) + counts[field] * level, counts[field])


def stage_kernel(*refs):
    count = len(STAGED)
    targets = refs[count : 2 * count]
    side_out, down_out, up_out, sems = refs[2 * count :]
    copies = copies_of(refs[:count], targets, sems)
    motion_ref, strain_ref, resist_ref, frozen_ref = targets[3:7]
    for copy in copies[:3]:
        copy.wait()
    lane = lanes_of((ROWS, LANES))
    packed = jnp.zeros((ROWS, LANES), jnp.float32)
    for field, ref in enumerate(targets[:3]):
        for level in range(LEVELS):
            cells = ref[level]
            at = 4 * (field * LEVELS + level)
            moved = pltpu.roll(cells, 2 + at, 1)
            packed = jnp.where((lane >= at) & (lane < at + 4), moved, packed)
            down_out[slab_rows(DOWN_ROWS, field, level), :] = cells[: DOWN_ROWS[field]]
            up_out[slab_rows(UP_ROWS, field, level), :] = cells[ROWS - UP_ROWS[field] :]
    for copy in copies[3:]:
        copy.wait()
    edge = jnp.zeros((1, LANES), jnp.float32)
    lane = lanes_of((1, LANES))
    for row, first, shift in ((ICE_ROWS - 1, 0, EVP), (0, 3, 0)):
        here = pl.ds(row, 1)
        strength = resist_ref[here] * (0.1 + 0.9 * frozen_ref[here].astype(jnp.float32))
        for at, cells in enumerate((motion_ref[here], strain_ref[here], strength), first):
            moved = pltpu.roll(cells, (EVP * at + shift) % LANES, 1)
            edge = jnp.where((lane >= EVP * at) & (lane < EVP * at + EVP), moved, edge)
    edge = jnp.broadcast_to(edge, (ROWS, LANES))
    side_out[pl.ds(0, ROWS), :] = packed
    side_out[pl.ds(ROWS, ROWS), :] = edge
    down_out[pl.ds(DOWN, 2), :] = packed[:2]
    up_out[pl.ds(UP, 2), :] = packed[ROWS - 2 :]
    down_out[pl.ds(DOWN + 2, 6), :] = edge[:6]
    up_out[pl.ds(UP + 2, 6), :] = edge[:6]


def factor_kernel(*refs):
    count = len(AFTER)
    speed_ref, _, *refs = refs
    targets = refs[count : 2 * count]
    speed_out, gain_out, inverse_out, answer_out, slot_out, speeds, sems = refs[2 * count :]
    speed_copy = pltpu.make_async_copy(speed_ref, speeds, sems.at[count])
    speed_copy.start()
    copies = copies_of(refs[:count], targets, sems)
    link_ref, site_ref, area_ref = targets[:3]
    copies[0].wait()
    link = link_ref[0]
    inverse = 1.0 / (1.0 + link)
    gain = link * inverse
    inverse_out[0] = inverse
    gain_out[0] = gain
    for level in range(1, LEVELS - 1):
        earlier, link = link, link_ref[level]
        inverse = 1.0 / (1.0 + earlier + link - earlier * gain)
        gain = link * inverse
        inverse_out[level] = inverse
        gain_out[level] = gain
    inverse = 1.0 / (1.0 + link * (1.0 - gain))
    beta = gravity_step * inverse
    inverse_out[LEVELS - 1] = inverse
    answer_out[LEVELS - 1] = answer = beta
    for level in range(LEVELS - 2, -1, -1):
        answer = gain_out[level] * answer
        answer_out[level] = answer
    drag = link_ref[LEVELS - 1]
    table = spread_rows(drag / (1.0 + drag * beta))
    for copy in copies[1:3]:
        copy.wait()
    for start in range(0, SOURCES, ROWS):
        here = pl.ds(start, ROWS)
        (found,) = look_up((table,), site_ref[here, :])
        slot_out[here, :] = area_ref[here, :] * found
    speed_copy.wait()
    for level in range(LEVELS):
        speed_out[pl.ds(level, 1), :] = jnp.full((1, LANES), speeds[level])
    for copy in copies[3:]:
        copy.wait()


def side_kernel(side_ref, above_ref, below_ref, out_ref):
    out_ref[pl.ds(0, ROWS + 3), :] = side_ref[pl.ds(0, ROWS + 3), :]
    out_ref[pl.ds(8, 2), :] = above_ref[pl.ds(DOWN, 2), :]
    out_ref[pl.ds(11, 1), :] = below_ref[pl.ds(UP + 2, 1), :]
    out_ref[pl.ds(12, 2), :] = above_ref[pl.ds(DOWN + 2, 2), :]
    out_ref[pl.ds(14, 2), :] = below_ref[pl.ds(UP, 2), :]


def widen_kernel(p_ref, u_ref, v_ref, above_ref, below_ref, wide_out):
    for field, ref in enumerate((p_ref, u_ref, v_ref)):
        above, below = DOWN_ROWS[field], UP_ROWS[field]
        for level in range(LEVELS):
            at = field * LEVELS + level
            wide_out[at, pl.ds(0, ROWS), :] = ref[level]
            wide_out[at, pl.ds(8, 8), :] = jnp.zeros((8, LANES), jnp.float32)
            wide_out[at, pl.ds(8, above), :] = above_ref[slab_rows(DOWN_ROWS, field, level), :]
            wide_out[at, pl.ds(16 - below, below), :] = below_ref[
                slab_rows(UP_ROWS, field, level), :
            ]


def look_up(tables, index):
    high = index // LANES
    low = index % LANES
    found = [None] * len(tables)
    for row in range(len(tables[0])):
        here = high == row
        for at, rows in enumerate(tables):
            taken = jnp.take_along_axis(rows[row], low, axis=1, mode="promise_in_bounds")
            found[at] = taken if row == 0 else jnp.where(here, taken, found[at])
    return found


def spread_rows(table):
    return [
        jnp.broadcast_to(table[row : row + 1], (ROWS, LANES)) for row in range(table.shape[0])
    ]


def columns_kernel(
    speed_ref,
    wide_ref,
    heat_ref,
    link_ref,
    site_ref,
    area_ref,
    inverse_ref,
    weight_ref,
    twin_ref,
    cross_ref,
    press_out,
    rest_out,
    halo_out,
    slots_out,
):
    shape = (2 * ROWS, LANES)
    place = lax.axis_index("tile")
    even = place % 2 == 0
    left = jnp.where(even, cross_ref[...], twin_ref[...])
    right = jnp.where(even, twin_ref[...], cross_ref[...])
    border = jnp.where(lanes_of(shape) % 4 < 2, left, right)
    temps = []
    for level in range(LEVELS):
        speed = jnp.broadcast_to(speed_ref[pl.ds(level, 1), 0:1], (2 * ROWS, 2 * LANES))
        now = []
        for field in range(3):
            at = field * LEVELS + level
            outer = pltpu.roll(border, (126 - 4 * at) % LANES, 1)
            now.append(jnp.concatenate([wide_ref[at], outer], axis=1))
        press, zonal, merid = now
        for _ in range(SUBS):
            zonal = zonal - speed * (pltpu.roll(press, 15, 0) - press)
            merid = merid - speed * (pltpu.roll(press, 255, 1) - press)
            press = press - speed * (
                zonal - pltpu.roll(zonal, 1, 0) + merid - pltpu.roll(merid, 1, 1)
            )
        final = press[:ROWS, :LANES]
        press_out[level] = final
        temps.append(heat_ref[level] + isentropic_lapse * final)
    last_zonal = zonal[:ROWS, :LANES]
    last_merid = merid[:ROWS, :LANES]

    rest = temps[0] * inverse_ref[0]
    rest_out[0] = rest
    for level in range(1, LEVELS):
        rest = (temps[level] + link_ref[level - 1] * rest) * inverse_ref[level]
        rest_out[level] = rest
    gamma = rest
    stress = link_ref[LEVELS - 1] * (last_zonal + 0.5 * last_merid)

    tables = [spread_rows(table) for table in (gamma, stress)]
    for start in range(0, SOURCES, ROWS):
        here = pl.ds(start, ROWS)
        found = look_up(tables, site_ref[here, :])
        slot_w = weight_ref[here, :]
        slots_out[pl.ds(3 * start, ROWS, stride=3), :] = slot_w
        slots_out[pl.ds(3 * start + 1, ROWS, stride=3), :] = slot_w * found[0]
        slots_out[pl.ds(3 * start + 2, ROWS, stride=3), :] = area_ref[here, :] * found[1]
    before = jnp.where(place == 0, left[11:12], left[10:11])
    after = jnp.where(place == TILES - 1, right[12:13], right[10:11])
    for at in range(3):
        halo_out[pl.ds(at, 1), :] = pltpu.roll(before, LANES - EVP - EVP * at, 1)
        halo_out[pl.ds(4 + at, 1), :] = pltpu.roll(after, LANES - EVP * (at + 3), 1)


def in_three(values):
    first = values.astype(jnp.bfloat16)
    left = values - first.astype(jnp.float32)
    second = left.astype(jnp.bfloat16)
    third = (left - second.astype(jnp.float32)).astype(jnp.bfloat16)
    return first.astype(jnp.float32), second.astype(jnp.float32), third.astype(jnp.float32)


def segment_sums(read, index_ref, values, high_row, low_count, group=32):
    high_count = len(high_row)
    shape = (high_count, LANES)
    rows = rows_of(shape)
    high_here = sum(jnp.where(rows == at, high, 0) for high, at in enumerate(high_row))
    low_here = rows_of((low_count, LANES))
    count = 3 * values * high_count

    def step(block, total):
        start = pl.multiple_of(block * group, group)
        index = index_ref[pl.ds(start, group), :]
        high = index // low_count
        low = index % low_count
        parts = [part for value in range(values) for part in in_three(read(value, start, group))]
        carried, spread = [], []
        for row in range(group):
            here = high_here == high[row : row + 1]
            carried.append(
                jnp.concatenate(
                    [
                        jnp.where(here, jnp.broadcast_to(part[row : row + 1], shape), 0.0).astype(
                            jnp.bfloat16
                        )
                        for part in parts
                    ],
                    axis=0,
                )
            )
            spread.append(
                jnp.where(low_here == low[row : row + 1], 1.0, 0.0).astype(jnp.bfloat16)
            )
        return total + lax.dot_general(
            jnp.concatenate(carried, axis=1),
            jnp.concatenate(spread, axis=1),
            (((1,), (1,)), ((), ())),
            preferred_element_type=jnp.float32,
        )

    total = lax.fori_loop(
        0, SOURCES // group, step, jnp.zeros((count, low_count), jnp.float32), unroll=True
    )
    sums = []
    for value in range(values):
        at = 3 * value * high_count
        sums.append(
            total[at + 2 * high_count : at + 3 * high_count]
            + total[at + high_count : at + 2 * high_count]
            + total[at : at + high_count]
        )
    return sums


def ice_kernel(
    slots_ref, target_ref, skin_ref, frozen_ref, resist_ref, _, skin_out, flux_out, ice_out
):
    def read(value, start, group):
        return slots_ref[pl.ds(3 * start + value, group, stride=3), :]

    heat, warmth, tau = segment_sums(read, target_ref, 3, range(ICE_ROWS), LANES, group=8)
    skin = skin_ref[...]
    frozen = frozen_ref[...]
    fresh = jnp.where(
        frozen == 1,
        (floe_warmth * skin + warmth) / (floe_warmth + floor_conductance + heat),
        skin,
    )
    skin_out[...] = fresh
    table = spread_rows(fresh)
    for start in range(0, SOURCES, ROWS):
        (at_floe,) = look_up((table,), target_ref[pl.ds(start, ROWS), :])
        flux_out[pl.ds(2 * start, ROWS, stride=2), :] = (
            slots_ref[pl.ds(3 * start, ROWS, stride=3), :] * at_floe
            - slots_ref[pl.ds(3 * start + 1, ROWS, stride=3), :]
        )
    ends = jnp.where(
        lanes_of((1, LANES)) < LANES // 2, tau[0:1], tau[ICE_ROWS - 1 : ICE_ROWS]
    )
    flux_out[pl.ds(1, SOURCES, stride=2), :] = jnp.broadcast_to(ends, (SOURCES, LANES))
    ice_out[0] = resist_ref[...] * (0.1 + 0.9 * frozen.astype(jnp.float32))
    ice_out[1] = tau


def paired(even_rows, odd_rows):
    lane = lanes_of((ROWS, LANES))
    out = []
    for at in range(2):
        index = (2 * lane + at) % LANES
        out.append(
            jnp.where(
                lane < LANES // 2,
                jnp.take_along_axis(even_rows, index, axis=1, mode="promise_in_bounds"),
                jnp.take_along_axis(odd_rows, index, axis=1, mode="promise_in_bounds"),
            )
        )
    return out


def neighbourhood(even_rows, odd_rows, before, after):
    shape = (ROWS, LANES)
    lane = lanes_of(shape)
    row = rows_of(shape)
    own = paired(even_rows, odd_rows)
    behind = paired(jnp.broadcast_to(before, shape), jnp.broadcast_to(before, shape))
    ahead = paired(jnp.broadcast_to(after, shape), jnp.broadcast_to(after, shape))
    cells = {}
    for at in range(2):
        cells[at] = own[at]
        up = jnp.where(row == ROWS - 1, ahead[at], pltpu.roll(own[at], ROWS - 1, 0))
        down = jnp.where(row == 0, behind[at], pltpu.roll(own[at], 1, 0))
        for far in range(1, EVP // 2 + 1):
            cells[at + 2 * far] = pltpu.roll(
                jnp.where(lane < far, up, own[at]), LANES - far, 1
            )
            cells[at - 2 * far] = pltpu.roll(
                jnp.where(lane >= LANES - far, down, own[at]), far, 1
            )
    return cells


def drift_kernel(motion_ref, strain_ref, ice_ref, halo_ref, out_ref, held):
    place = lax.axis_index("face") * TILES + lax.axis_index("tile")
    blank = jnp.zeros((1, LANES), jnp.float32)
    even, odd = pl.ds(0, ROWS, stride=2), pl.ds(1, ROWS, stride=2)
    first = jnp.where(place == 0, 0.0, 1.0)
    last = jnp.where(place == SOURCES - 1, 0.0, 1.0)
    slow = 1.0 / (1.0 + mobility * water_drag)
    fade = 1.0 / (1.0 + stress_decay)
    arrays = (
        (motion_ref[even], motion_ref[odd], halo_ref[0:1], halo_ref[4:5], 1.0),
        (strain_ref[even], strain_ref[odd], halo_ref[1:2], halo_ref[5:6], mobility * slow),
        (
            ice_ref[0, even],
            ice_ref[0, odd],
            halo_ref[2:3],
            halo_ref[6:7],
            mobility * slow * relaxation * fade,
        ),
        (ice_ref[1, even], ice_ref[1, odd], blank, blank, mobility * slow),
    )
    for at, (even_rows, odd_rows, before, after, scale) in enumerate(arrays):
        cells = neighbourhood(
            even_rows * scale,
            odd_rows * scale,
            before * (first * scale),
            after * (last * scale),
        )
        for cell, values in cells.items():
            held[at, cell + EVP] = values
    shape = (ROWS, LANES)
    where = LANES * rows_of(shape) + lanes_of(shape)

    def inside(cell):
        end = (ROWS * LANES * 2 - cell) // 2
        return jnp.where((where == end) & (place == SOURCES - 1), 0.0, 1.0)

    width = 2 * EVP + 2
    velocity = [held[0, at] for at in range(width)]
    stress = [held[1, at] for at in range(width)]
    for turn in range(EVP):
        for at in range(turn, width - turn - 1):
            stress[at] = stress[at] * fade + held[2, at] * (velocity[at + 1] - velocity[at])
        for at in range(turn + 1, width - turn - 1):
            force = stress[at] - stress[at - 1] + held[3, at]
            if at >= EVP + 2 and at % 2 == 0:
                force = force * inside(at - EVP)
            velocity[at] = velocity[at] * slow + force
    lane = lanes_of(shape)
    for rows, half in ((even, 0), (odd, LANES // 2)):
        index = lane // 2 + half
        out_ref[rows] = jnp.where(
            lane % 2 == 0,
            jnp.take_along_axis(velocity[EVP], index, axis=1, mode="promise_in_bounds"),
            jnp.take_along_axis(velocity[EVP + 1], index, axis=1, mode="promise_in_bounds"),
        )


def edge_kernel(
    resist_ref, frozen_ref, halo_ref, gain_ref, rest_ref, out_ref, calm_out, held
):
    calm_out[LEVELS - 1] = calm = rest_ref[LEVELS - 1]
    for level in range(LEVELS - 2, -1, -1):
        calm = gain_ref[level] * calm + rest_ref[level]
        calm_out[level] = calm
    slow = 1.0 / (1.0 + mobility * water_drag)
    fade = 1.0 / (1.0 + stress_decay)
    half = LANES // 2
    here = lanes_of((1, LANES)) < half
    ends = [
        resist_ref[pl.ds(row, 1)] * (0.1 + 0.9 * frozen_ref[pl.ds(row, 1)].astype(jnp.float32))
        for row in (0, ICE_ROWS - 1)
    ]
    strength = (
        jnp.where(here, ends[0], halo_ref[2:3]),
        jnp.where(here, halo_ref[6:7], ends[1]),
    )
    pull = jnp.concatenate(
        [jnp.broadcast_to(pltpu.roll(row, half, 1), (24, LANES)) for row in strength], axis=0
    ) * (mobility * slow * relaxation * fade)
    shape = (48, LANES)
    row = rows_of(shape)
    lane = lanes_of(shape)
    source = jnp.where(row < 24, half - EVP + row, half - 24 + row)
    push = jnp.where((lane == source) & (row % 24 < EVP), mobility * slow, 0.0)
    velocity = jnp.zeros(shape, jnp.float32)
    stress = jnp.zeros(shape, jnp.float32)
    for _ in range(EVP):
        stress = stress * fade + pull * (pltpu.roll(velocity, LANES - 1, 1) - velocity)
        velocity = velocity * slow + (stress - pltpu.roll(stress, 1, 1) + push)
    velocity = pltpu.roll(velocity, half, 1)
    velocity = jnp.where(
        ((row < 24) & (lane < EVP)) | ((row >= 24) & (lane >= LANES - EVP)), velocity, 0.0
    )
    held[...] = jnp.zeros((LANES, LANES), jnp.float32)
    held[pl.ds(0, EVP), :] = velocity[24 : 24 + EVP]
    held[pl.ds(LANES - EVP, EVP), :] = velocity[:EVP]
    out_ref[...] = jnp.concatenate(in_three(held[...]), axis=1).astype(jnp.bfloat16)


def last_kernel(
    flux_ref, site_ref, answer_ref, calm_ref, drift_ref, edge_ref, heat_out, motion_out
):
    def read(value, start, group):
        return flux_ref[pl.ds(2 * start, group, stride=2), :]

    place = lax.axis_index("face") * TILES + lax.axis_index("tile")
    lane = lanes_of((1, LANES))
    before = flux_ref[pl.ds(2 * jnp.maximum(place - 1, 0) + 1, 1), :]
    after = flux_ref[pl.ds(2 * jnp.minimum(place + 1, SOURCES - 1) + 1, 1), :]
    outside = jnp.where(
        lane < LANES // 2,
        after * jnp.where(place == SOURCES - 1, 0.0, 1.0),
        before * jnp.where(place == 0, 0.0, 1.0),
    )
    products = lax.dot_general(
        jnp.concatenate(
            [jnp.broadcast_to(part, (ROWS, LANES)) for part in in_three(outside)]
            + [jnp.zeros((ROWS, LANES), jnp.float32)],
            axis=0,
        ).astype(jnp.bfloat16),
        edge_ref[...],
        (((1,), (0,)), ((), ())),
        preferred_element_type=jnp.float32,
    )
    by_part = [
        products[:, LANES * part : LANES * (part + 1)] for part in range(3)
    ]
    by_part = [part[:ROWS] + part[ROWS : 2 * ROWS] + part[2 * ROWS : 3 * ROWS] for part in by_part]
    added = (by_part[0] + by_part[1] + by_part[2])[0:1]
    motion_out[...] = drift_ref[...]
    motion_out[0:1] = drift_ref[0:1] + jnp.where(lane < EVP, added, 0.0)
    end = pl.ds(ICE_ROWS - 1, 1)
    motion_out[end] = drift_ref[end] + jnp.where(lane >= LANES - EVP, added, 0.0)

    order = [ROWS * (half % 2) + half // 2 for half in range(2 * ROWS)]
    (halves,) = segment_sums(read, site_ref, 1, order, LANES // 2)
    surface_flux = jnp.concatenate([halves[:ROWS], halves[ROWS:]], axis=1)
    for level in range(LEVELS):
        heat_out[level] = answer_ref[level] * surface_flux + calm_ref[level]


def ring(axis, step):
    count = lax.axis_size(axis)
    return [(i, (i + step) % count) for i in range(count)]


def swaps(axis, first):
    count = lax.axis_size(axis)
    pairs = [(i, (i + 1) % count) for i in range(first, count, 2)]
    return sorted(pairs + [(b, a) for a, b in pairs])


def exchanged(rows, count):
    blocks = rows.reshape(SOURCES, count, 1, LANES)
    blocks = lax.all_to_all(blocks, BOTH, split_axis=0, concat_axis=0, tiled=True)
    return near(blocks.reshape(SOURCES * count, LANES))


def local(
    squeeze_anomaly,
    eastward_airflow,
    northward_airflow,
    thermal_anomaly,
    diffusivity_link,
    sound_stability_ratio,
    overlay_source_site,
    overlay_target_floe,
    overlay_fraction,
    floe_skin_kelvin,
    frozen_indicator,
    floe_motion,
    floe_strain_tensor,
    floe_compress_resist,
):
    ice = (ICE_ROWS, LANES)
    slot = (SOURCES, LANES)
    arguments = dict(
        press=squeeze_anomaly,
        zonal=eastward_airflow,
        merid=northward_airflow,
        motion=floe_motion.reshape(ice),
        strain=floe_strain_tensor.reshape(ice),
        resist=floe_compress_resist.reshape(ice),
        frozen=frozen_indicator.reshape(ice),
        skin=floe_skin_kelvin.reshape(ice),
        heat=thermal_anomaly,
        link=diffusivity_link,
        site=overlay_source_site.reshape(slot),
        area=overlay_fraction.reshape(slot),
        target=overlay_target_floe.reshape(slot),
    )
    hbm = pl.BlockSpec(memory_space=pl.ANY)
    sources = [arguments[name] for name in STAGED]
    *staged, sides, down, up = pl.pallas_call(
        stage_kernel,
        out_shape=[pltpu.VMEM(source.shape, source.dtype) for source in sources]
        + [kept(2 * ROWS, LANES), kept(DOWN + 8, LANES), kept(UP + 8, LANES)],
        in_specs=[hbm] * len(sources),
        out_specs=[VMEM] * (len(sources) + 3),
        scratch_shapes=[pltpu.SemaphoreType.DMA((len(sources),))],
    )(*sources)
    at = {name: near(values) for name, values in zip(STAGED, staged)}
    sides = near(sides)
    sources = [arguments[name] for name in AFTER]
    *staged, speeds, gain, inverse, answer, weight = pl.pallas_call(
        factor_kernel,
        out_shape=[pltpu.VMEM(source.shape, source.dtype) for source in sources]
        + [kept(LEVELS, LANES)]
        + [kept(LEVELS, ROWS, LANES)] * 3
        + [kept(*slot)],
        in_specs=[hbm, VMEM] + [hbm] * len(sources),
        out_specs=[VMEM] * (len(sources) + 5),
        scratch_shapes=[
            pltpu.SMEM((LEVELS,), jnp.float32),
            pltpu.SemaphoreType.DMA((len(sources) + 1,)),
        ],
    )(sound_stability_ratio, sides, *sources)
    at.update({name: near(values) for name, values in zip(AFTER, staged)})
    above = near(lax.ppermute(down, "face", ring("face", -1)))
    below = near(lax.ppermute(up, "face", ring("face", 1)))
    sides = pl.pallas_call(
        side_kernel, out_shape=kept(2 * ROWS, LANES), in_specs=[VMEM] * 3, out_specs=VMEM
    )(sides, above, below)
    wide = pl.pallas_call(
        widen_kernel, out_shape=kept(FIELDS, 2 * ROWS, LANES), in_specs=[VMEM] * 5, out_specs=VMEM
    )(*(at[name] for name in ("press", "zonal", "merid")), above, below)
    twin = near(lax.ppermute(sides, "tile", swaps("tile", 0)))
    cross = near(lax.ppermute(sides, "tile", swaps("tile", 1)))
    pressure_new, rest, halo, slots = pl.pallas_call(
        columns_kernel,
        out_shape=[
            struct(LEVELS, ROWS, LANES),
            kept(LEVELS, ROWS, LANES),
            kept(8, LANES),
            struct(3 * SOURCES, LANES),
        ],
        in_specs=[VMEM] * 10,
        out_specs=[VMEM] * 4,
    )(
        near(speeds),
        near(wide),
        at["heat"],
        at["link"],
        at["site"],
        at["area"],
        near(inverse),
        near(weight),
        twin,
        cross,
    )
    arrived = exchanged(slots, 3)
    edge, calm = pl.pallas_call(
        edge_kernel,
        out_shape=[pltpu.VMEM((LANES, 3 * LANES), jnp.bfloat16), kept(LEVELS, ROWS, LANES)],
        in_specs=[VMEM] * 5,
        out_specs=[VMEM] * 2,
        scratch_shapes=[pltpu.VMEM((LANES, LANES), jnp.float32)],
    )(at["resist"], at["frozen"], near(halo), near(gain), near(rest))
    edge = near(edge)
    fresh, flux, ice_terms = pl.pallas_call(
        ice_kernel,
        out_shape=[struct(*ice), struct(2 * SOURCES, LANES), kept(2, *ice)],
        in_specs=[VMEM] * 6,
        out_specs=[VMEM] * 3,
    )(arrived, *(at[name] for name in ("target", "skin", "frozen", "resist")), edge)
    returned = exchanged(flux, 2)
    drifted = pl.pallas_call(
        drift_kernel,
        out_shape=kept(*ice),
        in_specs=[VMEM] * 4,
        out_specs=VMEM,
        scratch_shapes=[pltpu.VMEM((4, 2 * EVP + 2, ROWS, LANES), jnp.float32)],
    )(at["motion"], at["strain"], near(ice_terms), near(halo))
    temp_new, velocity = pl.pallas_call(
        last_kernel,
        out_shape=[struct(LEVELS, ROWS, LANES), struct(*ice)],
        in_specs=[VMEM] * 6,
        out_specs=[VMEM] * 2,
    )(returned, at["site"], near(answer), near(calm), near(drifted), edge)
    return (temp_new, pressure_new, fresh.reshape(-1), velocity.reshape(-1))


def solution(mesh):
    block = P(None, "face", "tile")
    slot = P(BOTH, None, None)
    cells = P(BOTH)
    return jax.shard_map(
        local,
        mesh=mesh,
        in_specs=(block,) * 5 + (P(),) + (slot,) * 3 + (cells,) * 5,
        out_specs=(block, block, cells, cells),
        check_vma=False,
    )
```

```python
import functools

import jax
import jax.numpy as jnp
from jax import lax
from jax.experimental import pallas as pl
from jax.experimental.pallas import tpu as pltpu
from jax.sharding import PartitionSpec as P

SUBS = 2
EVP = 20
LEVELS = 8
ROWS = 8
LANES = 128
SOURCES = 128
ICE_ROWS = 16
FIELDS = 3 * LEVELS
UP_ROWS = (2, 2, 1)
DOWN_ROWS = (2, 1, 1)
UP = LEVELS * sum(UP_ROWS)
DOWN = LEVELS * sum(DOWN_ROWS)
TILES = 32
STAGED = ("press", "zonal", "merid", "motion", "strain", "resist", "frozen")
AFTER = ("link", "site", "area", "heat", "target", "skin")

isentropic_lapse = 0.3
gravity_step = 0.5
floe_warmth = 2.0
floor_conductance = 1.0
relaxation = 0.5
stress_decay = 0.05
mobility = 0.3
water_drag = 0.1

BOTH = ("face", "tile")
VMEM = pl.BlockSpec(memory_space=pltpu.VMEM)


def struct(*shape):
    return jax.ShapeDtypeStruct(shape, jnp.float32)


def kept(*shape):
    return pltpu.VMEM(shape, jnp.float32)


def near(values):
    return pltpu.with_memory_space_constraint(values, pltpu.VMEM)


def lanes_of(shape):
    return lax.broadcasted_iota(jnp.int32, shape, len(shape) - 1)


def rows_of(shape):
    return lax.broadcasted_iota(jnp.int32, shape, len(shape) - 2)


def copies_of(sources, targets, sems):
    copies = [
        pltpu.make_async_copy(source, target, sems.at[at])
        for at, (source, target) in enumerate(zip(sources, targets))
    ]
    for copy in copies:
        copy.start()
    return copies


def slab_rows(counts, field, level):
    return pl.ds(LEVELS * sum(counts[:field]) + counts[field] * level, counts[field])


def stage_kernel(*refs):
    count = len(STAGED)
    targets = refs[count : 2 * count]
    side_out, down_out, up_out, sems = refs[2 * count :]
    copies = copies_of(refs[:count], targets, sems)
    motion_ref, strain_ref, resist_ref, frozen_ref = targets[3:7]
    for copy in copies[:3]:
        copy.wait()
    lane = lanes_of((ROWS, LANES))
    packed = jnp.zeros((ROWS, LANES), jnp.float32)
    for field, ref in enumerate(targets[:3]):
        for level in range(LEVELS):
            cells = ref[level]
            at = 4 * (field * LEVELS + level)
            moved = pltpu.roll(cells, 2 + at, 1)
            packed = jnp.where((lane >= at) & (lane < at + 4), moved, packed)
            down_out[slab_rows(DOWN_ROWS, field, level), :] = cells[: DOWN_ROWS[field]]
            up_out[slab_rows(UP_ROWS, field, level), :] = cells[ROWS - UP_ROWS[field] :]
    for copy in copies[3:]:
        copy.wait()
    edge = jnp.zeros((1, LANES), jnp.float32)
    lane = lanes_of((1, LANES))
    for row, first, shift in ((ICE_ROWS - 1, 0, EVP), (0, 3, 0)):
        here = pl.ds(row, 1)
        strength = resist_ref[here] * (0.1 + 0.9 * frozen_ref[here].astype(jnp.float32))
        for at, cells in enumerate((motion_ref[here], strain_ref[here], strength), first):
            moved = pltpu.roll(cells, (EVP * at + shift) % LANES, 1)
            edge = jnp.where((lane >= EVP * at) & (lane < EVP * at + EVP), moved, edge)
    edge = jnp.broadcast_to(edge, (ROWS, LANES))
    side_out[pl.ds(0, ROWS), :] = packed
    side_out[pl.ds(ROWS, ROWS), :] = edge
    down_out[pl.ds(DOWN, 2), :] = packed[:2]
    up_out[pl.ds(UP, 2), :] = packed[ROWS - 2 :]
    down_out[pl.ds(DOWN + 2, 6), :] = edge[:6]
    up_out[pl.ds(UP + 2, 6), :] = edge[:6]


def factor_kernel(*refs):
    count = len(AFTER)
    speed_ref, _, *refs = refs
    targets = refs[count : 2 * count]
    speed_out, gain_out, inverse_out, answer_out, slot_out, speeds, sems = refs[2 * count :]
    speed_copy = pltpu.make_async_copy(speed_ref, speeds, sems.at[count])
    speed_copy.start()
    copies = copies_of(refs[:count], targets, sems)
    link_ref, site_ref, area_ref = targets[:3]
    copies[0].wait()
    link = link_ref[0]
    inverse = 1.0 / (1.0 + link)
    gain = link * inverse
    inverse_out[0] = inverse
    gain_out[0] = gain
    for level in range(1, LEVELS - 1):
        earlier, link = link, link_ref[level]
        inverse = 1.0 / (1.0 + earlier + link - earlier * gain)
        gain = link * inverse
        inverse_out[level] = inverse
        gain_out[level] = gain
    inverse = 1.0 / (1.0 + link * (1.0 - gain))
    beta = gravity_step * inverse
    inverse_out[LEVELS - 1] = inverse
    answer_out[LEVELS - 1] = answer = beta
    for level in range(LEVELS - 2, -1, -1):
        answer = gain_out[level] * answer
        answer_out[level] = answer
    drag = link_ref[LEVELS - 1]
    table = spread_rows(drag / (1.0 + drag * beta))
    for copy in copies[1:3]:
        copy.wait()
    for start in range(0, SOURCES, ROWS):
        here = pl.ds(start, ROWS)
        (found,) = look_up((table,), site_ref[here, :])
        slot_out[here, :] = area_ref[here, :] * found
    speed_copy.wait()
    for level in range(LEVELS):
        speed_out[pl.ds(level, 1), :] = jnp.full((1, LANES), speeds[level])
    for copy in copies[3:]:
        copy.wait()


def side_kernel(side_ref, above_ref, below_ref, out_ref):
    out_ref[pl.ds(0, ROWS + 3), :] = side_ref[pl.ds(0, ROWS + 3), :]
    out_ref[pl.ds(8, 2), :] = above_ref[pl.ds(DOWN, 2), :]
    out_ref[pl.ds(11, 1), :] = below_ref[pl.ds(UP + 2, 1), :]
    out_ref[pl.ds(12, 2), :] = above_ref[pl.ds(DOWN + 2, 2), :]
    out_ref[pl.ds(14, 2), :] = below_ref[pl.ds(UP, 2), :]


def widen_kernel(p_ref, u_ref, v_ref, above_ref, below_ref, wide_out):
    for field, ref in enumerate((p_ref, u_ref, v_ref)):
        above, below = DOWN_ROWS[field], UP_ROWS[field]
        for level in range(LEVELS):
            at = field * LEVELS + level
            wide_out[at, pl.ds(0, ROWS), :] = ref[level]
            wide_out[at, pl.ds(8, 8), :] = jnp.zeros((8, LANES), jnp.float32)
            wide_out[at, pl.ds(8, above), :] = above_ref[slab_rows(DOWN_ROWS, field, level), :]
            wide_out[at, pl.ds(16 - below, below), :] = below_ref[
                slab_rows(UP_ROWS, field, level), :
            ]


def look_up(tables, index):
    high = index >> 7
    low = index & (LANES - 1)
    found = [None] * len(tables)
    for row in range(len(tables[0])):
        here = high == row
        for at, rows in enumerate(tables):
            taken = jnp.take_along_axis(rows[row], low, axis=1, mode="promise_in_bounds")
            found[at] = taken if row == 0 else jnp.where(here, taken, found[at])
    return found


def spread_rows(table):
    return [
        jnp.broadcast_to(table[row : row + 1], (ROWS, LANES)) for row in range(table.shape[0])
    ]


def columns_kernel(
    speed_ref,
    wide_ref,
    heat_ref,
    link_ref,
    site_ref,
    area_ref,
    inverse_ref,
    weight_ref,
    twin_ref,
    cross_ref,
    press_out,
    rest_out,
    halo_out,
    slots_out,
):
    shape = (2 * ROWS, LANES)
    place = lax.axis_index("tile")
    even = place % 2 == 0
    left = jnp.where(even, cross_ref[...], twin_ref[...])
    right = jnp.where(even, twin_ref[...], cross_ref[...])
    border = jnp.where(lanes_of(shape) % 4 < 2, left, right)
    temps = []
    for level in range(LEVELS):
        speed = jnp.broadcast_to(speed_ref[pl.ds(level, 1), 0:1], (2 * ROWS, 2 * LANES))
        now = []
        for field in range(3):
            at = field * LEVELS + level
            outer = pltpu.roll(border, (126 - 4 * at) % LANES, 1)
            now.append(jnp.concatenate([wide_ref[at], outer], axis=1))
        press, zonal, merid = now
        for _ in range(SUBS):
            zonal = zonal - speed * (pltpu.roll(press, 15, 0) - press)
            merid = merid - speed * (pltpu.roll(press, 255, 1) - press)
            press = press - speed * (
                zonal - pltpu.roll(zonal, 1, 0) + merid - pltpu.roll(merid, 1, 1)
            )
        final = press[:ROWS, :LANES]
        press_out[level] = final
        temps.append(heat_ref[level] + isentropic_lapse * final)
    last_zonal = zonal[:ROWS, :LANES]
    last_merid = merid[:ROWS, :LANES]

    rest = temps[0] * inverse_ref[0]
    rest_out[0] = rest
    for level in range(1, LEVELS):
        rest = (temps[level] + link_ref[level - 1] * rest) * inverse_ref[level]
        rest_out[level] = rest
    gamma = rest
    stress = link_ref[LEVELS - 1] * (last_zonal + 0.5 * last_merid)

    tables = [spread_rows(table) for table in (gamma, stress)]
    for start in range(0, SOURCES, ROWS):
        here = pl.ds(start, ROWS)
        found = look_up(tables, site_ref[here, :])
        slot_w = weight_ref[here, :]
        slots_out[pl.ds(3 * start, ROWS, stride=3), :] = slot_w
        slots_out[pl.ds(3 * start + 1, ROWS, stride=3), :] = slot_w * found[0]
        slots_out[pl.ds(3 * start + 2, ROWS, stride=3), :] = area_ref[here, :] * found[1]
    before = jnp.where(place == 0, left[11:12], left[10:11])
    after = jnp.where(place == TILES - 1, right[12:13], right[10:11])
    for at in range(3):
        halo_out[pl.ds(at, 1), :] = pltpu.roll(before, LANES - EVP - EVP * at, 1)
        halo_out[pl.ds(4 + at, 1), :] = pltpu.roll(after, LANES - EVP * (at + 3), 1)


def in_three(values):
    first = values.astype(jnp.bfloat16)
    left = values - first.astype(jnp.float32)
    second = left.astype(jnp.bfloat16)
    third = (left - second.astype(jnp.float32)).astype(jnp.bfloat16)
    return first.astype(jnp.float32), second.astype(jnp.float32), third.astype(jnp.float32)


def segment_sums(read, index_ref, values, high_row, low_count, group=32):
    high_count = len(high_row)
    shape = (high_count, LANES)
    rows = rows_of(shape)
    high_here = sum(jnp.where(rows == at, high, 0) for high, at in enumerate(high_row))
    low_here = rows_of((low_count, LANES))
    count = 3 * values * high_count

    def step(block, total):
        start = pl.multiple_of(block * group, group)
        index = index_ref[pl.ds(start, group), :]
        high = index >> (low_count.bit_length() - 1)
        low = index & (low_count - 1)
        parts = [part for value in range(values) for part in in_three(read(value, start, group))]
        carried, spread = [], []
        for row in range(group):
            here = high_here == high[row : row + 1]
            carried.append(
                jnp.concatenate(
                    [
                        jnp.where(here, jnp.broadcast_to(part[row : row + 1], shape), 0.0).astype(
                            jnp.bfloat16
                        )
                        for part in parts
                    ],
                    axis=0,
                )
            )
            spread.append(
                jnp.where(low_here == low[row : row + 1], 1.0, 0.0).astype(jnp.bfloat16)
            )
        return total + lax.dot_general(
            jnp.concatenate(carried, axis=1),
            jnp.concatenate(spread, axis=1),
            (((1,), (1,)), ((), ())),
            preferred_element_type=jnp.float32,
        )

    total = lax.fori_loop(
        0, SOURCES // group, step, jnp.zeros((count, low_count), jnp.float32), unroll=True
    )
    sums = []
    for value in range(values):
        at = 3 * value * high_count
        sums.append(
            total[at + 2 * high_count : at + 3 * high_count]
            + total[at + high_count : at + 2 * high_count]
            + total[at : at + high_count]
        )
    return sums


def ice_kernel(
    slots_ref, target_ref, skin_ref, frozen_ref, resist_ref, _, skin_out, flux_out, ice_out
):
    def read(value, start, group):
        return slots_ref[pl.ds(3 * start + value, group, stride=3), :]

    heat, warmth, tau = segment_sums(read, target_ref, 3, range(ICE_ROWS), LANES, group=8)
    skin = skin_ref[...]
    frozen = frozen_ref[...]
    fresh = jnp.where(
        frozen == 1,
        (floe_warmth * skin + warmth) / (floe_warmth + floor_conductance + heat),
        skin,
    )
    skin_out[...] = fresh
    table = spread_rows(fresh)
    for start in range(0, SOURCES, ROWS):
        (at_floe,) = look_up((table,), target_ref[pl.ds(start, ROWS), :])
        flux_out[pl.ds(2 * start, ROWS, stride=2), :] = (
            slots_ref[pl.ds(3 * start, ROWS, stride=3), :] * at_floe
            - slots_ref[pl.ds(3 * start + 1, ROWS, stride=3), :]
        )
    ends = jnp.where(
        lanes_of((1, LANES)) < LANES // 2, tau[0:1], tau[ICE_ROWS - 1 : ICE_ROWS]
    )
    flux_out[pl.ds(1, SOURCES, stride=2), :] = jnp.broadcast_to(ends, (SOURCES, LANES))
    ice_out[0] = resist_ref[...] * (0.1 + 0.9 * frozen.astype(jnp.float32))
    ice_out[1] = tau


def paired(even_rows, odd_rows):
    lane = lanes_of((ROWS, LANES))
    out = []
    for at in range(2):
        index = (2 * lane + at) % LANES
        out.append(
            jnp.where(
                lane < LANES // 2,
                jnp.take_along_axis(even_rows, index, axis=1, mode="promise_in_bounds"),
                jnp.take_along_axis(odd_rows, index, axis=1, mode="promise_in_bounds"),
            )
        )
    return out


def neighbourhood(even_rows, odd_rows, before, after):
    shape = (ROWS, LANES)
    lane = lanes_of(shape)
    row = rows_of(shape)
    own = paired(even_rows, odd_rows)
    behind = paired(jnp.broadcast_to(before, shape), jnp.broadcast_to(before, shape))
    ahead = paired(jnp.broadcast_to(after, shape), jnp.broadcast_to(after, shape))
    cells = {}
    for at in range(2):
        cells[at] = own[at]
        up = jnp.where(row == ROWS - 1, ahead[at], pltpu.roll(own[at], ROWS - 1, 0))
        down = jnp.where(row == 0, behind[at], pltpu.roll(own[at], 1, 0))
        for far in range(1, EVP // 2 + 1):
            cells[at + 2 * far] = pltpu.roll(
                jnp.where(lane < far, up, own[at]), LANES - far, 1
            )
            cells[at - 2 * far] = pltpu.roll(
                jnp.where(lane >= LANES - far, down, own[at]), far, 1
            )
    return cells


def drift_kernel(motion_ref, strain_ref, ice_ref, halo_ref, out_ref, held):
    place = lax.axis_index("face") * TILES + lax.axis_index("tile")
    blank = jnp.zeros((1, LANES), jnp.float32)
    even, odd = pl.ds(0, ROWS, stride=2), pl.ds(1, ROWS, stride=2)
    first = jnp.where(place == 0, 0.0, 1.0)
    last = jnp.where(place == SOURCES - 1, 0.0, 1.0)
    slow = 1.0 / (1.0 + mobility * water_drag)
    fade = 1.0 / (1.0 + stress_decay)
    arrays = (
        (motion_ref[even], motion_ref[odd], halo_ref[0:1], halo_ref[4:5], 1.0),
        (strain_ref[even], strain_ref[odd], halo_ref[1:2], halo_ref[5:6], mobility * slow),
        (
            ice_ref[0, even],
            ice_ref[0, odd],
            halo_ref[2:3],
            halo_ref[6:7],
            mobility * slow * relaxation * fade,
        ),
        (ice_ref[1, even], ice_ref[1, odd], blank, blank, mobility * slow),
    )
    for at, (even_rows, odd_rows, before, after, scale) in enumerate(arrays):
        cells = neighbourhood(
            even_rows * scale,
            odd_rows * scale,
            before * (first * scale),
            after * (last * scale),
        )
        for cell, values in cells.items():
            held[at, cell + EVP] = values
    shape = (ROWS, LANES)
    where = LANES * rows_of(shape) + lanes_of(shape)

    def inside(cell):
        end = (ROWS * LANES * 2 - cell) // 2
        return jnp.where((where == end) & (place == SOURCES - 1), 0.0, 1.0)

    width = 2 * EVP + 2
    velocity = [held[0, at] for at in range(width)]
    stress = [held[1, at] for at in range(width)]
    for turn in range(EVP):
        for at in range(turn, width - turn - 1):
            stress[at] = stress[at] * fade + held[2, at] * (velocity[at + 1] - velocity[at])
        for at in range(turn + 1, width - turn - 1):
            force = stress[at] - stress[at - 1] + held[3, at]
            if at >= EVP + 2 and at % 2 == 0:
                force = force * inside(at - EVP)
            velocity[at] = velocity[at] * slow + force
    lane = lanes_of(shape)
    for rows, half in ((even, 0), (odd, LANES // 2)):
        index = lane // 2 + half
        out_ref[rows] = jnp.where(
            lane % 2 == 0,
            jnp.take_along_axis(velocity[EVP], index, axis=1, mode="promise_in_bounds"),
            jnp.take_along_axis(velocity[EVP + 1], index, axis=1, mode="promise_in_bounds"),
        )


def edge_kernel(
    resist_ref, frozen_ref, halo_ref, gain_ref, rest_ref, out_ref, calm_out, held
):
    calm_out[LEVELS - 1] = calm = rest_ref[LEVELS - 1]
    for level in range(LEVELS - 2, -1, -1):
        calm = gain_ref[level] * calm + rest_ref[level]
        calm_out[level] = calm
    slow = 1.0 / (1.0 + mobility * water_drag)
    fade = 1.0 / (1.0 + stress_decay)
    half = LANES // 2
    here = lanes_of((1, LANES)) < half
    ends = [
        resist_ref[pl.ds(row, 1)] * (0.1 + 0.9 * frozen_ref[pl.ds(row, 1)].astype(jnp.float32))
        for row in (0, ICE_ROWS - 1)
    ]
    strength = (
        jnp.where(here, ends[0], halo_ref[2:3]),
        jnp.where(here, halo_ref[6:7], ends[1]),
    )
    pull = jnp.concatenate(
        [jnp.broadcast_to(pltpu.roll(row, half, 1), (24, LANES)) for row in strength], axis=0
    ) * (mobility * slow * relaxation * fade)
    shape = (48, LANES)
    row = rows_of(shape)
    lane = lanes_of(shape)
    source = jnp.where(row < 24, half - EVP + row, half - 24 + row)
    push = jnp.where((lane == source) & (row % 24 < EVP), mobility * slow, 0.0)
    velocity = jnp.zeros(shape, jnp.float32)
    stress = jnp.zeros(shape, jnp.float32)
    for _ in range(EVP):
        stress = stress * fade + pull * (pltpu.roll(velocity, LANES - 1, 1) - velocity)
        velocity = velocity * slow + (stress - pltpu.roll(stress, 1, 1) + push)
    velocity = pltpu.roll(velocity, half, 1)
    velocity = jnp.where(
        ((row < 24) & (lane < EVP)) | ((row >= 24) & (lane >= LANES - EVP)), velocity, 0.0
    )
    held[...] = jnp.zeros((LANES, LANES), jnp.float32)
    held[pl.ds(0, EVP), :] = velocity[24 : 24 + EVP]
    held[pl.ds(LANES - EVP, EVP), :] = velocity[:EVP]
    out_ref[...] = jnp.concatenate(in_three(held[...]), axis=1).astype(jnp.bfloat16)


def last_kernel(
    flux_ref, site_ref, answer_ref, calm_ref, drift_ref, edge_ref, heat_out, motion_out
):
    def read(value, start, group):
        return flux_ref[pl.ds(2 * start, group, stride=2), :]

    place = lax.axis_index("face") * TILES + lax.axis_index("tile")
    lane = lanes_of((1, LANES))
    before = flux_ref[pl.ds(2 * jnp.maximum(place - 1, 0) + 1, 1), :]
    after = flux_ref[pl.ds(2 * jnp.minimum(place + 1, SOURCES - 1) + 1, 1), :]
    outside = jnp.where(
        lane < LANES // 2,
        after * jnp.where(place == SOURCES - 1, 0.0, 1.0),
        before * jnp.where(place == 0, 0.0, 1.0),
    )
    products = lax.dot_general(
        jnp.concatenate(
            [jnp.broadcast_to(part, (ROWS, LANES)) for part in in_three(outside)]
            + [jnp.zeros((ROWS, LANES), jnp.float32)],
            axis=0,
        ).astype(jnp.bfloat16),
        edge_ref[...],
        (((1,), (0,)), ((), ())),
        preferred_element_type=jnp.float32,
    )
    by_part = [
        products[:, LANES * part : LANES * (part + 1)] for part in range(3)
    ]
    by_part = [part[:ROWS] + part[ROWS : 2 * ROWS] + part[2 * ROWS : 3 * ROWS] for part in by_part]
    added = (by_part[0] + by_part[1] + by_part[2])[0:1]
    motion_out[...] = drift_ref[...]
    motion_out[0:1] = drift_ref[0:1] + jnp.where(lane < EVP, added, 0.0)
    end = pl.ds(ICE_ROWS - 1, 1)
    motion_out[end] = drift_ref[end] + jnp.where(lane >= LANES - EVP, added, 0.0)

    order = [ROWS * (half % 2) + half // 2 for half in range(2 * ROWS)]
    (halves,) = segment_sums(read, site_ref, 1, order, LANES // 2)
    surface_flux = jnp.concatenate([halves[:ROWS], halves[ROWS:]], axis=1)
    for level in range(LEVELS):
        heat_out[level] = answer_ref[level] * surface_flux + calm_ref[level]


def ring(axis, step):
    count = lax.axis_size(axis)
    return [(i, (i + step) % count) for i in range(count)]


def swaps(axis, first):
    count = lax.axis_size(axis)
    pairs = [(i, (i + 1) % count) for i in range(first, count, 2)]
    return sorted(pairs + [(b, a) for a, b in pairs])


def exchanged(rows, count):
    blocks = rows.reshape(SOURCES, count, 1, LANES)
    blocks = lax.all_to_all(blocks, BOTH, split_axis=0, concat_axis=0, tiled=True)
    return near(blocks.reshape(SOURCES * count, LANES))


def local(
    squeeze_anomaly,
    eastward_airflow,
    northward_airflow,
    thermal_anomaly,
    diffusivity_link,
    sound_stability_ratio,
    overlay_source_site,
    overlay_target_floe,
    overlay_fraction,
    floe_skin_kelvin,
    frozen_indicator,
    floe_motion,
    floe_strain_tensor,
    floe_compress_resist,
):
    ice = (ICE_ROWS, LANES)
    slot = (SOURCES, LANES)
    arguments = dict(
        press=squeeze_anomaly,
        zonal=eastward_airflow,
        merid=northward_airflow,
        motion=floe_motion.reshape(ice),
        strain=floe_strain_tensor.reshape(ice),
        resist=floe_compress_resist.reshape(ice),
        frozen=frozen_indicator.reshape(ice),
        skin=floe_skin_kelvin.reshape(ice),
        heat=thermal_anomaly,
        link=diffusivity_link,
        site=overlay_source_site.reshape(slot),
        area=overlay_fraction.reshape(slot),
        target=overlay_target_floe.reshape(slot),
    )
    hbm = pl.BlockSpec(memory_space=pl.ANY)
    sources = [arguments[name] for name in STAGED]
    *staged, sides, down, up = pl.pallas_call(
        stage_kernel,
        out_shape=[pltpu.VMEM(source.shape, source.dtype) for source in sources]
        + [kept(2 * ROWS, LANES), kept(DOWN + 8, LANES), kept(UP + 8, LANES)],
        in_specs=[hbm] * len(sources),
        out_specs=[VMEM] * (len(sources) + 3),
        scratch_shapes=[pltpu.SemaphoreType.DMA((len(sources),))],
    )(*sources)
    at = {name: near(values) for name, values in zip(STAGED, staged)}
    sides = near(sides)
    sources = [arguments[name] for name in AFTER]
    *staged, speeds, gain, inverse, answer, weight = pl.pallas_call(
        factor_kernel,
        out_shape=[pltpu.VMEM(source.shape, source.dtype) for source in sources]
        + [kept(LEVELS, LANES)]
        + [kept(LEVELS, ROWS, LANES)] * 3
        + [kept(*slot)],
        in_specs=[hbm, VMEM] + [hbm] * len(sources),
        out_specs=[VMEM] * (len(sources) + 5),
        scratch_shapes=[
            pltpu.SMEM((LEVELS,), jnp.float32),
            pltpu.SemaphoreType.DMA((len(sources) + 1,)),
        ],
    )(sound_stability_ratio, sides, *sources)
    at.update({name: near(values) for name, values in zip(AFTER, staged)})
    above = near(lax.ppermute(down, "face", ring("face", -1)))
    below = near(lax.ppermute(up, "face", ring("face", 1)))
    sides = pl.pallas_call(
        side_kernel, out_shape=kept(2 * ROWS, LANES), in_specs=[VMEM] * 3, out_specs=VMEM
    )(sides, above, below)
    wide = pl.pallas_call(
        widen_kernel, out_shape=kept(FIELDS, 2 * ROWS, LANES), in_specs=[VMEM] * 5, out_specs=VMEM
    )(*(at[name] for name in ("press", "zonal", "merid")), above, below)
    twin = near(lax.ppermute(sides, "tile", swaps("tile", 0)))
    cross = near(lax.ppermute(sides, "tile", swaps("tile", 1)))
    pressure_new, rest, halo, slots = pl.pallas_call(
        columns_kernel,
        out_shape=[
            struct(LEVELS, ROWS, LANES),
            kept(LEVELS, ROWS, LANES),
            kept(8, LANES),
            struct(3 * SOURCES, LANES),
        ],
        in_specs=[VMEM] * 10,
        out_specs=[VMEM] * 4,
    )(
        near(speeds),
        near(wide),
        at["heat"],
        at["link"],
        at["site"],
        at["area"],
        near(inverse),
        near(weight),
        twin,
        cross,
    )
    arrived = exchanged(slots, 3)
    edge, calm = pl.pallas_call(
        edge_kernel,
        out_shape=[pltpu.VMEM((LANES, 3 * LANES), jnp.bfloat16), kept(LEVELS, ROWS, LANES)],
        in_specs=[VMEM] * 5,
        out_specs=[VMEM] * 2,
        scratch_shapes=[pltpu.VMEM((LANES, LANES), jnp.float32)],
    )(at["resist"], at["frozen"], near(halo), near(gain), near(rest))
    edge = near(edge)
    fresh, flux, ice_terms = pl.pallas_call(
        ice_kernel,
        out_shape=[struct(*ice), struct(2 * SOURCES, LANES), kept(2, *ice)],
        in_specs=[VMEM] * 6,
        out_specs=[VMEM] * 3,
    )(arrived, *(at[name] for name in ("target", "skin", "frozen", "resist")), edge)
    returned = exchanged(flux, 2)
    drifted = pl.pallas_call(
        drift_kernel,
        out_shape=kept(*ice),
        in_specs=[VMEM] * 4,
        out_specs=VMEM,
        scratch_shapes=[pltpu.VMEM((4, 2 * EVP + 2, ROWS, LANES), jnp.float32)],
    )(at["motion"], at["strain"], near(ice_terms), near(halo))
    temp_new, velocity = pl.pallas_call(
        last_kernel,
        out_shape=[struct(LEVELS, ROWS, LANES), struct(*ice)],
        in_specs=[VMEM] * 6,
        out_specs=[VMEM] * 2,
    )(returned, at["site"], near(answer), near(calm), near(drifted), edge)
    return (temp_new, pressure_new, fresh.reshape(-1), velocity.reshape(-1))


def solution(mesh):
    block = P(None, "face", "tile")
    slot = P(BOTH, None, None)
    cells = P(BOTH)
    return jax.shard_map(
        local,
        mesh=mesh,
        in_specs=(block,) * 5 + (P(),) + (slot,) * 3 + (cells,) * 5,
        out_specs=(block, block, cells, cells),
        check_vma=False,
    )
```

```python
import functools

import jax
import jax.numpy as jnp
from jax import lax
from jax.experimental import pallas as pl
from jax.experimental.pallas import tpu as pltpu
from jax.sharding import PartitionSpec as P

SUBS = 2
EVP = 20
LEVELS = 8
ROWS = 8
LANES = 128
SOURCES = 128
ICE_ROWS = 16
FIELDS = 3 * LEVELS
UP_ROWS = (2, 2, 1)
DOWN_ROWS = (2, 1, 1)
UP = LEVELS * sum(UP_ROWS)
DOWN = LEVELS * sum(DOWN_ROWS)
TILES = 32
STAGED = ("press", "zonal", "merid", "motion", "strain", "resist", "frozen")
AFTER = ("link", "site", "area", "heat", "target", "skin")

isentropic_lapse = 0.3
gravity_step = 0.5
floe_warmth = 2.0
floor_conductance = 1.0
relaxation = 0.5
stress_decay = 0.05
mobility = 0.3
water_drag = 0.1

BOTH = ("face", "tile")
VMEM = pl.BlockSpec(memory_space=pltpu.VMEM)


def struct(*shape):
    return jax.ShapeDtypeStruct(shape, jnp.float32)


def kept(*shape):
    return pltpu.VMEM(shape, jnp.float32)


def near(values):
    return pltpu.with_memory_space_constraint(values, pltpu.VMEM)


def lanes_of(shape):
    return lax.broadcasted_iota(jnp.int32, shape, len(shape) - 1)


def rows_of(shape):
    return lax.broadcasted_iota(jnp.int32, shape, len(shape) - 2)


def copies_of(sources, targets, sems):
    copies = [
        pltpu.make_async_copy(source, target, sems.at[at])
        for at, (source, target) in enumerate(zip(sources, targets))
    ]
    for copy in copies:
        copy.start()
    return copies


def slab_rows(counts, field, level):
    return pl.ds(LEVELS * sum(counts[:field]) + counts[field] * level, counts[field])


def stage_kernel(*refs):
    count = len(STAGED)
    targets = refs[count : 2 * count]
    side_out, down_out, up_out, sems = refs[2 * count :]
    copies = copies_of(refs[:count], targets, sems)
    motion_ref, strain_ref, resist_ref, frozen_ref = targets[3:7]
    for copy in copies[:3]:
        copy.wait()
    lane = lanes_of((ROWS, LANES))
    packed = jnp.zeros((ROWS, LANES), jnp.float32)
    for field, ref in enumerate(targets[:3]):
        for level in range(LEVELS):
            cells = ref[level]
            at = 4 * (field * LEVELS + level)
            moved = pltpu.roll(cells, 2 + at, 1)
            packed = jnp.where((lane >= at) & (lane < at + 4), moved, packed)
            down_out[slab_rows(DOWN_ROWS, field, level), :] = cells[: DOWN_ROWS[field]]
            up_out[slab_rows(UP_ROWS, field, level), :] = cells[ROWS - UP_ROWS[field] :]
    for copy in copies[3:]:
        copy.wait()
    edge = jnp.zeros((1, LANES), jnp.float32)
    lane = lanes_of((1, LANES))
    for row, first, shift in ((ICE_ROWS - 1, 0, EVP), (0, 3, 0)):
        here = pl.ds(row, 1)
        strength = resist_ref[here] * (0.1 + 0.9 * frozen_ref[here].astype(jnp.float32))
        for at, cells in enumerate((motion_ref[here], strain_ref[here], strength), first):
            moved = pltpu.roll(cells, (EVP * at + shift) % LANES, 1)
            edge = jnp.where((lane >= EVP * at) & (lane < EVP * at + EVP), moved, edge)
    edge = jnp.broadcast_to(edge, (ROWS, LANES))
    side_out[pl.ds(0, ROWS), :] = packed
    side_out[pl.ds(ROWS, ROWS), :] = edge
    down_out[pl.ds(DOWN, 2), :] = packed[:2]
    up_out[pl.ds(UP, 2), :] = packed[ROWS - 2 :]
    down_out[pl.ds(DOWN + 2, 6), :] = edge[:6]
    up_out[pl.ds(UP + 2, 6), :] = edge[:6]


def factor_kernel(*refs):
    count = len(AFTER)
    speed_ref, _, *refs = refs
    targets = refs[count : 2 * count]
    speed_out, gain_out, inverse_out, answer_out, slot_out, speeds, sems = refs[2 * count :]
    speed_copy = pltpu.make_async_copy(speed_ref, speeds, sems.at[count])
    speed_copy.start()
    copies = copies_of(refs[:count], targets, sems)
    link_ref, site_ref, area_ref = targets[:3]
    copies[0].wait()
    link = link_ref[0]
    inverse = 1.0 / (1.0 + link)
    gain = link * inverse
    inverse_out[0] = inverse
    gain_out[0] = gain
    for level in range(1, LEVELS - 1):
        earlier, link = link, link_ref[level]
        inverse = 1.0 / (1.0 + earlier + link - earlier * gain)
        gain = link * inverse
        inverse_out[level] = inverse
        gain_out[level] = gain
    inverse = 1.0 / (1.0 + link * (1.0 - gain))
    beta = gravity_step * inverse
    inverse_out[LEVELS - 1] = inverse
    answer_out[LEVELS - 1] = answer = beta
    for level in range(LEVELS - 2, -1, -1):
        answer = gain_out[level] * answer
        answer_out[level] = answer
    drag = link_ref[LEVELS - 1]
    table = spread_rows(drag / (1.0 + drag * beta))
    for copy in copies[1:3]:
        copy.wait()
    for start in range(0, SOURCES, ROWS):
        here = pl.ds(start, ROWS)
        (found,) = look_up((table,), site_ref[here, :])
        slot_out[here, :] = area_ref[here, :] * found
    speed_copy.wait()
    for level in range(LEVELS):
        speed_out[pl.ds(level, 1), :] = jnp.full((1, LANES), speeds[level])
    for copy in copies[3:]:
        copy.wait()


def side_kernel(side_ref, above_ref, below_ref, out_ref):
    out_ref[pl.ds(0, ROWS + 3), :] = side_ref[pl.ds(0, ROWS + 3), :]
    out_ref[pl.ds(8, 2), :] = above_ref[pl.ds(DOWN, 2), :]
    out_ref[pl.ds(11, 1), :] = below_ref[pl.ds(UP + 2, 1), :]
    out_ref[pl.ds(12, 2), :] = above_ref[pl.ds(DOWN + 2, 2), :]
    out_ref[pl.ds(14, 2), :] = below_ref[pl.ds(UP, 2), :]


def widen_kernel(p_ref, u_ref, v_ref, above_ref, below_ref, wide_out):
    for field, ref in enumerate((p_ref, u_ref, v_ref)):
        above, below = DOWN_ROWS[field], UP_ROWS[field]
        for level in range(LEVELS):
            at = field * LEVELS + level
            wide_out[at, pl.ds(0, ROWS), :] = ref[level]
            wide_out[at, pl.ds(8, 8), :] = jnp.zeros((8, LANES), jnp.float32)
            wide_out[at, pl.ds(8, above), :] = above_ref[slab_rows(DOWN_ROWS, field, level), :]
            wide_out[at, pl.ds(16 - below, below), :] = below_ref[
                slab_rows(UP_ROWS, field, level), :
            ]


def look_up(tables, index):
    high = index >> 7
    low = index & (LANES - 1)
    found = [None] * len(tables)
    for row in range(len(tables[0])):
        here = high == row
        for at, rows in enumerate(tables):
            taken = jnp.take_along_axis(rows[row], low, axis=1, mode="promise_in_bounds")
            found[at] = taken if row == 0 else jnp.where(here, taken, found[at])
    return found


def spread_rows(table):
    return [
        jnp.broadcast_to(table[row : row + 1], (ROWS, LANES)) for row in range(table.shape[0])
    ]


def columns_kernel(
    speed_ref,
    wide_ref,
    heat_ref,
    link_ref,
    site_ref,
    area_ref,
    inverse_ref,
    weight_ref,
    twin_ref,
    cross_ref,
    press_out,
    rest_out,
    halo_out,
    slots_out,
):
    shape = (2 * ROWS, LANES)
    place = lax.axis_index("tile")
    even = place % 2 == 0
    left = jnp.where(even, cross_ref[...], twin_ref[...])
    right = jnp.where(even, twin_ref[...], cross_ref[...])
    border = jnp.where(lanes_of(shape) % 4 < 2, left, right)
    temps = []
    for level in range(LEVELS):
        speed = jnp.broadcast_to(speed_ref[pl.ds(level, 1), 0:1], (2 * ROWS, 2 * LANES))
        now = []
        for field in range(3):
            at = field * LEVELS + level
            outer = pltpu.roll(border, (126 - 4 * at) % LANES, 1)
            now.append(jnp.concatenate([wide_ref[at], outer], axis=1))
        press, zonal, merid = now
        for _ in range(SUBS):
            zonal = zonal - speed * (pltpu.roll(press, 15, 0) - press)
            merid = merid - speed * (pltpu.roll(press, 255, 1) - press)
            press = press - speed * (
                zonal - pltpu.roll(zonal, 1, 0) + merid - pltpu.roll(merid, 1, 1)
            )
        final = press[:ROWS, :LANES]
        press_out[level] = final
        temps.append(heat_ref[level] + isentropic_lapse * final)
    last_zonal = zonal[:ROWS, :LANES]
    last_merid = merid[:ROWS, :LANES]

    rest = temps[0] * inverse_ref[0]
    rest_out[0] = rest
    for level in range(1, LEVELS):
        rest = (temps[level] + link_ref[level - 1] * rest) * inverse_ref[level]
        rest_out[level] = rest
    gamma = rest
    stress = link_ref[LEVELS - 1] * (last_zonal + 0.5 * last_merid)

    tables = [spread_rows(table) for table in (gamma, stress)]
    for start in range(0, SOURCES, ROWS):
        here = pl.ds(start, ROWS)
        found = look_up(tables, site_ref[here, :])
        slot_w = weight_ref[here, :]
        slots_out[pl.ds(3 * start, ROWS, stride=3), :] = slot_w
        slots_out[pl.ds(3 * start + 1, ROWS, stride=3), :] = slot_w * found[0]
        slots_out[pl.ds(3 * start + 2, ROWS, stride=3), :] = area_ref[here, :] * found[1]
    before = jnp.where(place == 0, left[11:12], left[10:11])
    after = jnp.where(place == TILES - 1, right[12:13], right[10:11])
    halo_out[pl.ds(0, 1), :] = before
    halo_out[pl.ds(1, 1), :] = after
    halo_out[pl.ds(2, 6), :] = jnp.zeros((6, LANES), jnp.float32)


def in_three(values):
    first = values.astype(jnp.bfloat16)
    left = values - first.astype(jnp.float32)
    second = left.astype(jnp.bfloat16)
    third = (left - second.astype(jnp.float32)).astype(jnp.bfloat16)
    return first.astype(jnp.float32), second.astype(jnp.float32), third.astype(jnp.float32)


def segment_sums(read, index_ref, values, high_row, low_count, group=32):
    high_count = len(high_row)
    shape = (high_count, LANES)
    rows = rows_of(shape)
    high_here = sum(jnp.where(rows == at, high, 0) for high, at in enumerate(high_row))
    low_here = rows_of((low_count, LANES))
    count = 3 * values * high_count

    def step(block, total):
        start = pl.multiple_of(block * group, group)
        index = index_ref[pl.ds(start, group), :]
        high = index >> (low_count.bit_length() - 1)
        low = index & (low_count - 1)
        parts = [part for value in range(values) for part in in_three(read(value, start, group))]
        carried, spread = [], []
        for row in range(group):
            here = high_here == high[row : row + 1]
            carried.append(
                jnp.concatenate(
                    [
                        jnp.where(here, jnp.broadcast_to(part[row : row + 1], shape), 0.0).astype(
                            jnp.bfloat16
                        )
                        for part in parts
                    ],
                    axis=0,
                )
            )
            spread.append(
                jnp.where(low_here == low[row : row + 1], 1.0, 0.0).astype(jnp.bfloat16)
            )
        return total + lax.dot_general(
            jnp.concatenate(carried, axis=1),
            jnp.concatenate(spread, axis=1),
            (((1,), (1,)), ((), ())),
            preferred_element_type=jnp.float32,
        )

    total = lax.fori_loop(
        0, SOURCES // group, step, jnp.zeros((count, low_count), jnp.float32), unroll=True
    )
    sums = []
    for value in range(values):
        at = 3 * value * high_count
        sums.append(
            total[at + 2 * high_count : at + 3 * high_count]
            + total[at + high_count : at + 2 * high_count]
            + total[at : at + high_count]
        )
    return sums


def ice_kernel(
    slots_ref, target_ref, skin_ref, frozen_ref, resist_ref, _, skin_out, flux_out, ice_out
):
    def read(value, start, group):
        return slots_ref[pl.ds(3 * start + value, group, stride=3), :]

    heat, warmth, tau = segment_sums(read, target_ref, 3, range(ICE_ROWS), LANES, group=8)
    skin = skin_ref[...]
    frozen = frozen_ref[...]
    fresh = jnp.where(
        frozen == 1,
        (floe_warmth * skin + warmth) / (floe_warmth + floor_conductance + heat),
        skin,
    )
    skin_out[...] = fresh
    table = spread_rows(fresh)
    for start in range(0, SOURCES, ROWS):
        (at_floe,) = look_up((table,), target_ref[pl.ds(start, ROWS), :])
        flux_out[pl.ds(2 * start, ROWS, stride=2), :] = (
            slots_ref[pl.ds(3 * start, ROWS, stride=3), :] * at_floe
            - slots_ref[pl.ds(3 * start + 1, ROWS, stride=3), :]
        )
    ends = jnp.where(
        lanes_of((1, LANES)) < LANES // 2, tau[0:1], tau[ICE_ROWS - 1 : ICE_ROWS]
    )
    flux_out[pl.ds(1, SOURCES, stride=2), :] = jnp.broadcast_to(ends, (SOURCES, LANES))
    ice_out[0] = resist_ref[...] * (0.1 + 0.9 * frozen.astype(jnp.float32))
    ice_out[1] = tau


def paired(even_rows, odd_rows):
    lane = lanes_of((ROWS, LANES))
    out = []
    for at in range(2):
        index = (2 * lane + at) % LANES
        out.append(
            jnp.where(
                lane < LANES // 2,
                jnp.take_along_axis(even_rows, index, axis=1, mode="promise_in_bounds"),
                jnp.take_along_axis(odd_rows, index, axis=1, mode="promise_in_bounds"),
            )
        )
    return out


def neighbourhood(even_rows, odd_rows, before, after):
    shape = (ROWS, LANES)
    lane = lanes_of(shape)
    row = rows_of(shape)
    own = paired(even_rows, odd_rows)
    behind = paired(jnp.broadcast_to(before, shape), jnp.broadcast_to(before, shape))
    ahead = paired(jnp.broadcast_to(after, shape), jnp.broadcast_to(after, shape))
    cells = {}
    for at in range(2):
        cells[at] = own[at]
        up = jnp.where(row == ROWS - 1, ahead[at], pltpu.roll(own[at], ROWS - 1, 0))
        down = jnp.where(row == 0, behind[at], pltpu.roll(own[at], 1, 0))
        for far in range(1, EVP // 2 + 1):
            cells[at + 2 * far] = pltpu.roll(
                jnp.where(lane < far, up, own[at]), LANES - far, 1
            )
            cells[at - 2 * far] = pltpu.roll(
                jnp.where(lane >= LANES - far, down, own[at]), far, 1
            )
    return cells


def drift_kernel(motion_ref, strain_ref, ice_ref, halo_ref, out_ref, held):
    place = lax.axis_index("face") * TILES + lax.axis_index("tile")
    blank = jnp.zeros((1, LANES), jnp.float32)
    even, odd = pl.ds(0, ROWS, stride=2), pl.ds(1, ROWS, stride=2)
    first = jnp.where(place == 0, 0.0, 1.0)
    last = jnp.where(place == SOURCES - 1, 0.0, 1.0)
    slow = 1.0 / (1.0 + mobility * water_drag)
    fade = 1.0 / (1.0 + stress_decay)
    arrays = (
        (motion_ref[even], motion_ref[odd], halo_ref[0:1], halo_ref[4:5], 1.0),
        (strain_ref[even], strain_ref[odd], halo_ref[1:2], halo_ref[5:6], mobility * slow),
        (
            ice_ref[0, even],
            ice_ref[0, odd],
            halo_ref[2:3],
            halo_ref[6:7],
            mobility * slow * relaxation * fade,
        ),
        (ice_ref[1, even], ice_ref[1, odd], blank, blank, mobility * slow),
    )
    for at, (even_rows, odd_rows, before, after, scale) in enumerate(arrays):
        cells = neighbourhood(
            even_rows * scale,
            odd_rows * scale,
            before * (first * scale),
            after * (last * scale),
        )
        for cell, values in cells.items():
            held[at, cell + EVP] = values
    shape = (ROWS, LANES)
    where = LANES * rows_of(shape) + lanes_of(shape)

    def inside(cell):
        end = (ROWS * LANES * 2 - cell) // 2
        return jnp.where((where == end) & (place == SOURCES - 1), 0.0, 1.0)

    width = 2 * EVP + 2
    velocity = [held[0, at] for at in range(width)]
    stress = [held[1, at] for at in range(width)]
    for turn in range(EVP):
        for at in range(turn, width - turn - 1):
            stress[at] = stress[at] * fade + held[2, at] * (velocity[at + 1] - velocity[at])
        for at in range(turn + 1, width - turn - 1):
            force = stress[at] - stress[at - 1] + held[3, at]
            if at >= EVP + 2 and at % 2 == 0:
                force = force * inside(at - EVP)
            velocity[at] = velocity[at] * slow + force
    lane = lanes_of(shape)
    for rows, half in ((even, 0), (odd, LANES // 2)):
        index = lane // 2 + half
        out_ref[rows] = jnp.where(
            lane % 2 == 0,
            jnp.take_along_axis(velocity[EVP], index, axis=1, mode="promise_in_bounds"),
            jnp.take_along_axis(velocity[EVP + 1], index, axis=1, mode="promise_in_bounds"),
        )


def edge_kernel(
    resist_ref, frozen_ref, ends_ref, gain_ref, rest_ref, out_ref, calm_out, halo_out, held
):
    halo = [None] * 8
    for at in range(3):
        halo[at] = pltpu.roll(ends_ref[0:1], LANES - EVP - EVP * at, 1)
        halo[4 + at] = pltpu.roll(ends_ref[1:2], LANES - EVP * (at + 3), 1)
    halo[3] = halo[7] = jnp.zeros((1, LANES), jnp.float32)
    for at, row in enumerate(halo):
        halo_out[pl.ds(at, 1), :] = row
    calm_out[LEVELS - 1] = calm = rest_ref[LEVELS - 1]
    for level in range(LEVELS - 2, -1, -1):
        calm = gain_ref[level] * calm + rest_ref[level]
        calm_out[level] = calm
    slow = 1.0 / (1.0 + mobility * water_drag)
    fade = 1.0 / (1.0 + stress_decay)
    half = LANES // 2
    here = lanes_of((1, LANES)) < half
    ends = [
        resist_ref[pl.ds(row, 1)] * (0.1 + 0.9 * frozen_ref[pl.ds(row, 1)].astype(jnp.float32))
        for row in (0, ICE_ROWS - 1)
    ]
    strength = (
        jnp.where(here, ends[0], halo[2]),
        jnp.where(here, halo[6], ends[1]),
    )
    pull = jnp.concatenate(
        [jnp.broadcast_to(pltpu.roll(row, half, 1), (24, LANES)) for row in strength], axis=0
    ) * (mobility * slow * relaxation * fade)
    shape = (48, LANES)
    row = rows_of(shape)
    lane = lanes_of(shape)
    source = jnp.where(row < 24, half - EVP + row, half - 24 + row)
    push = jnp.where((lane == source) & (row % 24 < EVP), mobility * slow, 0.0)
    velocity = jnp.zeros(shape, jnp.float32)
    stress = jnp.zeros(shape, jnp.float32)
    for _ in range(EVP):
        stress = stress * fade + pull * (pltpu.roll(velocity, LANES - 1, 1) - velocity)
        velocity = velocity * slow + (stress - pltpu.roll(stress, 1, 1) + push)
    velocity = pltpu.roll(velocity, half, 1)
    velocity = jnp.where(
        ((row < 24) & (lane < EVP)) | ((row >= 24) & (lane >= LANES - EVP)), velocity, 0.0
    )
    held[...] = jnp.zeros((LANES, LANES), jnp.float32)
    held[pl.ds(0, EVP), :] = velocity[24 : 24 + EVP]
    held[pl.ds(LANES - EVP, EVP), :] = velocity[:EVP]
    out_ref[...] = jnp.concatenate(in_three(held[...]), axis=1).astype(jnp.bfloat16)


def last_kernel(
    flux_ref, site_ref, answer_ref, calm_ref, drift_ref, edge_ref, heat_out, motion_out
):
    def read(value, start, group):
        return flux_ref[pl.ds(2 * start, group, stride=2), :]

    place = lax.axis_index("face") * TILES + lax.axis_index("tile")
    lane = lanes_of((1, LANES))
    before = flux_ref[pl.ds(2 * jnp.maximum(place - 1, 0) + 1, 1), :]
    after = flux_ref[pl.ds(2 * jnp.minimum(place + 1, SOURCES - 1) + 1, 1), :]
    outside = jnp.where(
        lane < LANES // 2,
        after * jnp.where(place == SOURCES - 1, 0.0, 1.0),
        before * jnp.where(place == 0, 0.0, 1.0),
    )
    products = lax.dot_general(
        jnp.concatenate(
            [jnp.broadcast_to(part, (ROWS, LANES)) for part in in_three(outside)]
            + [jnp.zeros((ROWS, LANES), jnp.float32)],
            axis=0,
        ).astype(jnp.bfloat16),
        edge_ref[...],
        (((1,), (0,)), ((), ())),
        preferred_element_type=jnp.float32,
    )
    by_part = [
        products[:, LANES * part : LANES * (part + 1)] for part in range(3)
    ]
    by_part = [part[:ROWS] + part[ROWS : 2 * ROWS] + part[2 * ROWS : 3 * ROWS] for part in by_part]
    added = (by_part[0] + by_part[1] + by_part[2])[0:1]
    motion_out[...] = drift_ref[...]
    motion_out[0:1] = drift_ref[0:1] + jnp.where(lane < EVP, added, 0.0)
    end = pl.ds(ICE_ROWS - 1, 1)
    motion_out[end] = drift_ref[end] + jnp.where(lane >= LANES - EVP, added, 0.0)

    order = [ROWS * (half % 2) + half // 2 for half in range(2 * ROWS)]
    (halves,) = segment_sums(read, site_ref, 1, order, LANES // 2)
    surface_flux = jnp.concatenate([halves[:ROWS], halves[ROWS:]], axis=1)
    for level in range(LEVELS):
        heat_out[level] = answer_ref[level] * surface_flux + calm_ref[level]


def ring(axis, step):
    count = lax.axis_size(axis)
    return [(i, (i + step) % count) for i in range(count)]


def swaps(axis, first):
    count = lax.axis_size(axis)
    pairs = [(i, (i + 1) % count) for i in range(first, count, 2)]
    return sorted(pairs + [(b, a) for a, b in pairs])


def exchanged(rows, count):
    blocks = rows.reshape(SOURCES, count, 1, LANES)
    blocks = lax.all_to_all(blocks, BOTH, split_axis=0, concat_axis=0, tiled=True)
    return near(blocks.reshape(SOURCES * count, LANES))


def local(
    squeeze_anomaly,
    eastward_airflow,
    northward_airflow,
    thermal_anomaly,
    diffusivity_link,
    sound_stability_ratio,
    overlay_source_site,
    overlay_target_floe,
    overlay_fraction,
    floe_skin_kelvin,
    frozen_indicator,
    floe_motion,
    floe_strain_tensor,
    floe_compress_resist,
):
    ice = (ICE_ROWS, LANES)
    slot = (SOURCES, LANES)
    arguments = dict(
        press=squeeze_anomaly,
        zonal=eastward_airflow,
        merid=northward_airflow,
        motion=floe_motion.reshape(ice),
        strain=floe_strain_tensor.reshape(ice),
        resist=floe_compress_resist.reshape(ice),
        frozen=frozen_indicator.reshape(ice),
        skin=floe_skin_kelvin.reshape(ice),
        heat=thermal_anomaly,
        link=diffusivity_link,
        site=overlay_source_site.reshape(slot),
        area=overlay_fraction.reshape(slot),
        target=overlay_target_floe.reshape(slot),
    )
    hbm = pl.BlockSpec(memory_space=pl.ANY)
    sources = [arguments[name] for name in STAGED]
    *staged, sides, down, up = pl.pallas_call(
        stage_kernel,
        out_shape=[pltpu.VMEM(source.shape, source.dtype) for source in sources]
        + [kept(2 * ROWS, LANES), kept(DOWN + 8, LANES), kept(UP + 8, LANES)],
        in_specs=[hbm] * len(sources),
        out_specs=[VMEM] * (len(sources) + 3),
        scratch_shapes=[pltpu.SemaphoreType.DMA((len(sources),))],
    )(*sources)
    at = {name: near(values) for name, values in zip(STAGED, staged)}
    sides = near(sides)
    sources = [arguments[name] for name in AFTER]
    *staged, speeds, gain, inverse, answer, weight = pl.pallas_call(
        factor_kernel,
        out_shape=[pltpu.VMEM(source.shape, source.dtype) for source in sources]
        + [kept(LEVELS, LANES)]
        + [kept(LEVELS, ROWS, LANES)] * 3
        + [kept(*slot)],
        in_specs=[hbm, VMEM] + [hbm] * len(sources),
        out_specs=[VMEM] * (len(sources) + 5),
        scratch_shapes=[
            pltpu.SMEM((LEVELS,), jnp.float32),
            pltpu.SemaphoreType.DMA((len(sources) + 1,)),
        ],
    )(sound_stability_ratio, sides, *sources)
    at.update({name: near(values) for name, values in zip(AFTER, staged)})
    above = near(lax.ppermute(down, "face", ring("face", -1)))
    below = near(lax.ppermute(up, "face", ring("face", 1)))
    sides = pl.pallas_call(
        side_kernel, out_shape=kept(2 * ROWS, LANES), in_specs=[VMEM] * 3, out_specs=VMEM
    )(sides, above, below)
    wide = pl.pallas_call(
        widen_kernel, out_shape=kept(FIELDS, 2 * ROWS, LANES), in_specs=[VMEM] * 5, out_specs=VMEM
    )(*(at[name] for name in ("press", "zonal", "merid")), above, below)
    twin = near(lax.ppermute(sides, "tile", swaps("tile", 0)))
    cross = near(lax.ppermute(sides, "tile", swaps("tile", 1)))
    pressure_new, rest, halo, slots = pl.pallas_call(
        columns_kernel,
        out_shape=[
            struct(LEVELS, ROWS, LANES),
            kept(LEVELS, ROWS, LANES),
            kept(8, LANES),
            struct(3 * SOURCES, LANES),
        ],
        in_specs=[VMEM] * 10,
        out_specs=[VMEM] * 4,
    )(
        near(speeds),
        near(wide),
        at["heat"],
        at["link"],
        at["site"],
        at["area"],
        near(inverse),
        near(weight),
        twin,
        cross,
    )
    arrived = exchanged(slots, 3)
    edge, calm, halo = pl.pallas_call(
        edge_kernel,
        out_shape=[pltpu.VMEM((LANES, 3 * LANES), jnp.bfloat16), kept(LEVELS, ROWS, LANES), kept(8, LANES)],
        in_specs=[VMEM] * 5,
        out_specs=[VMEM] * 3,
        scratch_shapes=[pltpu.VMEM((LANES, LANES), jnp.float32)],
    )(at["resist"], at["frozen"], near(halo), near(gain), near(rest))
    edge = near(edge)
    fresh, flux, ice_terms = pl.pallas_call(
        ice_kernel,
        out_shape=[struct(*ice), struct(2 * SOURCES, LANES), kept(2, *ice)],
        in_specs=[VMEM] * 6,
        out_specs=[VMEM] * 3,
    )(arrived, *(at[name] for name in ("target", "skin", "frozen", "resist")), edge)
    returned = exchanged(flux, 2)
    drifted = pl.pallas_call(
        drift_kernel,
        out_shape=kept(*ice),
        in_specs=[VMEM] * 4,
        out_specs=VMEM,
        scratch_shapes=[pltpu.VMEM((4, 2 * EVP + 2, ROWS, LANES), jnp.float32)],
    )(at["motion"], at["strain"], near(ice_terms), near(halo))
    temp_new, velocity = pl.pallas_call(
        last_kernel,
        out_shape=[struct(LEVELS, ROWS, LANES), struct(*ice)],
        in_specs=[VMEM] * 6,
        out_specs=[VMEM] * 2,
    )(returned, at["site"], near(answer), near(calm), near(drifted), edge)
    return (temp_new, pressure_new, fresh.reshape(-1), velocity.reshape(-1))


def solution(mesh):
    block = P(None, "face", "tile")
    slot = P(BOTH, None, None)
    cells = P(BOTH)
    return jax.shard_map(
        local,
        mesh=mesh,
        in_specs=(block,) * 5 + (P(),) + (slot,) * 3 + (cells,) * 5,
        out_specs=(block, block, cells, cells),
        check_vma=False,
    )
```
